256 devices in a mesh: grp: 2 (over x_lo), tile: 32 (over y, z), mem: 4 (over x_hi, core).
Axes of the slice: x: 4 (x_hi: 2, x_lo: 2; x = x_hi * 2 + x_lo), y: 4, z: 8, core: 2. Of those that a mesh axis runs over, the one named last changes fastest.
Arguments:
- current_state: float32 [512, 2, 65536], P(('grp', 'mem'), None, 'tile'), may hold values from -6 to 6
- lagged_states: float32 [3, 32, 8, 512, 512], P(None, 'tile', ('grp', 'mem')), may hold values from -6 to 6
- water_depth: float32 [65536], P('tile'), may hold values from 0.4 to 1
- obs_cells: int32 [32768], replicated, may hold values from 0 to 65535, as said below
- obs_values: float32 [32768], replicated, may hold values from -6 to 6
- obs_errors: float32 [32768], replicated, may hold values from 0.5 to 2
- tile_obs: int32 [32, 8, 1024], P('tile', ('grp', 'mem')), may hold values from -1 to 32767, as said below
Outputs:
- analysis_state: float32 [512, 2, 65536], P(('grp', 'mem'), None, 'tile')
- smoothed_lags: float32 [3, 32, 8, 512, 512], P(None, 'tile', ('grp', 'mem'))
The draws below stay inside these ranges and needn't reach their ends.
Inputs may be any that keep to these rules, and one draw needn't show every extreme that they name: `obs_cells`: observation o lies in grid tile o // 1024, that is at a cell from (o // 1024) * 2048 to that plus 2048 - 1. `tile_obs`: each list holds distinct indices of observations in its own grid tile or the two beside it (periodically), used slots first and -1 after them; at least 256 slots are used in every list, all 1024 in some list.
All inputs are finite; a program needn't handle non-finite values. Where the reference program divides by a largest or mean magnitude, that divisor is 1e-20 or more.
Results may differ from the reference program's by a relative error of at most 0.0003.
Values sent between devices are 32-bit elements; how exact they have to be, the bound alone decides.
No kernel may reach another device: no remote copies, remote signals or barrier semaphores. Data moves between devices by JAX's collectives and lax.ppermute only.
A program may use at most 64 MiB of HBM per device.

```python
import math
import jax
import jax.numpy as jnp
from jax import lax

TRIAL_TOTAL = 512
PATCH_POINTS = 256
OBS_DEV = 1024
ITERS = 6
LAGS = 3
MODEL_STEPS = 2
P_MAX = 1024
LOC = 512
PATCH_UNKNOWNS = 512
SUBT = 8
GRID = 32
CELLS_DEV = 2048
NCELLS = 65536
NOBS = 32768


def obs_layout(key):
    base = jax.random.fold_in(key, 11)
    key_cells, key_counts, key_full = jax.random.split(base, 3)
    offsets = jax.random.randint(key_cells, (GRID, OBS_DEV), 0, CELLS_DEV)
    obs_sites = (offsets + jnp.arange(GRID, dtype=jnp.int32)[:, None] * CELLS_DEV).reshape(NOBS)
    counts = jax.random.randint(key_counts, (GRID * SUBT,), P_MAX // 4, P_MAX + 1)
    full_tile = jax.random.randint(key_full, (), 0, GRID * SUBT)
    counts = jnp.where(jnp.arange(GRID * SUBT) == full_tile, P_MAX, counts)

    def one_tile(tile_number):
        grid_index = tile_number // SUBT
        part_index = tile_number % SUBT
        center = grid_index * CELLS_DEV + part_index * PATCH_POINTS + PATCH_POINTS // 2
        candidates = ((grid_index - 1) * OBS_DEV + jnp.arange(3 * OBS_DEV, dtype=jnp.int32)) % NOBS
        distance = jnp.abs(obs_sites[candidates] - center)
        distance = jnp.minimum(distance, NCELLS - distance)
        score = distance * (3 * OBS_DEV) + jnp.arange(3 * OBS_DEV, dtype=jnp.int32)
        chosen = candidates[jnp.argsort(score)[:P_MAX]]
        return jnp.where(jnp.arange(P_MAX) < counts[tile_number], chosen, -1)
    row_lists = jax.vmap(one_tile)(jnp.arange(GRID * SUBT, dtype=jnp.int32))
    return (obs_sites.astype(jnp.int32), row_lists.reshape(GRID, SUBT, P_MAX).astype(jnp.int32))


def draw_obs_cells(key, part):
    return obs_layout(key)[0]


def draw_tile_obs(key, part):
    return obs_layout(key)[1]


def levels(own_key, dims, pieces, low, top_value):
    def one(position, parts):
        heights = jax.random.uniform(jax.random.fold_in(jax.random.fold_in(own_key, 6), position), (parts,), jnp.float32, low / len(pieces), top_value / len(pieces))
        return jnp.repeat(jnp.exp(heights), dims[position] // parts).reshape((-1,) + (1,) * (len(dims) - position - 1))

    gain = one(*pieces[0])
    for cut in pieces[1:]:
        gain = gain * one(*cut)
    return gain


def scatter_about(own_key, shape, width, bound, pieces=(), kind=jnp.bfloat16):
    values = width * jax.random.normal(own_key, shape, jnp.float32)
    if pieces:
        values = values * levels(own_key, shape, pieces, -0.22, 0.18)
    return jnp.clip(values, -bound, bound).astype(kind)


def setup_inputs(seed: int = 0) -> dict:
    splits = jax.random.split(jax.random.key(seed), 8)
    return {
        "current_state": scatter_about(splits[0], (TRIAL_TOTAL, 2, NCELLS), 1.0, 6.0, ((0, 8), (2, 32)), jnp.float32),
        "lagged_states": scatter_about(splits[1], (LAGS, GRID, SUBT, TRIAL_TOTAL, PATCH_UNKNOWNS), 1.0, 6.0, ((1, 32), (2, 8)), jnp.float32),
        "water_depth": jnp.clip(jnp.exp(math.log(1.0) - 0.9162907 * jax.random.uniform(splits[2], (NCELLS,), jnp.float32) ** levels(splits[2], (NCELLS,), ((0, 32),), -0.2, 0.2)), 0.4, 1.0),
        "obs_cells": draw_obs_cells(jax.random.fold_in(splits[7], 71), 0),
        "obs_values": scatter_about(splits[4], (NOBS,), 1.0, 6.0, (), jnp.float32),
        "obs_errors": jnp.clip(jnp.exp(jax.random.uniform(splits[5], (NOBS,), jnp.float32, math.log(0.5), math.log(2.0))), 0.5, 2.0),
        "tile_obs": draw_tile_obs(jax.random.fold_in(splits[7], 71), 0),
    }


flux_scale = 0.9
wave_scale = 0.9
highest = lax.Precision.HIGHEST

def advance(free_elevation, fluid_speed, water_depth):
    for repeat in range(MODEL_STEPS):
        free_elevation = free_elevation - flux_scale * water_depth * (fluid_speed - jnp.roll(fluid_speed, 1, axis=-1))
        fluid_speed = fluid_speed - wave_scale * (jnp.roll(free_elevation, -1, axis=-1) - free_elevation)
    return (free_elevation, fluid_speed)

def inverse_root(matrix, members):
    row_bound = jnp.max(lax.optimization_barrier(jnp.sum(jnp.abs(matrix), axis=1)))
    identity = jnp.eye(members, dtype=jnp.float32)
    approx = matrix / row_bound
    root_inv = identity
    for repeat in range(ITERS):
        middle = 1.5 * identity - 0.5 * jnp.dot(root_inv, approx, precision=highest)
        approx = jnp.dot(approx, middle, precision=highest)
        root_inv = jnp.dot(middle, root_inv, precision=highest)
    return root_inv / jnp.sqrt(row_bound)

def analyse(states, predicted, obs_level, obs_spread, obs_sites, usable, center, cell_total):
    members = predicted.shape[0]
    mean_obs = lax.optimization_barrier(jnp.mean(predicted, axis=0))
    spread = predicted - mean_obs
    departure = obs_level - mean_obs
    distance = jnp.abs(obs_sites - center)
    distance = jnp.minimum(distance, cell_total - distance).astype(jnp.float32)
    weight = jnp.exp(-0.5 * (distance / LOC) ** 2) / (obs_spread * obs_spread)
    weight = jnp.where(usable, weight, jnp.zeros_like(weight))
    identity = jnp.eye(members, dtype=jnp.float32)
    precision_matrix = (members - 1) * identity + jnp.dot(spread * weight, spread.T, precision=highest)
    root_cover = inverse_root(precision_matrix, members)
    covariance = jnp.dot(root_cover, root_cover, precision=highest)
    mean_weight = jnp.dot(covariance, jnp.dot(spread, weight * departure, precision=highest), precision=highest)
    transform = math.sqrt(members - 1) * root_cover + mean_weight[:, None]
    state_mean = lax.optimization_barrier(jnp.mean(states, axis=1, keepdims=True))
    return state_mean + jnp.einsum('ij,liv->ljv', transform, states - state_mean, precision=highest)

def reference(current_state, lagged_states, water_depth, obs_cells, obs_values, obs_errors, tile_obs):
    free_elevation, fluid_speed = advance(current_state[:, 0], current_state[:, 1], water_depth)
    prior_fields = jnp.stack([free_elevation, fluid_speed], axis=1)
    predicted_all = free_elevation[:, obs_cells]

    def one_tile(tile_number):
        grid_index = tile_number // SUBT
        part_index = tile_number % SUBT
        initial_shift = (grid_index * CELLS_DEV + part_index * PATCH_POINTS).astype(jnp.int32)
        patch_field_slab = lax.dynamic_slice_in_dim(prior_fields, initial_shift, PATCH_POINTS, 2).reshape(TRIAL_TOTAL, PATCH_UNKNOWNS)
        lag_block = lagged_states[:, grid_index, part_index]
        row_list = tile_obs[grid_index, part_index]
        usable = row_list >= 0
        clamped = jnp.maximum(row_list, 0)
        predicted = jnp.take(predicted_all, clamped, axis=1)
        center = initial_shift + PATCH_POINTS // 2
        states = jnp.concatenate([patch_field_slab[None], lag_block], axis=0)
        return analyse(states, predicted, obs_values[clamped], obs_errors[clamped], obs_cells[clamped], usable, center, NCELLS)
    results = lax.map(one_tile, jnp.arange(GRID * SUBT, dtype=jnp.int32))
    results = results.reshape(GRID, SUBT, LAGS + 1, TRIAL_TOTAL, 2, PATCH_POINTS)
    analysis = results[:, :, 0].transpose(2, 3, 0, 1, 4).reshape(TRIAL_TOTAL, 2, NCELLS)
    older_out = results[:, :, 1:].reshape(GRID, SUBT, LAGS, TRIAL_TOTAL, PATCH_UNKNOWNS).transpose(2, 0, 1, 3, 4)
    return (analysis, older_out)
```

```python
import functools
import math

import jax
import jax.numpy as jnp
from jax import lax
from jax.experimental import pallas as pl
from jax.experimental.pallas import tpu as pltpu
from jax.sharding import PartitionSpec as P

GROUP = ("grp", "mem")
PARTS = 8
ROWS = 64
MEMBERS = 512
CELLS = 2048
CHUNKS = 16
CELLS_TILE = 256
STATE = 512
OBS = 1024
SLOTS = 1024
NOBS = 32768
NCELLS = 65536
TILES = 32
LOC = 512
LAGS = 3
f32 = jnp.float32
bf16 = jnp.bfloat16
VMEM = pl.BlockSpec(memory_space=pltpu.VMEM)
SMEM = pl.BlockSpec(memory_space=pltpu.SMEM)


def params(mib):
    return pltpu.CompilerParams(vmem_limit_bytes=mib * 1024 * 1024)


def halves(x):
    hi = x.astype(bf16)
    return hi, (x - hi.astype(f32)).astype(bf16)


def dot(a, b):
    return jnp.dot(a, b, preferred_element_type=f32)


def dot_nt(a, b):
    return lax.dot_general(a, b, (((1,), (1,)), ((), ())), preferred_element_type=f32)


def product(a, b):
    (ah, al), (bh, bl) = a, b
    return dot(ah, bh) + (dot(ah, bl) + dot(al, bh))


def forecast_kernel(cur, depth, left, right, cells, fields, own, packed, hbuf, ubuf, table):
    lane = lax.broadcasted_iota(jnp.int32, (ROWS, 128), 1)
    first, last = lane == 0, lane == 127

    def old(c, v):
        if c < 0:
            return left[pl.ds(v, ROWS, stride=2), :]
        if c == CHUNKS:
            return right[pl.ds(v, ROWS, stride=2), :]
        return cur[pl.ds(2 * c + v, ROWS, stride=2 * CHUNKS), :]

    def scaled_depth(c):
        if c < 0:
            row = left[128:129, :]
        elif c == CHUNKS:
            row = right[128:129, :]
        else:
            row = depth[c : c + 1, :]
        return 0.9 * row

    def height_step(h_of, u_of, put, low):
        before = None
        for c in range(low, CHUNKS + 1):
            u = u_of(c)
            turned = pltpu.roll(u, 1, 1)
            previous = turned if before is None else jnp.where(first, before, turned)
            before = turned
            put(c, h_of(c) - scaled_depth(c) * (u - previous))

    def speed_step(h_of, u_of, put, low, high):
        turned = pltpu.roll(h_of(low), 127, 1)
        for c in range(low, high):
            after = pltpu.roll(h_of(c + 1), 127, 1) if c < CHUNKS else turned
            following = jnp.where(last, after, turned)
            turned = after
            put(c, u_of(c) - 0.9 * (following - h_of(c)))

    def put_h(c, x):
        hbuf[c + 1] = x

    def put_u(c, x):
        ubuf[c + 1] = x

    def h_new(c):
        return hbuf[c + 1]

    def u_new(c):
        return ubuf[c + 1]

    height_step(lambda c: old(c, 0), lambda c: old(c, 1), put_h, -1)
    speed_step(h_new, lambda c: old(c, 1), put_u, -1, CHUNKS + 1)
    height_step(h_new, u_new, put_h, -1)

    def put_fields(v, c, x):
        fields[c // 2, :, v * CELLS_TILE + (c % 2) * 128 : v * CELLS_TILE + (c % 2 + 1) * 128] = x

    speed_step(h_new, u_new, functools.partial(put_fields, 1), 0, CHUNKS)
    for c in range(CHUNKS):
        h = h_new(c)
        put_fields(0, c, h)
        table[c * 128 : (c + 1) * 128, :] = jnp.concatenate([h, h], axis=0).T

    def pick(i, carry):
        for j in range(32):
            o = i * 32 + j
            own[pl.ds(o, 1), :] = table[pl.ds(cells[o], 1), :]
        return carry

    lax.fori_loop(0, OBS // 32, pick, 0)
    low_half = lax.broadcasted_iota(jnp.int32, (OBS // 2, 128), 1) < ROWS
    packed[...] = jnp.where(low_half, own[: OBS // 2, :], own[OBS // 2 :, :])


def forecast(cur, depth, left, right, cells):
    return pl.pallas_call(
        forecast_kernel,
        out_shape=(
            jax.ShapeDtypeStruct((PARTS, ROWS, STATE), f32),
            jax.ShapeDtypeStruct((OBS, 128), f32),
            jax.ShapeDtypeStruct((OBS // 2, 128), f32),
        ),
        in_specs=[VMEM, VMEM, VMEM, VMEM, SMEM],
        out_specs=(VMEM, VMEM, VMEM),
        scratch_shapes=[
            pltpu.VMEM((CHUNKS + 2, ROWS, 128), f32),
            pltpu.VMEM((CHUNKS + 2, ROWS, 128), f32),
            pltpu.VMEM((CELLS, 128), f32),
        ],
        compiler_params=params(24),
        name="forecast",
    )(cur, depth, left, right, cells)


def pick_kernel(lists, below, own, above, out, table, stage):
    low_half = lax.broadcasted_iota(jnp.int32, (OBS // 2, 128), 1) < ROWS
    for place, packed in ((0, below), (2, above)):
        x = packed[...]
        turned = pltpu.roll(x, ROWS, 1)
        table[place * OBS : place * OBS + OBS // 2, :] = jnp.where(low_half, x, turned)
        table[place * OBS + OBS // 2 : (place + 1) * OBS, :] = jnp.where(low_half, turned, x)
    table[OBS : 2 * OBS, :] = own[...]
    low_row = lax.broadcasted_iota(jnp.int32, (1, 128), 1) < ROWS

    def block(i, carry):
        k = i // 4
        q = i % 4
        for j in range(128):
            a = lists[k, q * 128 + j]
            b = lists[k, SLOTS // 2 + q * 128 + j]
            stage[j : j + 1, :] = jnp.where(low_row, table[pl.ds(a, 1), :], table[pl.ds(b, 1), :])
        turned = stage[...].T
        out[k, :, pl.ds(pl.multiple_of(q * 128, 128), 128)] = turned[:ROWS]
        out[k, :, pl.ds(pl.multiple_of(SLOTS // 2 + q * 128, 128), 128)] = turned[ROWS:]
        return carry

    lax.fori_loop(0, PARTS * 4, block, 0)


def pick(lists, below, own, above):
    return pl.pallas_call(
        pick_kernel,
        out_shape=jax.ShapeDtypeStruct((PARTS, ROWS, SLOTS), f32),
        in_specs=[SMEM, VMEM, VMEM, VMEM],
        out_specs=VMEM,
        scratch_shapes=[pltpu.VMEM((3 * OBS, 128), f32), pltpu.VMEM((128, 128), f32)],
        compiler_params=params(24),
        name="pick",
    )(lists, below, own, above)


def slots_kernel(where_ref, rel, values, errors, cells, out, rows):
    tile = where_ref[0]
    center = where_ref[1]
    for n in range(3):
        t = lax.rem(tile + (TILES - 1 + n), TILES)
        for j in range(8):
            at = n * OBS + j * 128
            rows[0:1, at : at + 128] = values[t, j : j + 1, :]
            rows[1:2, at : at + 128] = errors[t, j : j + 1, :]
            rows[2:3, at : at + 128] = cells[t, j : j + 1, :].astype(f32)
    listed = rel[...]
    total = jnp.zeros((9, SLOTS), f32)
    for n in range(12):
        x = rows[0:3, n * 256 : (n + 1) * 256]
        a, rest = x.astype(bf16), None
        rest = x - a.astype(f32)
        b = rest.astype(bf16)
        c = (rest - b.astype(f32)).astype(bf16)
        parts = jnp.concatenate([a.astype(f32), b.astype(f32), c.astype(f32)], axis=0).astype(bf16)
        here = lax.broadcasted_iota(jnp.int32, (256, SLOTS), 0) + n * 256
        chosen = jnp.where(here == listed, 1.0, 0.0).astype(bf16)
        total = total + dot(parts, chosen)
    found = total[0:3] + total[3:6] + total[6:9]
    value, error, cell = found[0:1], found[1:2], found[2:3].astype(jnp.int32)
    distance = jnp.abs(cell - center)
    distance = jnp.minimum(distance, NCELLS - distance).astype(f32)
    used = listed >= 0
    weight = jnp.exp(-0.5 * (distance / LOC) ** 2) / (error * error)
    out[0:1, :] = jnp.where(used, weight, 0.0)
    out[1:2, :] = jnp.where(used, value, 0.0)


def slots(where_arr, rel, values, errors, cells):
    return pl.pallas_call(
        slots_kernel,
        out_shape=jax.ShapeDtypeStruct((8, SLOTS), f32),
        in_specs=[SMEM, VMEM, VMEM, VMEM, VMEM],
        out_specs=VMEM,
        scratch_shapes=[pltpu.VMEM((8, 3 * OBS), f32)],
        compiler_params=params(24),
        name="slots",
    )(where_arr, rel, values, errors, cells)


def analyse_kernel(predicted, slot_rows, state, gain_hi, gain_lo, analysis):
    y = predicted[...]
    weight = slot_rows[0:1, :]
    mean = jnp.sum(y, axis=0, keepdims=True) * (1.0 / MEMBERS)
    root_weight = jnp.sqrt(weight)
    spread = (y - mean) * root_weight
    departure = (slot_rows[1:2, :] - mean) * root_weight
    sh, sl = halves(spread)
    dh, dl = halves(jnp.broadcast_to(departure, (16, SLOTS)))
    rows_i = lax.broadcasted_iota(jnp.int32, (MEMBERS, MEMBERS), 0)
    cols_i = lax.broadcasted_iota(jnp.int32, (MEMBERS, MEMBERS), 1)
    eye = jnp.where(rows_i == cols_i, 1.0, 0.0)
    a = dot_nt(sh, sh) + (dot_nt(sh, sl) + dot_nt(sl, sh)) + (MEMBERS - 1.0) * eye
    innovation = (dot_nt(dh, sh) + (dot_nt(dh, sl) + dot_nt(dl, sh)))[0:1, :]
    bound = jnp.max(jnp.sum(jnp.abs(a), axis=0, keepdims=True), axis=1, keepdims=True)
    approx = a / bound

    def two_steps(m):
        mp = halves(m)
        m2 = product(mp, mp)
        q = 1.6875 * eye - 0.5625 * m + 0.0625 * m2
        return 2.25 * eye - 2.4375 * m + product(halves(m2), halves(q))

    r = halves(two_steps(approx))
    z = r
    w = halves(product(halves(approx), r))
    r = halves(two_steps(product(z, w)))
    z, w = halves(product(r, z)), halves(product(w, r))
    r = halves(two_steps(product(z, w)))
    root = product(r, z) * lax.rsqrt(bound)
    once = jnp.sum(root * innovation, axis=1, keepdims=True)
    mean_weight = jnp.sum(root * once, axis=0, keepdims=True)
    moved = math.sqrt(MEMBERS - 1) * root + mean_weight
    gain = moved + (1.0 - jnp.sum(moved, axis=1, keepdims=True)) * (1.0 / MEMBERS)
    gh, gl = halves(gain)
    gain_hi[...] = gh
    gain_lo[...] = gl
    analysis[...] = product((gh, gl), halves(state[...]))


def analyse(predicted, slot_rows, state):
    return pl.pallas_call(
        analyse_kernel,
        out_shape=(
            jax.ShapeDtypeStruct((MEMBERS, MEMBERS), bf16),
            jax.ShapeDtypeStruct((MEMBERS, MEMBERS), bf16),
            jax.ShapeDtypeStruct((MEMBERS, STATE), f32),
        ),
        in_specs=[VMEM, VMEM, VMEM],
        out_specs=(VMEM, VMEM, VMEM),
        compiler_params=params(40),
        name="analyse",
    )(predicted, slot_rows, state)


def smooth_kernel(gain_hi, gain_lo, state, out):
    out[0] = product((gain_hi[...], gain_lo[...]), halves(state[0]))


def smooth(gain_hi, gain_lo, states):
    whole = pl.BlockSpec((MEMBERS, MEMBERS), lambda i: (0, 0))
    one = pl.BlockSpec((1, MEMBERS, STATE), lambda i: (i, 0, 0))
    return pl.pallas_call(
        smooth_kernel,
        out_shape=jax.ShapeDtypeStruct((LAGS, MEMBERS, STATE), f32),
        grid=(LAGS,),
        in_specs=[whole, whole, one],
        out_specs=one,
        compiler_params=params(24),
        cost_estimate=pl.CostEstimate(
            flops=2 * 3 * LAGS * MEMBERS**2 * STATE, bytes_accessed=8 * LAGS * MEMBERS * STATE, transcendentals=0
        ),
        name="smooth",
    )(gain_hi, gain_lo, states)


def assemble_kernel(parts, out):
    for k in range(PARTS):
        for v in range(2):
            for b in range(2):
                at = v * CELLS_TILE + b * 128
                out[pl.ds(2 * (2 * k + b) + v, ROWS, stride=2 * CHUNKS), :] = parts[k, :, at : at + 128]


def assemble(parts):
    return pl.pallas_call(
        assemble_kernel,
        out_shape=jax.ShapeDtypeStruct((ROWS * 2 * CHUNKS, 128), f32),
        in_specs=[VMEM],
        out_specs=VMEM,
        compiler_params=params(24),
        name="assemble",
    )(parts)


def along_tiles(x, by):
    return lax.ppermute(x, "tile", [(i, (i + by) % TILES) for i in range(TILES)])


def exchange(x):
    return lax.all_to_all(x, GROUP, split_axis=0, concat_axis=0, tiled=True)


def per_device(
    current_state, lagged_states, water_depth, obs_cells, obs_values, obs_errors, tile_obs
):
    tile = lax.axis_index("tile")
    part = lax.axis_index("grp") * lax.axis_size("mem") + lax.axis_index("mem")
    by_chunk = current_state.reshape(ROWS, 2, CHUNKS, 128).transpose(0, 2, 1, 3)
    depth = water_depth.reshape(CHUNKS, 128)

    def edge(c):
        return jnp.concatenate(
            [by_chunk[:, c].reshape(2 * ROWS, 128), jnp.broadcast_to(depth[c], (8, 128))], axis=0
        )

    left = along_tiles(edge(CHUNKS - 1), 1)
    right = along_tiles(edge(0), -1)
    listed = tile_obs[0, 0]
    rel = jnp.where(listed >= 0, (listed - (tile - 1) * OBS) & (NOBS - 1), -1)
    lists = lax.all_gather(jnp.maximum(rel, 0), GROUP, axis=0)
    local_cells = lax.dynamic_slice_in_dim(obs_cells, tile * OBS, OBS) - tile * CELLS
    fields, own, packed = forecast(
        by_chunk.reshape(ROWS * 2 * CHUNKS, 128), depth, left, right, local_cells
    )
    below = along_tiles(packed, 1)
    above = along_tiles(packed, -1)
    state = exchange(fields).reshape(MEMBERS, STATE)
    picked = pick(lists, below, own, above)
    predicted = exchange(picked).reshape(MEMBERS, SLOTS)
    center = tile * CELLS + part * CELLS_TILE + CELLS_TILE // 2
    slot_rows = slots(
        jnp.stack([tile, center]),
        rel.reshape(1, SLOTS),
        obs_values.reshape(TILES, 8, 128),
        obs_errors.reshape(TILES, 8, 128),
        obs_cells.reshape(TILES, 8, 128),
    )
    gain_hi, gain_lo, analysis = analyse(predicted, slot_rows, state)
    returned = exchange(analysis.reshape(PARTS, ROWS, STATE))
    older = smooth(gain_hi, gain_lo, lagged_states.reshape(LAGS, MEMBERS, STATE))
    analysed = assemble(returned).reshape(ROWS, CHUNKS, 2, 128).transpose(0, 2, 1, 3)
    return (
        analysed.reshape(ROWS, 2, CELLS),
        older.reshape(LAGS, 1, 1, MEMBERS, STATE),
    )


def solution(mesh):
    placed = (
        P(GROUP, None, "tile"),
        P(None, "tile", GROUP, None, None),
        P("tile"),
        P(),
        P(),
        P(),
        P("tile", GROUP, None),
    )
    return jax.shard_map(
        per_device,
        mesh=mesh,
        in_specs=placed,
        out_specs=(P(GROUP, None, "tile"), P(None, "tile", GROUP, None, None)),
        check_vma=False,
    )
```

```python
import functools
import math

import jax
import jax.numpy as jnp
from jax import lax
from jax.experimental import pallas as pl
from jax.experimental.pallas import tpu as pltpu
from jax.sharding import PartitionSpec as P

GROUP = ("grp", "mem")
PARTS = 8
ROWS = 64
MEMBERS = 512
CELLS = 2048
CHUNKS = 16
CELLS_TILE = 256
STATE = 512
OBS = 1024
SLOTS = 1024
NOBS = 32768
NCELLS = 65536
TILES = 32
LOC = 512
LAGS = 3
f32 = jnp.float32
bf16 = jnp.bfloat16
VMEM = pl.BlockSpec(memory_space=pltpu.VMEM)
HBM = pl.BlockSpec(memory_space=pltpu.HBM)
SMEM = pl.BlockSpec(memory_space=pltpu.SMEM)


def params(mib):
    return pltpu.CompilerParams(vmem_limit_bytes=mib * 1024 * 1024)


def cost(flops):
    return pl.CostEstimate(flops=flops, bytes_accessed=2**20, transcendentals=0)


def halves(x):
    hi = x.astype(bf16)
    return hi, (x - hi.astype(f32)).astype(bf16)


def dot(a, b):
    return jnp.dot(a, b, preferred_element_type=f32)


def dot_nt(a, b):
    return lax.dot_general(a, b, (((1,), (1,)), ((), ())), preferred_element_type=f32)


def product(a, b):
    (ah, al), (bh, bl) = a, b
    return dot(ah, bh) + (dot(ah, bl) + dot(al, bh))


def edges_kernel(cur, depth, to_right, to_left, ends, sems):
    copies = [
        pltpu.make_async_copy(cur.at[:, pl.ds(at, 8), :], ends.at[n], sems.at[n])
        for n, at in enumerate((0, 2 * CHUNKS - 8))
    ]
    for copy in copies:
        copy.start()
    low_half = lax.broadcasted_iota(jnp.int32, (ROWS, 128), 1) < ROWS
    end = CHUNKS - 1
    to_right[ROWS:, :] = jnp.broadcast_to(depth[end : end + 1, :], (8, 128))
    to_left[ROWS:, :] = jnp.broadcast_to(depth[0:1, :], (8, 128))
    copies[1].wait()
    h, u = ends[1, :, 6, :], ends[1, :, 7, :]
    to_right[:ROWS, :] = jnp.where(low_half, pltpu.roll(h, ROWS, 1), u)
    copies[0].wait()
    h, u = ends[0, :, 0, :], ends[0, :, 1, :]
    to_left[:ROWS, :] = jnp.where(low_half, h, pltpu.roll(u, ROWS, 1))


def edges(cur, depth):
    message = jax.ShapeDtypeStruct((ROWS + 8, 128), f32)
    return pl.pallas_call(
        edges_kernel,
        out_shape=(message, message),
        in_specs=[HBM, VMEM],
        out_specs=(VMEM, VMEM),
        scratch_shapes=[pltpu.VMEM((2, ROWS, 8, 128), f32), pltpu.SemaphoreType.DMA((2,))],
        compiler_params=params(8),
        name="edges",
    )(cur, depth)


def order_kernel(where_ref, tile_list, ordered, copies, row_list, row_place):
    listed = tile_list[...]
    rel = jnp.where(listed >= 0, (listed - (where_ref[0] - 1) * OBS) & (NOBS - 1), -1)
    count = jnp.sum(jnp.where(rel >= 0, 1.0, 0.0))
    top = jnp.max(rel)
    for j in range(8):
        row_list[0:1, j * 128 : (j + 1) * 128] = rel[j : j + 1, :]
    row = row_list[0:1, :]
    chunks = 3 * OBS // 128

    def iota(shape, dim):
        return lax.broadcasted_iota(jnp.int32, shape, dim)

    def flags(x):
        return jnp.where(x, 1.0, 0.0).astype(bf16)

    in_chunk = flags((row >> 7) == iota((32, SLOTS), 0))
    in_lane = flags((row & 127) == iota((128, SLOTS), 0))
    present = dot_nt(in_chunk, in_lane).astype(bf16)
    before = dot(present, flags(iota((128, 128), 0) < iota((128, 128), 1)))
    totals = dot(present, jnp.ones((128, 128), bf16)).astype(bf16)
    place = before + dot(flags(iota((32, 32), 1) < iota((32, 32), 0)), totals)
    place = jnp.where(present.astype(f32) > 0.5, place, -1.0).astype(jnp.int32)
    for c in range(chunks):
        row_place[0:1, c * 128 : (c + 1) * 128] = place[c : c + 1, :]
    row = row_place[0:1, :]
    wide = 3 * OBS
    to_row = (row >> 7) == iota((8, wide), 0)
    number = iota((8, wide), 1)
    parts = jnp.concatenate(
        [jnp.where(to_row, number >> 7, 0), jnp.where(to_row, number & 127, 0)], axis=0
    )
    found = dot_nt(parts.astype(f32).astype(bf16), flags((row & 127) == iota((128, wide), 0)))
    found = (found[:8] * 128.0 + found[8:]).astype(jnp.int32)
    used = (iota((8, 128), 0) * 128 + iota((8, 128), 1)).astype(f32) < count
    ordered[...] = jnp.where(used, found, -1)
    filled = jnp.where(used, found, jnp.maximum(top, 0))
    for k in range(PARTS):
        copies[k] = filled


def order(where_arr, tile_list):
    return pl.pallas_call(
        order_kernel,
        out_shape=(
            jax.ShapeDtypeStruct((8, 128), jnp.int32),
            jax.ShapeDtypeStruct((PARTS, 8, 128), jnp.int32),
        ),
        in_specs=[SMEM, VMEM],
        out_specs=(VMEM, VMEM),
        scratch_shapes=[pltpu.VMEM((8, SLOTS), jnp.int32), pltpu.VMEM((8, 3 * OBS), jnp.int32)],
        cost_estimate=pl.CostEstimate(flops=0, bytes_accessed=100 * 2**20, transcendentals=0),
        compiler_params=params(12),
        name="order",
    )(where_arr, tile_list)


def take_lanes(chunk_of, chunks, index):
    at = jnp.broadcast_to(index, (8, 128))
    lane = at & 127
    chunk = at >> 7
    out = []
    for g in range(ROWS // 8):
        found = jnp.take_along_axis(chunk_of(g, 0), lane, axis=1)
        out.append(found)
    for c in range(1, chunks):
        here = chunk == c
        for g in range(ROWS // 8):
            out[g] = jnp.where(here, jnp.take_along_axis(chunk_of(g, c), lane, axis=1), out[g])
    return out


def heights_kernel(cur, depth, left, right, cells, hbuf, ubuf, own):
    lane = lax.broadcasted_iota(jnp.int32, (ROWS, 128), 1)
    first, last = lane == 0, lane == 127

    def old(c, v):
        if c < 0:
            x = left[:ROWS, :]
            return x if v else pltpu.roll(x, ROWS, 1)
        if c == CHUNKS:
            x = right[:ROWS, :]
            return pltpu.roll(x, ROWS, 1) if v else x
        return cur[pl.ds(2 * c + v, ROWS, stride=2 * CHUNKS), :]

    def scaled_depth(c):
        if c < 0:
            row = left[ROWS : ROWS + 1, :]
        elif c == CHUNKS:
            row = right[ROWS : ROWS + 1, :]
        else:
            row = depth[c : c + 1, :]
        return 0.9 * row

    def height_step(h_of, u_of):
        before = None
        for c in range(-1, CHUNKS + 1):
            u = u_of(c)
            turned = pltpu.roll(u, 1, 1)
            previous = turned if before is None else jnp.where(first, before, turned)
            before = turned
            hbuf[c + 1] = h_of(c) - scaled_depth(c) * (u - previous)

    height_step(lambda c: old(c, 0), lambda c: old(c, 1))
    turned = pltpu.roll(hbuf[0], 127, 1)
    for c in range(-1, CHUNKS + 1):
        after = pltpu.roll(hbuf[c + 2], 127, 1) if c < CHUNKS else turned
        following = jnp.where(last, after, turned)
        turned = after
        ubuf[c + 1] = old(c, 1) - 0.9 * (following - hbuf[c + 1])
    height_step(lambda c: hbuf[c + 1], lambda c: ubuf[c + 1])

    for j in range(OBS // 128):
        rows = take_lanes(lambda g, c: hbuf[c + 1, g * 8 : g * 8 + 8, :], CHUNKS, cells[j : j + 1, :])
        for g in range(ROWS // 8):
            own[g * 8 : g * 8 + 8, j * 128 : (j + 1) * 128] = rows[g]


def heights(cur, depth, left, right, cells):
    buffer = jax.ShapeDtypeStruct((CHUNKS + 2, ROWS, 128), f32)
    return pl.pallas_call(
        heights_kernel,
        out_shape=(buffer, buffer, jax.ShapeDtypeStruct((ROWS, OBS), f32)),
        in_specs=[VMEM] * 5,
        out_specs=(VMEM,) * 3,
        compiler_params=params(12),
        cost_estimate=cost(10**12),
        name="heights",
    )(cur, depth, left, right, cells)


def fields_kernel(hbuf, ubuf, fields):
    last = lax.broadcasted_iota(jnp.int32, (ROWS, 128), 1) == 127
    turned = pltpu.roll(hbuf[1], 127, 1)
    for c in range(CHUNKS):
        h = hbuf[c + 1]
        after = pltpu.roll(hbuf[c + 2], 127, 1)
        following = jnp.where(last, after, turned)
        turned = after
        at = (c % 2) * 128
        fields[c // 2, :, at : at + 128] = h
        at += CELLS_TILE
        fields[c // 2, :, at : at + 128] = ubuf[c + 1] - 0.9 * (following - h)


def fields_by_tile(hbuf, ubuf):
    return pl.pallas_call(
        fields_kernel,
        out_shape=jax.ShapeDtypeStruct((PARTS, ROWS, STATE), f32),
        in_specs=[VMEM] * 2,
        out_specs=VMEM,
        compiler_params=params(8),
        cost_estimate=cost(1000),
        name="fields",
    )(hbuf, ubuf)


def pick_kernel(bounds, lists, below, own, above, out, source):
    for n, part in enumerate((below, own, above)):
        for c in range(8):
            source[n * 8 + c] = part[:, c * 128 : (c + 1) * 128]

    def block(i, carry):
        k = i // 8
        j = i % 8
        at = jnp.broadcast_to(lists[k, pl.ds(j, 1), :], (8, 128))
        lane = at & 127
        chunk = at >> 7

        def rows(c):
            return [
                jnp.take_along_axis(source[c, g * 8 : g * 8 + 8, :], lane, axis=1)
                for g in range(ROWS // 8)
            ]

        def more(c, found):
            here = chunk == c
            return tuple(jnp.where(here, new, old) for new, old in zip(rows(c), found))

        low = bounds[k, j, 0] >> 7
        high = bounds[k, j, 127] >> 7
        found = lax.fori_loop(low + 1, high + 1, more, tuple(rows(low)))
        to = pl.ds(pl.multiple_of(j * 128, 128), 128)
        for g in range(ROWS // 8):
            out[k, g * 8 : g * 8 + 8, to] = found[g]
        return carry

    lax.fori_loop(0, PARTS * 8, block, 0)


def pick(lists, below, own, above):
    return pl.pallas_call(
        pick_kernel,
        out_shape=jax.ShapeDtypeStruct((PARTS, ROWS, SLOTS), f32),
        in_specs=[SMEM] + [VMEM] * 4,
        out_specs=VMEM,
        scratch_shapes=[pltpu.VMEM((24, ROWS, 128), f32)],
        compiler_params=params(16),
        cost_estimate=cost(10**12),
        name="pick",
    )(lists, lists, below, own, above)


def slots_kernel(where_ref, rel, values, errors, cells, out):
    tile = where_ref[0]
    center = where_ref[1]
    listed = rel[...]
    at = jnp.maximum(listed, 0)
    lane = at & 127
    chunk = at >> 7
    value = jnp.zeros((8, 128), f32)
    error = jnp.ones((8, 128), f32)
    cell = jnp.zeros((8, 128), jnp.int32)
    for n in range(3):
        t = lax.rem(tile + (TILES - 1 + n), TILES)
        for j in range(8):
            here = chunk == n * 8 + j

            def found(ref):
                row = jnp.broadcast_to(ref[t, j : j + 1, :], (8, 128))
                return jnp.take_along_axis(row, lane, axis=1)

            value = jnp.where(here, found(values), value)
            error = jnp.where(here, found(errors), error)
            cell = jnp.where(here, found(cells), cell)
    distance = jnp.abs(cell - center)
    distance = jnp.minimum(distance, NCELLS - distance).astype(f32)
    weight = jnp.exp(-0.5 * (distance / LOC) ** 2) / (error * error)
    weight = jnp.where(listed >= 0, weight, 0.0)
    for j in range(8):
        out[0:1, j * 128 : (j + 1) * 128] = weight[j : j + 1, :]
        out[1:2, j * 128 : (j + 1) * 128] = value[j : j + 1, :]


def slots(where_arr, rel, values, errors, cells):
    return pl.pallas_call(
        slots_kernel,
        out_shape=jax.ShapeDtypeStruct((8, SLOTS), f32),
        in_specs=[SMEM, VMEM, VMEM, VMEM, VMEM],
        out_specs=VMEM,
        compiler_params=params(8),
        name="slots",
    )(where_arr, rel, values, errors, cells)


def analyse_kernel(predicted, slot_rows, state, gain_hi, gain_lo, analysis, held, result, sems):
    y = predicted[...]
    weight = slot_rows[0:1, :]
    mean = jnp.sum(y, axis=0, keepdims=True) * (1.0 / MEMBERS)
    root_weight = jnp.sqrt(weight)
    spread = (y - mean) * root_weight
    departure = (slot_rows[1:2, :] - mean) * root_weight
    sh, sl = halves(spread)
    dh, dl = halves(jnp.broadcast_to(departure, (16, SLOTS)))
    rows_i = lax.broadcasted_iota(jnp.int32, (MEMBERS, MEMBERS), 0)
    cols_i = lax.broadcasted_iota(jnp.int32, (MEMBERS, MEMBERS), 1)
    eye = jnp.where(rows_i == cols_i, 1.0, 0.0)
    a = dot_nt(sh, sh) + (dot_nt(sh, sl) + dot_nt(sl, sh)) + (MEMBERS - 1.0) * eye
    innovation = (dot_nt(dh, sh) + (dot_nt(dh, sl) + dot_nt(dl, sh)))[0:1, :]
    bound = jnp.max(jnp.sum(jnp.abs(a), axis=0, keepdims=True), axis=1, keepdims=True)
    approx = a / bound

    def two_steps(m):
        mp = halves(m)
        m2 = product(mp, mp)
        q = 1.6875 * eye - 0.5625 * m + 0.0625 * m2
        return 2.25 * eye - 2.4375 * m + product(halves(m2), halves(q))

    r = halves(two_steps(approx))
    z = r
    w = halves(product(halves(approx), r))
    r = halves(two_steps(product(z, w)))
    z, w = halves(product(r, z)), halves(product(w, r))
    r = halves(two_steps(product(z, w)))
    root = product(r, z) * lax.rsqrt(bound)
    once = jnp.sum(root * innovation, axis=1, keepdims=True)
    mean_weight = jnp.sum(root * once, axis=0, keepdims=True)
    moved = math.sqrt(MEMBERS - 1) * root + mean_weight
    gain = moved + (1.0 - jnp.sum(moved, axis=1, keepdims=True)) * (1.0 / MEMBERS)
    gain = halves(gain)
    held[0], held[1] = gain
    copies = [
        pltpu.make_async_copy(held.at[0], gain_hi, sems.at[0]),
        pltpu.make_async_copy(held.at[1], gain_lo, sems.at[1]),
        pltpu.make_async_copy(result, analysis, sems.at[2]),
    ]
    copies[0].start()
    copies[1].start()
    result[...] = product(gain, halves(state[...]))
    copies[2].start()
    for copy in copies:
        copy.wait()


def analyse(predicted, slot_rows, state):
    return pl.pallas_call(
        analyse_kernel,
        out_shape=(
            pltpu.HBM((MEMBERS, MEMBERS), bf16),
            pltpu.HBM((MEMBERS, MEMBERS), bf16),
            pltpu.HBM((MEMBERS, STATE), f32),
        ),
        in_specs=[VMEM, VMEM, VMEM],
        out_specs=(HBM, HBM, HBM),
        scratch_shapes=[
            pltpu.VMEM((2, MEMBERS, MEMBERS), bf16),
            pltpu.VMEM((MEMBERS, STATE), f32),
            pltpu.SemaphoreType.DMA((3,)),
        ],
        compiler_params=params(32),
        name="analyse",
    )(predicted, slot_rows, state)


def smooth_kernel(gain_hi, gain_lo, state, out):
    out[0] = product((gain_hi[...], gain_lo[...]), halves(state[0]))


def smooth(gain_hi, gain_lo, states):
    whole = pl.BlockSpec((MEMBERS, MEMBERS), lambda i: (0, 0))
    one = pl.BlockSpec((1, MEMBERS, STATE), lambda i: (i, 0, 0))
    return pl.pallas_call(
        smooth_kernel,
        out_shape=jax.ShapeDtypeStruct((LAGS, MEMBERS, STATE), f32),
        grid=(LAGS,),
        in_specs=[whole, whole, one],
        out_specs=one,
        compiler_params=params(24),
        cost_estimate=pl.CostEstimate(
            flops=2 * 3 * LAGS * MEMBERS**2 * STATE, bytes_accessed=8 * LAGS * MEMBERS * STATE, transcendentals=0
        ),
        name="smooth",
    )(gain_hi, gain_lo, states)


def assemble_kernel(parts, out):
    for k in range(PARTS):
        for v in range(2):
            for b in range(2):
                at = v * CELLS_TILE + b * 128
                out[pl.ds(2 * (2 * k + b) + v, ROWS, stride=2 * CHUNKS), :] = parts[k, :, at : at + 128]


def assemble(parts):
    return pl.pallas_call(
        assemble_kernel,
        out_shape=jax.ShapeDtypeStruct((ROWS * 2 * CHUNKS, 128), f32),
        in_specs=[VMEM],
        out_specs=VMEM,
        compiler_params=params(24),
        name="assemble",
    )(parts)


def along_tiles(x, by):
    return lax.ppermute(x, "tile", [(i, (i + by) % TILES) for i in range(TILES)])


def exchange(x):
    return lax.all_to_all(x, GROUP, split_axis=0, concat_axis=0, tiled=True)


def per_device(
    current_state, lagged_states, water_depth, obs_cells, obs_values, obs_errors, tile_obs
):
    tile = lax.axis_index("tile")
    part = lax.axis_index("grp") * lax.axis_size("mem") + lax.axis_index("mem")
    where_arr = jnp.stack([tile, tile * CELLS + part * CELLS_TILE + CELLS_TILE // 2])
    cur = current_state.reshape(ROWS, 2, CHUNKS, 128).transpose(0, 2, 1, 3)
    depth = water_depth.reshape(CHUNKS, 128)
    whole = pltpu.with_memory_space_constraint(cur.reshape(ROWS, 2 * CHUNKS, 128), pltpu.HBM)
    to_right, to_left = edges(whole, depth)
    cur = cur.reshape(ROWS * 2 * CHUNKS, 128)
    left = along_tiles(to_right, 1)
    right = along_tiles(to_left, -1)
    to_left, where_arr = lax.optimization_barrier((to_left, where_arr))
    ordered, copies = order(where_arr, tile_obs[0, 0].reshape(8, 128))
    lists = exchange(copies)
    left, right, copies = lax.optimization_barrier((left, right, copies))
    local_cells = lax.dynamic_slice_in_dim(obs_cells, tile * OBS, OBS) - tile * CELLS
    hbuf, ubuf, own = heights(cur, depth, left, right, local_cells.reshape(8, 128))
    own, lists = lax.optimization_barrier((own, lists))
    below = along_tiles(own, 1)
    above = along_tiles(own, -1)
    state = exchange(fields_by_tile(hbuf, ubuf)).reshape(MEMBERS, STATE)
    picked = pick(lists, below, own, above)
    predicted = exchange(picked).reshape(MEMBERS, SLOTS)
    slot_rows = slots(
        where_arr,
        ordered,
        obs_values.reshape(TILES, 8, 128),
        obs_errors.reshape(TILES, 8, 128),
        obs_cells.reshape(TILES, 8, 128),
    )
    gain_hi, gain_lo, analysis = analyse(predicted, slot_rows, state)
    returned = exchange(analysis.reshape(PARTS, ROWS, STATE))
    older = smooth(gain_hi, gain_lo, lagged_states.reshape(LAGS, MEMBERS, STATE))
    analysed = assemble(returned).reshape(ROWS, CHUNKS, 2, 128).transpose(0, 2, 1, 3)
    return (
        analysed.reshape(ROWS, 2, CELLS),
        older.reshape(LAGS, 1, 1, MEMBERS, STATE),
    )


def solution(mesh):
    placed = (
        P(GROUP, None, "tile"),
        P(None, "tile", GROUP, None, None),
        P("tile"),
        P(),
        P(),
        P(),
        P("tile", GROUP, None),
    )
    return jax.shard_map(
        per_device,
        mesh=mesh,
        in_specs=placed,
        out_specs=(P(GROUP, None, "tile"), P(None, "tile", GROUP, None, None)),
        check_vma=False,
    )
```

```python
import functools
import math

import jax
import jax.numpy as jnp
from jax import lax
from jax.experimental import pallas as pl
from jax.experimental.pallas import tpu as pltpu
from jax.sharding import PartitionSpec as P

GROUP = ("grp", "mem")
PARTS = 8
ROWS = 64
MEMBERS = 512
CELLS = 2048
CHUNKS = 16
CELLS_TILE = 256
STATE = 512
OBS = 1024
SLOTS = 1024
NOBS = 32768
NCELLS = 65536
TILES = 32
LOC = 512
LAGS = 3
DIRECT = 3
f32 = jnp.float32
bf16 = jnp.bfloat16
VMEM = pl.BlockSpec(memory_space=pltpu.VMEM)
HBM = pl.BlockSpec(memory_space=pltpu.HBM)
SMEM = pl.BlockSpec(memory_space=pltpu.SMEM)


def params(mib):
    return pltpu.CompilerParams(vmem_limit_bytes=mib * 1024 * 1024)


def cost(flops):
    return pl.CostEstimate(flops=flops, bytes_accessed=2**20, transcendentals=0)


def halves(x):
    hi = x.astype(bf16)
    return hi, (x - hi.astype(f32)).astype(bf16)


def dot(a, b):
    return jnp.dot(a, b, preferred_element_type=f32)


def dot_nt(a, b):
    return lax.dot_general(a, b, (((1,), (1,)), ((), ())), preferred_element_type=f32)


def product(a, b):
    (ah, al), (bh, bl) = a, b
    return dot(ah, bh) + (dot(ah, bl) + dot(al, bh))


def edges_kernel(cur, far_depth, to_right, to_left, ends, depth, sems):
    copies = [
        pltpu.make_async_copy(cur.at[:, pl.ds(at, 8), :], ends.at[n], sems.at[n])
        for n, at in enumerate((0, 2 * CHUNKS - 8))
    ]
    copies.append(pltpu.make_async_copy(far_depth, depth, sems.at[2]))
    for copy in copies:
        copy.start()
    low_half = lax.broadcasted_iota(jnp.int32, (ROWS, 128), 1) < ROWS
    end = CHUNKS - 1
    copies[2].wait()
    to_right[ROWS:, :] = jnp.broadcast_to(depth[end : end + 1, :], (8, 128))
    to_left[ROWS:, :] = jnp.broadcast_to(depth[0:1, :], (8, 128))
    copies[1].wait()
    h, u = ends[1, :, 6, :], ends[1, :, 7, :]
    to_right[:ROWS, :] = jnp.where(low_half, pltpu.roll(h, ROWS, 1), u)
    copies[0].wait()
    h, u = ends[0, :, 0, :], ends[0, :, 1, :]
    to_left[:ROWS, :] = jnp.where(low_half, h, pltpu.roll(u, ROWS, 1))


def edges(cur, depth):
    message = jax.ShapeDtypeStruct((ROWS + 8, 128), f32)
    return pl.pallas_call(
        edges_kernel,
        out_shape=(message, message),
        in_specs=[HBM, HBM],
        out_specs=(VMEM, VMEM),
        scratch_shapes=[
            pltpu.VMEM((2, ROWS, 8, 128), f32),
            pltpu.VMEM((CHUNKS, 128), f32),
            pltpu.SemaphoreType.DMA((3,)),
        ],
        compiler_params=params(8),
        name="edges",
    )(cur, depth)


def order_kernel(
    far_list, far_cur, far_depth, far_cells,
    ordered, copies, cur, depth, cells, tile_list, row_list, row_place, sems,
):
    tile = lax.axis_index("tile")
    arrivals = [
        pltpu.make_async_copy(source, target, sems.at[n])
        for n, (source, target) in enumerate(
            ((far_list, tile_list), (far_cells.at[tile], cells), (far_depth, depth), (far_cur, cur))
        )
    ]
    for arrival in arrivals:
        arrival.start()
    arrivals[0].wait()
    listed = tile_list[...]
    rel = jnp.where(listed >= 0, (listed - (tile - 1) * OBS) & (NOBS - 1), -1)
    count = jnp.sum(jnp.where(rel >= 0, 1.0, 0.0))
    top = jnp.max(rel)
    for j in range(8):
        row_list[0:1, j * 128 : (j + 1) * 128] = rel[j : j + 1, :]
    row = row_list[0:1, :]
    chunks = 3 * OBS // 128

    def iota(shape, dim):
        return lax.broadcasted_iota(jnp.int32, shape, dim)

    def flags(x):
        return jnp.where(x, 1.0, 0.0).astype(bf16)

    in_chunk = flags((row >> 7) == iota((32, SLOTS), 0))
    in_lane = flags((row & 127) == iota((128, SLOTS), 0))
    present = dot_nt(in_chunk, in_lane).astype(bf16)
    before = dot(present, flags(iota((128, 128), 0) < iota((128, 128), 1)))
    totals = dot(present, jnp.ones((128, 128), bf16)).astype(bf16)
    place = before + dot(flags(iota((32, 32), 1) < iota((32, 32), 0)), totals)
    place = jnp.where(present.astype(f32) > 0.5, place, -1.0).astype(jnp.int32)
    for c in range(chunks):
        row_place[0:1, c * 128 : (c + 1) * 128] = place[c : c + 1, :]
    row = row_place[0:1, :]
    wide = 3 * OBS
    to_row = (row >> 7) == iota((8, wide), 0)
    number = iota((8, wide), 1)
    parts = jnp.concatenate(
        [jnp.where(to_row, number >> 7, 0), jnp.where(to_row, number & 127, 0)], axis=0
    )
    found = dot_nt(parts.astype(f32).astype(bf16), flags((row & 127) == iota((128, wide), 0)))
    found = (found[:8] * 128.0 + found[8:]).astype(jnp.int32)
    used = (iota((8, 128), 0) * 128 + iota((8, 128), 1)).astype(f32) < count
    ordered[...] = jnp.where(used, found, -1)
    filled = jnp.where(used, found, jnp.maximum(top, 0))
    for k in range(PARTS):
        copies[k] = filled
    for arrival in arrivals[1:]:
        arrival.wait()
    cells[...] = cells[...] - tile * CELLS


def order(tile_list, cur, depth, cells):
    return pl.pallas_call(
        order_kernel,
        out_shape=(
            jax.ShapeDtypeStruct((8, 128), jnp.int32),
            jax.ShapeDtypeStruct((PARTS, 8, 128), jnp.int32),
            jax.ShapeDtypeStruct(cur.shape, f32),
            jax.ShapeDtypeStruct(depth.shape, f32),
            jax.ShapeDtypeStruct((8, 128), jnp.int32),
        ),
        in_specs=[HBM] * 4,
        out_specs=(VMEM,) * 5,
        scratch_shapes=[
            pltpu.VMEM((8, 128), jnp.int32),
            pltpu.VMEM((8, SLOTS), jnp.int32),
            pltpu.VMEM((8, 3 * OBS), jnp.int32),
            pltpu.SemaphoreType.DMA((4,)),
        ],
        cost_estimate=pl.CostEstimate(flops=0, bytes_accessed=100 * 2**20, transcendentals=0),
        compiler_params=params(12),
        name="order",
    )(tile_list, cur, depth, cells)


def take_lanes(chunk_of, chunks, index):
    at = jnp.broadcast_to(index, (8, 128))
    lane = at & 127
    chunk = at >> 7
    out = []
    for g in range(ROWS // 8):
        found = jnp.take_along_axis(chunk_of(g, 0), lane, axis=1)
        out.append(found)
    for c in range(1, chunks):
        here = chunk == c
        for g in range(ROWS // 8):
            out[g] = jnp.where(here, jnp.take_along_axis(chunk_of(g, c), lane, axis=1), out[g])
    return out


def heights_kernel(cur, depth, left, right, cells, hbuf, ubuf, own):
    lane = lax.broadcasted_iota(jnp.int32, (ROWS, 128), 1)
    first, last = lane == 0, lane == 127

    def old(c, v):
        if c < 0:
            x = left[:ROWS, :]
            return x if v else pltpu.roll(x, ROWS, 1)
        if c == CHUNKS:
            x = right[:ROWS, :]
            return pltpu.roll(x, ROWS, 1) if v else x
        return cur[pl.ds(2 * c + v, ROWS, stride=2 * CHUNKS), :]

    def scaled_depth(c):
        if c < 0:
            row = left[ROWS : ROWS + 1, :]
        elif c == CHUNKS:
            row = right[ROWS : ROWS + 1, :]
        else:
            row = depth[c : c + 1, :]
        return 0.9 * row

    def height_step(h_of, u_of):
        before = None
        for c in range(-1, CHUNKS + 1):
            u = u_of(c)
            turned = pltpu.roll(u, 1, 1)
            previous = turned if before is None else jnp.where(first, before, turned)
            before = turned
            hbuf[c + 1] = h_of(c) - scaled_depth(c) * (u - previous)

    height_step(lambda c: old(c, 0), lambda c: old(c, 1))
    turned = pltpu.roll(hbuf[0], 127, 1)
    for c in range(-1, CHUNKS + 1):
        after = pltpu.roll(hbuf[c + 2], 127, 1) if c < CHUNKS else turned
        following = jnp.where(last, after, turned)
        turned = after
        ubuf[c + 1] = old(c, 1) - 0.9 * (following - hbuf[c + 1])
    height_step(lambda c: hbuf[c + 1], lambda c: ubuf[c + 1])

    for j in range(OBS // 128):
        rows = take_lanes(lambda g, c: hbuf[c + 1, g * 8 : g * 8 + 8, :], CHUNKS, cells[j : j + 1, :])
        for g in range(ROWS // 8):
            own[g * 8 : g * 8 + 8, j * 128 : (j + 1) * 128] = rows[g]


def heights(cur, depth, left, right, cells):
    buffer = jax.ShapeDtypeStruct((CHUNKS + 2, ROWS, 128), f32)
    return pl.pallas_call(
        heights_kernel,
        out_shape=(buffer, buffer, jax.ShapeDtypeStruct((ROWS, OBS), f32)),
        in_specs=[VMEM] * 5,
        out_specs=(VMEM,) * 3,
        compiler_params=params(12),
        cost_estimate=cost(10**12),
        name="heights",
    )(cur, depth, left, right, cells)


def fields_kernel(hbuf, ubuf, fields):
    last = lax.broadcasted_iota(jnp.int32, (ROWS, 128), 1) == 127
    turned = pltpu.roll(hbuf[1], 127, 1)
    for c in range(CHUNKS):
        h = hbuf[c + 1]
        after = pltpu.roll(hbuf[c + 2], 127, 1)
        following = jnp.where(last, after, turned)
        turned = after
        at = (c % 2) * 128
        fields[c // 2, :, at : at + 128] = h
        at += CELLS_TILE
        fields[c // 2, :, at : at + 128] = ubuf[c + 1] - 0.9 * (following - h)


def fields_by_tile(hbuf, ubuf):
    return pl.pallas_call(
        fields_kernel,
        out_shape=jax.ShapeDtypeStruct((PARTS, ROWS, STATE), f32),
        in_specs=[VMEM] * 2,
        out_specs=VMEM,
        compiler_params=params(8),
        cost_estimate=cost(1000),
        name="fields",
    )(hbuf, ubuf)


def pick_kernel(bounds, lists, below, own, above, out, source, held, sems):
    for n, part in enumerate((below, own, above)):
        for c in range(8):
            source[n * 8 + c] = part[:, c * 128 : (c + 1) * 128]

    def send(k):
        return pltpu.make_async_copy(held.at[k], out.at[k], sems.at[k])

    def take(c, g, lane):
        return jnp.take_along_axis(source[c, g * 8 : g * 8 + 8, :], lane, axis=1)

    def one_list(k, carry):
        blocks = []
        for j in range(8):
            at = jnp.broadcast_to(lists[k, j : j + 1, :], (8, 128))
            lane, chunk = at & 127, at >> 7
            low, high = bounds[k, j, 0] >> 7, bounds[k, j, 127] >> 7
            blocks.append((j, lane, chunk, low, high))
            found = [take(low, g, lane) for g in range(ROWS // 8)]
            for d in range(1, DIRECT):
                here = chunk == low + d
                found = [jnp.where(here, take(low + d, g, lane), f) for g, f in enumerate(found)]
            for g in range(ROWS // 8):
                held[k, g * 8 : g * 8 + 8, j * 128 : (j + 1) * 128] = found[g]
        for j, lane, chunk, low, high in blocks:

            def more(c, carry):
                here = chunk == c
                for g in range(ROWS // 8):
                    at = (k, slice(g * 8, g * 8 + 8), slice(j * 128, (j + 1) * 128))
                    held[at] = jnp.where(here, take(c, g, lane), held[at])
                return carry

            lax.fori_loop(low + DIRECT, high + 1, more, 0)
        send(k).start()
        return carry

    lax.fori_loop(0, PARTS, one_list, 0)
    for k in range(PARTS):
        send(k).wait()


def pick(lists, below, own, above):
    return pl.pallas_call(
        pick_kernel,
        out_shape=pltpu.HBM((PARTS, ROWS, SLOTS), f32),
        in_specs=[SMEM] + [VMEM] * 4,
        out_specs=HBM,
        scratch_shapes=[
            pltpu.VMEM((24 + DIRECT, ROWS, 128), f32),
            pltpu.VMEM((PARTS, ROWS, SLOTS), f32),
            pltpu.SemaphoreType.DMA((PARTS,)),
        ],
        compiler_params=params(16),
        cost_estimate=cost(10**12),
        name="pick",
    )(lists, lists, below, own, above)


def slots_kernel(rel, values, errors, cells, out):
    tile = lax.axis_index("tile")
    part = lax.axis_index("grp") * lax.axis_size("mem") + lax.axis_index("mem")
    center = tile * CELLS + part * CELLS_TILE + CELLS_TILE // 2
    listed = rel[...]
    at = jnp.maximum(listed, 0)
    lane = at & 127
    chunk = at >> 7
    value = jnp.zeros((8, 128), f32)
    error = jnp.ones((8, 128), f32)
    cell = jnp.zeros((8, 128), jnp.int32)
    for n in range(3):
        t = lax.rem(tile + (TILES - 1 + n), TILES)
        for j in range(8):
            here = chunk == n * 8 + j

            def found(ref):
                row = jnp.broadcast_to(ref[t, j : j + 1, :], (8, 128))
                return jnp.take_along_axis(row, lane, axis=1)

            value = jnp.where(here, found(values), value)
            error = jnp.where(here, found(errors), error)
            cell = jnp.where(here, found(cells), cell)
    distance = jnp.abs(cell - center)
    distance = jnp.minimum(distance, NCELLS - distance).astype(f32)
    weight = jnp.exp(-0.5 * (distance / LOC) ** 2) / (error * error)
    weight = jnp.where(listed >= 0, weight, 0.0)
    for j in range(8):
        out[0:1, j * 128 : (j + 1) * 128] = weight[j : j + 1, :]
        out[1:2, j * 128 : (j + 1) * 128] = value[j : j + 1, :]


def slots(rel, values, errors, cells):
    return pl.pallas_call(
        slots_kernel,
        out_shape=jax.ShapeDtypeStruct((8, SLOTS), f32),
        in_specs=[VMEM] * 4,
        out_specs=VMEM,
        compiler_params=params(8),
        name="slots",
    )(rel, values, errors, cells)


def analyse_kernel(predicted, slot_rows, state, gain_hi, gain_lo, analysis, held, result, sems):
    y = predicted[...]
    weight = slot_rows[0:1, :]
    mean = jnp.sum(y, axis=0, keepdims=True) * (1.0 / MEMBERS)
    root_weight = jnp.sqrt(weight)
    spread = (y - mean) * root_weight
    departure = (slot_rows[1:2, :] - mean) * root_weight
    sh, sl = halves(spread)
    dh, dl = halves(jnp.broadcast_to(departure, (16, SLOTS)))
    rows_i = lax.broadcasted_iota(jnp.int32, (MEMBERS, MEMBERS), 0)
    cols_i = lax.broadcasted_iota(jnp.int32, (MEMBERS, MEMBERS), 1)
    eye = jnp.where(rows_i == cols_i, 1.0, 0.0)
    a = dot_nt(sh, sh) + (dot_nt(sh, sl) + dot_nt(sl, sh)) + (MEMBERS - 1.0) * eye
    innovation = (dot_nt(dh, sh) + (dot_nt(dh, sl) + dot_nt(dl, sh)))[0:1, :]
    bound = jnp.max(jnp.sum(jnp.abs(a), axis=0, keepdims=True), axis=1, keepdims=True)
    approx = a / bound

    def two_steps(m):
        mp = halves(m)
        m2 = product(mp, mp)
        q = 1.6875 * eye - 0.5625 * m + 0.0625 * m2
        return 2.25 * eye - 2.4375 * m + product(halves(m2), halves(q))

    r = halves(two_steps(approx))
    z = r
    w = halves(product(halves(approx), r))
    r = halves(two_steps(product(z, w)))
    z, w = halves(product(r, z)), halves(product(w, r))
    r = halves(two_steps(product(z, w)))
    root = product(r, z) * lax.rsqrt(bound)
    once = jnp.sum(root * innovation, axis=1, keepdims=True)
    mean_weight = jnp.sum(root * once, axis=0, keepdims=True)
    moved = math.sqrt(MEMBERS - 1) * root + mean_weight
    gain = moved + (1.0 - jnp.sum(moved, axis=1, keepdims=True)) * (1.0 / MEMBERS)
    gain = halves(gain)
    held[0], held[1] = gain
    copies = [
        pltpu.make_async_copy(held.at[0], gain_hi, sems.at[0]),
        pltpu.make_async_copy(held.at[1], gain_lo, sems.at[1]),
        pltpu.make_async_copy(result, analysis, sems.at[2]),
    ]
    copies[0].start()
    copies[1].start()
    analysed = product(gain, halves(state[...]))
    for row in range(4):
        at = (row % 2) * CELLS_TILE + (row // 2) * 128
        result[pl.ds(row, MEMBERS, stride=4), :] = analysed[:, at : at + 128]
    copies[2].start()
    for copy in copies:
        copy.wait()


def analyse(predicted, slot_rows, state):
    return pl.pallas_call(
        analyse_kernel,
        out_shape=(
            pltpu.HBM((MEMBERS, MEMBERS), bf16),
            pltpu.HBM((MEMBERS, MEMBERS), bf16),
            pltpu.HBM((MEMBERS * 4, 128), f32),
        ),
        in_specs=[VMEM, VMEM, VMEM],
        out_specs=(HBM, HBM, HBM),
        scratch_shapes=[
            pltpu.VMEM((2, MEMBERS, MEMBERS), bf16),
            pltpu.VMEM((MEMBERS * 4, 128), f32),
            pltpu.SemaphoreType.DMA((3,)),
        ],
        compiler_params=params(32),
        name="analyse",
    )(predicted, slot_rows, state)


def smooth_kernel(gain_hi, gain_lo, state, out):
    out[0] = product((gain_hi[...], gain_lo[...]), halves(state[0]))


def smooth(gain_hi, gain_lo, states):
    whole = pl.BlockSpec((MEMBERS, MEMBERS), lambda i: (0, 0))
    one = pl.BlockSpec((1, MEMBERS, STATE), lambda i: (i, 0, 0))
    return pl.pallas_call(
        smooth_kernel,
        out_shape=jax.ShapeDtypeStruct((LAGS, MEMBERS, STATE), f32),
        grid=(LAGS,),
        in_specs=[whole, whole, one],
        out_specs=one,
        compiler_params=params(24),
        cost_estimate=pl.CostEstimate(
            flops=2 * 3 * LAGS * MEMBERS**2 * STATE, bytes_accessed=8 * LAGS * MEMBERS * STATE, transcendentals=0
        ),
        name="smooth",
    )(gain_hi, gain_lo, states)


def assemble_kernel(parts, out, sems):
    copies = [pltpu.make_async_copy(parts.at[k], out.at[:, k], sems.at[k]) for k in range(PARTS)]
    for copy in copies:
        copy.start()
    for copy in copies:
        copy.wait()


def assemble(parts):
    return pl.pallas_call(
        assemble_kernel,
        out_shape=pltpu.HBM((ROWS, PARTS, 4, 128), f32),
        in_specs=[pl.BlockSpec(memory_space=pl.ANY)],
        out_specs=HBM,
        scratch_shapes=[pltpu.SemaphoreType.DMA((PARTS,))],
        compiler_params=params(8),
        name="assemble",
    )(parts)


def along_tiles(x, by):
    return lax.ppermute(x, "tile", [(i, (i + by) % TILES) for i in range(TILES)])


def far(x):
    return pltpu.with_memory_space_constraint(x, pltpu.HBM)


def exchange(x):
    return lax.all_to_all(x, GROUP, split_axis=0, concat_axis=0, tiled=True)


def per_device(
    current_state, lagged_states, water_depth, obs_cells, obs_values, obs_errors, tile_obs
):
    cur = current_state.reshape(ROWS, 2, CHUNKS, 128).transpose(0, 2, 1, 3)
    depth = water_depth.reshape(CHUNKS, 128)
    to_right, to_left = edges(far(cur.reshape(ROWS, 2 * CHUNKS, 128)), far(depth))
    left = along_tiles(to_right, 1)
    right = along_tiles(to_left, -1)
    to_left, listed = lax.optimization_barrier((to_left, tile_obs[0, 0].reshape(8, 128)))
    ordered, copies, cur, depth, cells = order(
        far(listed),
        far(cur.reshape(ROWS * 2 * CHUNKS, 128)),
        far(depth),
        far(obs_cells.reshape(TILES, 8, 128)),
    )
    lists = exchange(copies)
    hbuf, ubuf, own = heights(cur, depth, left, right, cells)
    own, lists = lax.optimization_barrier((own, lists))
    below = along_tiles(own, 1)
    above = along_tiles(own, -1)
    state = exchange(fields_by_tile(hbuf, ubuf)).reshape(MEMBERS, STATE)
    picked = pick(lists, below, own, above)
    predicted = exchange(picked).reshape(MEMBERS, SLOTS)
    slot_rows = slots(
        ordered,
        obs_values.reshape(TILES, 8, 128),
        obs_errors.reshape(TILES, 8, 128),
        obs_cells.reshape(TILES, 8, 128),
    )
    gain_hi, gain_lo, analysis = analyse(predicted, slot_rows, state)
    returned = exchange(analysis.reshape(PARTS, ROWS * 4, 128))
    older = smooth(gain_hi, gain_lo, lagged_states.reshape(LAGS, MEMBERS, STATE))
    analysed = assemble(returned.reshape(PARTS, ROWS, 4, 128))
    analysed = analysed.reshape(ROWS, CHUNKS, 2, 128).transpose(0, 2, 1, 3)
    return (
        analysed.reshape(ROWS, 2, CELLS),
        older.reshape(LAGS, 1, 1, MEMBERS, STATE),
    )


def solution(mesh):
    placed = (
        P(GROUP, None, "tile"),
        P(None, "tile", GROUP, None, None),
        P("tile"),
        P(),
        P(),
        P(),
        P("tile", GROUP, None),
    )
    return jax.shard_map(
        per_device,
        mesh=mesh,
        in_specs=placed,
        out_specs=(P(GROUP, None, "tile"), P(None, "tile", GROUP, None, None)),
        check_vma=False,
    )
```

```python
import functools
import math

import jax
import jax.numpy as jnp
from jax import lax
from jax.experimental import pallas as pl
from jax.experimental.pallas import tpu as pltpu
from jax.sharding import PartitionSpec as P

GROUP = ("grp", "mem")
PARTS = 8
ROWS = 64
MEMBERS = 512
CELLS = 2048
CHUNKS = 16
CELLS_TILE = 256
STATE = 512
OBS = 1024
SLOTS = 1024
NOBS = 32768
NCELLS = 65536
TILES = 32
LOC = 512
LAGS = 3
DIRECT = 3
f32 = jnp.float32
bf16 = jnp.bfloat16
VMEM = pl.BlockSpec(memory_space=pltpu.VMEM)
HBM = pl.BlockSpec(memory_space=pltpu.HBM)
SMEM = pl.BlockSpec(memory_space=pltpu.SMEM)


def params(mib):
    return pltpu.CompilerParams(vmem_limit_bytes=mib * 1024 * 1024)


def cost(flops):
    return pl.CostEstimate(flops=flops, bytes_accessed=2**20, transcendentals=0)


def halves(x):
    hi = x.astype(bf16)
    return hi, (x - hi.astype(f32)).astype(bf16)


def dot(a, b):
    return jnp.dot(a, b, preferred_element_type=f32)


def dot_nt(a, b):
    return lax.dot_general(a, b, (((1,), (1,)), ((), ())), preferred_element_type=f32)


def product(a, b):
    (ah, al), (bh, bl) = a, b
    return dot(ah, bh) + (dot(ah, bl) + dot(al, bh))


def edges_kernel(cur, far_depth, to_right, to_left, ends, depth, sems):
    copies = [
        pltpu.make_async_copy(cur.at[:, pl.ds(at, 8), :], ends.at[n], sems.at[n])
        for n, at in enumerate((0, 2 * CHUNKS - 8))
    ]
    copies.append(pltpu.make_async_copy(far_depth, depth, sems.at[2]))
    for copy in copies:
        copy.start()
    low_half = lax.broadcasted_iota(jnp.int32, (ROWS, 128), 1) < ROWS
    end = CHUNKS - 1
    copies[2].wait()
    to_right[ROWS:, :] = jnp.broadcast_to(depth[end : end + 1, :], (8, 128))
    to_left[ROWS:, :] = jnp.broadcast_to(depth[0:1, :], (8, 128))
    copies[1].wait()
    h, u = ends[1, :, 6, :], ends[1, :, 7, :]
    to_right[:ROWS, :] = jnp.where(low_half, pltpu.roll(h, ROWS, 1), u)
    copies[0].wait()
    h, u = ends[0, :, 0, :], ends[0, :, 1, :]
    to_left[:ROWS, :] = jnp.where(low_half, h, pltpu.roll(u, ROWS, 1))


def edges(cur, depth):
    message = jax.ShapeDtypeStruct((ROWS + 8, 128), f32)
    return pl.pallas_call(
        edges_kernel,
        out_shape=(message, message),
        in_specs=[HBM, HBM],
        out_specs=(VMEM, VMEM),
        scratch_shapes=[
            pltpu.VMEM((2, ROWS, 8, 128), f32),
            pltpu.VMEM((CHUNKS, 128), f32),
            pltpu.SemaphoreType.DMA((3,)),
        ],
        compiler_params=params(8),
        name="edges",
    )(cur, depth)


def order_kernel(
    far_list, far_parts, far_cur, far_depth, far_cells,
    ordered, payload, cur, depth, cells, tile_list, row_list, row_place, filled, sems, sent,
):
    tile = lax.axis_index("tile")
    arrivals = [
        pltpu.make_async_copy(source, target, sems.at[n])
        for n, (source, target) in enumerate(
            ((far_list, tile_list), (far_cells.at[tile], cells), (far_depth, depth), (far_cur, cur))
        )
    ]
    raw = [
        pltpu.make_async_copy(far_parts.at[:, k], payload.at[k, pl.ds(0, ROWS)], sent.at[k])
        for k in range(PARTS)
    ]
    for arrival in arrivals + raw:
        arrival.start()
    arrivals[0].wait()
    listed = tile_list[...]
    rel = jnp.where(listed >= 0, (listed - (tile - 1) * OBS) & (NOBS - 1), -1)
    count = jnp.sum(jnp.where(rel >= 0, 1.0, 0.0))
    top = jnp.max(rel)
    for j in range(8):
        row_list[0:1, j * 128 : (j + 1) * 128] = rel[j : j + 1, :]
    row = row_list[0:1, :]
    chunks = 3 * OBS // 128

    def iota(shape, dim):
        return lax.broadcasted_iota(jnp.int32, shape, dim)

    def flags(x):
        return jnp.where(x, 1.0, 0.0).astype(bf16)

    in_chunk = flags((row >> 7) == iota((32, SLOTS), 0))
    in_lane = flags((row & 127) == iota((128, SLOTS), 0))
    present = dot_nt(in_chunk, in_lane).astype(bf16)
    before = dot(present, flags(iota((128, 128), 0) < iota((128, 128), 1)))
    totals = dot(present, jnp.ones((128, 128), bf16)).astype(bf16)
    place = before + dot(flags(iota((32, 32), 1) < iota((32, 32), 0)), totals)
    place = jnp.where(present.astype(f32) > 0.5, place, -1.0).astype(jnp.int32)
    for c in range(chunks):
        row_place[0:1, c * 128 : (c + 1) * 128] = place[c : c + 1, :]
    row = row_place[0:1, :]
    wide = 3 * OBS
    to_row = (row >> 7) == iota((8, wide), 0)
    number = iota((8, wide), 1)
    parts = jnp.concatenate(
        [jnp.where(to_row, number >> 7, 0), jnp.where(to_row, number & 127, 0)], axis=0
    )
    found = dot_nt(parts.astype(f32).astype(bf16), flags((row & 127) == iota((128, wide), 0)))
    found = (found[:8] * 128.0 + found[8:]).astype(jnp.int32)
    used = (iota((8, 128), 0) * 128 + iota((8, 128), 1)).astype(f32) < count
    ordered[...] = jnp.where(used, found, -1)
    whole = jnp.where(used, found, jnp.maximum(top, 0)).astype(f32)
    filled[0], filled[1] = whole[:4], whole[4:]
    lists = [
        pltpu.make_async_copy(filled, payload.at[k, pl.ds(ROWS, 2)], sent.at[PARTS + k])
        for k in range(PARTS)
    ]
    for copy in lists:
        copy.start()
    for copy in arrivals[1:] + raw + lists:
        copy.wait()
    cells[...] = cells[...] - tile * CELLS


def order(tile_list, parts, cur, depth, cells):
    return pl.pallas_call(
        order_kernel,
        out_shape=(
            jax.ShapeDtypeStruct((8, 128), jnp.int32),
            pltpu.HBM((PARTS, ROWS + 4, 4, 128), f32),
            jax.ShapeDtypeStruct((ROWS * 2 * CHUNKS, 128), f32),
            jax.ShapeDtypeStruct((CHUNKS, 128), f32),
            jax.ShapeDtypeStruct((8, 128), jnp.int32),
        ),
        in_specs=[HBM] * 5,
        out_specs=(VMEM, HBM, VMEM, VMEM, VMEM),
        scratch_shapes=[
            pltpu.VMEM((8, 128), jnp.int32),
            pltpu.VMEM((8, SLOTS), jnp.int32),
            pltpu.VMEM((8, 3 * OBS), jnp.int32),
            pltpu.VMEM((2, 4, 128), f32),
            pltpu.SemaphoreType.DMA((4,)),
            pltpu.SemaphoreType.DMA((2 * PARTS,)),
        ],
        cost_estimate=pl.CostEstimate(flops=0, bytes_accessed=100 * 2**20, transcendentals=0),
        compiler_params=params(12),
        name="order",
    )(tile_list, parts, cur, depth, cells)


def chunk_with_halo(cur, left, right, c, v):
    if c < 0:
        x = left[:ROWS, :]
        return x if v else pltpu.roll(x, ROWS, 1)
    if c == CHUNKS:
        x = right[:ROWS, :]
        return pltpu.roll(x, ROWS, 1) if v else x
    return cur[pl.ds(2 * c + v, ROWS, stride=2 * CHUNKS), :]


def beside_kernel(_, cur, left, right, payload, rows, sems):
    def turned(c):
        pair = [chunk_with_halo(cur, left, right, c, v) for v in range(2)]
        return jnp.concatenate(pair, axis=0).T

    upper = lax.broadcasted_iota(jnp.int32, (8, 128), 0) < 4
    copies = []
    for k in range(PARTS):
        chosen = jnp.where(upper, turned(2 * k + 2)[:8], turned(2 * k - 1)[120:])
        rows[k, 0], rows[k, 1] = chosen[:4], chosen[4:]
        copies.append(
            pltpu.make_async_copy(rows.at[k], payload.at[k, pl.ds(ROWS + 2, 2)], sems.at[k])
        )
        copies[k].start()
    for copy in copies:
        copy.wait()


def with_beside(payload, cur, left, right):
    return pl.pallas_call(
        beside_kernel,
        out_shape=pltpu.HBM(payload.shape, f32),
        in_specs=[HBM, VMEM, VMEM, VMEM],
        out_specs=HBM,
        scratch_shapes=[pltpu.VMEM((PARTS, 2, 4, 128), f32), pltpu.SemaphoreType.DMA((PARTS,))],
        input_output_aliases={0: 0},
        compiler_params=params(8),
        cost_estimate=cost(1000),
        name="beside",
    )(payload, cur, left, right)


def take_lanes(chunk_of, chunks, index):
    at = jnp.broadcast_to(index, (8, 128))
    lane = at & 127
    chunk = at >> 7
    out = []
    for g in range(ROWS // 8):
        found = jnp.take_along_axis(chunk_of(g, 0), lane, axis=1)
        out.append(found)
    for c in range(1, chunks):
        here = chunk == c
        for g in range(ROWS // 8):
            out[g] = jnp.where(here, jnp.take_along_axis(chunk_of(g, c), lane, axis=1), out[g])
    return out


def heights_kernel(cur, depth, left, right, cells, own, hbuf, ubuf):
    lane = lax.broadcasted_iota(jnp.int32, (ROWS, 128), 1)
    first, last = lane == 0, lane == 127

    def old(c, v):
        return chunk_with_halo(cur, left, right, c, v)

    def scaled_depth(c):
        if c < 0:
            row = left[ROWS : ROWS + 1, :]
        elif c == CHUNKS:
            row = right[ROWS : ROWS + 1, :]
        else:
            row = depth[c : c + 1, :]
        return 0.9 * row

    def height_step(h_of, u_of):
        before = None
        for c in range(-1, CHUNKS + 1):
            u = u_of(c)
            turned = pltpu.roll(u, 1, 1)
            previous = turned if before is None else jnp.where(first, before, turned)
            before = turned
            hbuf[c + 1] = h_of(c) - scaled_depth(c) * (u - previous)

    height_step(lambda c: old(c, 0), lambda c: old(c, 1))
    turned = pltpu.roll(hbuf[0], 127, 1)
    for c in range(-1, CHUNKS + 1):
        after = pltpu.roll(hbuf[c + 2], 127, 1) if c < CHUNKS else turned
        following = jnp.where(last, after, turned)
        turned = after
        ubuf[c + 1] = old(c, 1) - 0.9 * (following - hbuf[c + 1])
    height_step(lambda c: hbuf[c + 1], lambda c: ubuf[c + 1])

    for j in range(OBS // 128):
        rows = take_lanes(lambda g, c: hbuf[c + 1, g * 8 : g * 8 + 8, :], CHUNKS, cells[j : j + 1, :])
        for g in range(ROWS // 8):
            own[g * 8 : g * 8 + 8, j * 128 : (j + 1) * 128] = rows[g]


def heights(cur, depth, left, right, cells):
    buffer = pltpu.VMEM((CHUNKS + 2, ROWS, 128), f32)
    return pl.pallas_call(
        heights_kernel,
        out_shape=jax.ShapeDtypeStruct((ROWS, OBS), f32),
        in_specs=[VMEM] * 5,
        out_specs=VMEM,
        scratch_shapes=[buffer, buffer],
        compiler_params=params(12),
        cost_estimate=cost(10**12),
        name="heights",
    )(cur, depth, left, right, cells)


def forecast_kernel(received, depth, left, right, state, beside, depths):
    part = lax.axis_index("grp") * lax.axis_size("mem") + lax.axis_index("mem")
    depths[0:1, :] = left[ROWS : ROWS + 1, :]
    depths[1 : CHUNKS + 1, :] = depth[...]
    depths[CHUNKS + 1 : CHUNKS + 2, :] = right[ROWS : ROWS + 1, :]
    scaled = [0.9 * depths[pl.ds(2 * part + i, 1), :] for i in range(4)]
    lane = lax.broadcasted_iota(jnp.int32, (ROWS, 128), 1)
    first, last = lane == 0, lane == 127
    beside[...] = jnp.zeros((128, 128), f32)

    def height_step(h, u, low):
        turned = [pltpu.roll(x, 1, 1) for x in u]
        out = list(h)
        for i in range(low, 4):
            previous = turned[i] if i == 0 else jnp.where(first, turned[i - 1], turned[i])
            out[i] = h[i] - scaled[i] * (u[i] - previous)
        return out

    def speed_step(h, u, low, high):
        turned = [pltpu.roll(x, 127, 1) for x in h]
        out = list(u)
        for i in range(low, high):
            following = turned[i] if i == 3 else jnp.where(last, turned[i + 1], turned[i])
            out[i] = u[i] - 0.9 * (following - h[i])
        return out

    for b in range(PARTS):
        edge = received[b, 4 * ROWS + 8 : 4 * ROWS + 16, :]
        beside[0:8, :] = edge
        beside[120:128, :] = edge
        turned = beside[...].T
        own = [received[b, pl.ds(j, ROWS, stride=4), :] for j in range(4)]
        h = [turned[:ROWS], own[0], own[2], turned[:ROWS]]
        u = [turned[ROWS:], own[1], own[3], turned[ROWS:]]
        h = height_step(h, u, 0)
        u = speed_step(h, u, 0, 4)
        h = height_step(h, u, 1)
        u = speed_step(h, u, 1, 3)
        for i, x in enumerate((h[1], h[2], u[1], u[2])):
            state[b * ROWS : (b + 1) * ROWS, i * 128 : (i + 1) * 128] = x


def forecast(received, depth, left, right):
    return pl.pallas_call(
        forecast_kernel,
        out_shape=jax.ShapeDtypeStruct((MEMBERS, STATE), f32),
        in_specs=[VMEM] * 4,
        out_specs=VMEM,
        scratch_shapes=[pltpu.VMEM((128, 128), f32), pltpu.VMEM((24, 128), f32)],
        compiler_params=params(8),
        cost_estimate=cost(10**10),
        name="forecast",
    )(received, depth, left, right)


def pick_kernel(
    received, below, own, above, out, source, held, floats, lists, bounds, sems, list_sems
):
    arrivals = [
        pltpu.make_async_copy(
            received.at[k, pl.ds(4 * ROWS, 8), :], floats.at[k], list_sems.at[k]
        )
        for k in range(PARTS)
    ]
    for arrival in arrivals:
        arrival.start()
    for arrival in arrivals:
        arrival.wait()
    lists[...] = floats[...].astype(jnp.int32)
    to_scalars = pltpu.make_async_copy(lists, bounds, list_sems.at[PARTS])
    to_scalars.start()
    for n, part in enumerate((below, own, above)):
        for c in range(8):
            source[n * 8 + c] = part[:, c * 128 : (c + 1) * 128]
    to_scalars.wait()

    def send(k):
        return pltpu.make_async_copy(held.at[k], out.at[k], sems.at[k])

    def take(c, g, lane):
        return jnp.take_along_axis(source[c, g * 8 : g * 8 + 8, :], lane, axis=1)

    def one_list(k, carry):
        blocks = []
        for j in range(8):
            at = jnp.broadcast_to(lists[k, j : j + 1, :], (8, 128))
            lane, chunk = at & 127, at >> 7
            low, high = bounds[k, j, 0] >> 7, bounds[k, j, 127] >> 7
            blocks.append((j, lane, chunk, low, high))
            found = [take(low, g, lane) for g in range(ROWS // 8)]
            for d in range(1, DIRECT):
                here = chunk == low + d
                found = [jnp.where(here, take(low + d, g, lane), f) for g, f in enumerate(found)]
            for g in range(ROWS // 8):
                held[k, g * 8 : g * 8 + 8, j * 128 : (j + 1) * 128] = found[g]
        for j, lane, chunk, low, high in blocks:

            def more(c, carry):
                here = chunk == c
                for g in range(ROWS // 8):
                    at = (k, slice(g * 8, g * 8 + 8), slice(j * 128, (j + 1) * 128))
                    held[at] = jnp.where(here, take(c, g, lane), held[at])
                return carry

            lax.fori_loop(low + DIRECT, high + 1, more, 0)
        send(k).start()
        return carry

    lax.fori_loop(0, PARTS, one_list, 0)
    for k in range(PARTS):
        send(k).wait()


def pick(received, below, own, above):
    return pl.pallas_call(
        pick_kernel,
        out_shape=pltpu.HBM((PARTS, ROWS, SLOTS), f32),
        in_specs=[pl.BlockSpec(memory_space=pl.ANY)] + [VMEM] * 3,
        out_specs=HBM,
        scratch_shapes=[
            pltpu.VMEM((24 + DIRECT, ROWS, 128), f32),
            pltpu.VMEM((PARTS, ROWS, SLOTS), f32),
            pltpu.VMEM((PARTS, 8, 128), f32),
            pltpu.VMEM((PARTS, 8, 128), jnp.int32),
            pltpu.SMEM((PARTS, 8, 128), jnp.int32),
            pltpu.SemaphoreType.DMA((PARTS,)),
            pltpu.SemaphoreType.DMA((PARTS + 1,)),
        ],
        compiler_params=params(16),
        cost_estimate=cost(10**12),
        name="pick",
    )(received, below, own, above)


def slots_kernel(rel, values, errors, cells, out):
    tile = lax.axis_index("tile")
    part = lax.axis_index("grp") * lax.axis_size("mem") + lax.axis_index("mem")
    center = tile * CELLS + part * CELLS_TILE + CELLS_TILE // 2
    listed = rel[...]
    at = jnp.maximum(listed, 0)
    lane = at & 127
    chunk = at >> 7
    value = jnp.zeros((8, 128), f32)
    error = jnp.ones((8, 128), f32)
    cell = jnp.zeros((8, 128), jnp.int32)
    for n in range(3):
        t = lax.rem(tile + (TILES - 1 + n), TILES)
        for j in range(8):
            here = chunk == n * 8 + j

            def found(ref):
                row = jnp.broadcast_to(ref[t, j : j + 1, :], (8, 128))
                return jnp.take_along_axis(row, lane, axis=1)

            value = jnp.where(here, found(values), value)
            error = jnp.where(here, found(errors), error)
            cell = jnp.where(here, found(cells), cell)
    distance = jnp.abs(cell - center)
    distance = jnp.minimum(distance, NCELLS - distance).astype(f32)
    weight = jnp.exp(-0.5 * (distance / LOC) ** 2) / (error * error)
    weight = jnp.where(listed >= 0, weight, 0.0)
    for j in range(8):
        out[0:1, j * 128 : (j + 1) * 128] = weight[j : j + 1, :]
        out[1:2, j * 128 : (j + 1) * 128] = value[j : j + 1, :]


def slots(rel, values, errors, cells):
    return pl.pallas_call(
        slots_kernel,
        out_shape=jax.ShapeDtypeStruct((8, SLOTS), f32),
        in_specs=[VMEM] * 4,
        out_specs=VMEM,
        compiler_params=params(8),
        name="slots",
    )(rel, values, errors, cells)


def analyse_kernel(predicted, slot_rows, state, gain_hi, gain_lo, analysis, held, result, sems):
    y = predicted[...]
    weight = slot_rows[0:1, :]
    mean = jnp.sum(y, axis=0, keepdims=True) * (1.0 / MEMBERS)
    root_weight = jnp.sqrt(weight)
    spread = (y - mean) * root_weight
    departure = (slot_rows[1:2, :] - mean) * root_weight
    sh, sl = halves(spread)
    dh, dl = halves(jnp.broadcast_to(departure, (16, SLOTS)))
    rows_i = lax.broadcasted_iota(jnp.int32, (MEMBERS, MEMBERS), 0)
    cols_i = lax.broadcasted_iota(jnp.int32, (MEMBERS, MEMBERS), 1)
    eye = jnp.where(rows_i == cols_i, 1.0, 0.0)
    a = dot_nt(sh, sh) + (dot_nt(sh, sl) + dot_nt(sl, sh)) + (MEMBERS - 1.0) * eye
    innovation = (dot_nt(dh, sh) + (dot_nt(dh, sl) + dot_nt(dl, sh)))[0:1, :]
    bound = jnp.max(jnp.sum(jnp.abs(a), axis=0, keepdims=True), axis=1, keepdims=True)
    approx = a / bound

    def two_steps(m):
        mp = halves(m)
        m2 = product(mp, mp)
        q = 1.6875 * eye - 0.5625 * m + 0.0625 * m2
        return 2.25 * eye - 2.4375 * m + product(halves(m2), halves(q))

    r = halves(two_steps(approx))
    z = r
    w = halves(product(halves(approx), r))
    r = halves(two_steps(product(z, w)))
    z, w = halves(product(r, z)), halves(product(w, r))
    r = halves(two_steps(product(z, w)))
    root = product(r, z) * lax.rsqrt(bound)
    once = jnp.sum(root * innovation, axis=1, keepdims=True)
    mean_weight = jnp.sum(root * once, axis=0, keepdims=True)
    moved = math.sqrt(MEMBERS - 1) * root + mean_weight
    gain = moved + (1.0 - jnp.sum(moved, axis=1, keepdims=True)) * (1.0 / MEMBERS)
    gain = halves(gain)
    held[0], held[1] = gain
    copies = [
        pltpu.make_async_copy(held.at[0], gain_hi, sems.at[0]),
        pltpu.make_async_copy(held.at[1], gain_lo, sems.at[1]),
        pltpu.make_async_copy(result, analysis, sems.at[2]),
    ]
    copies[0].start()
    copies[1].start()
    analysed = product(gain, halves(state[...]))
    for row in range(4):
        at = (row % 2) * CELLS_TILE + (row // 2) * 128
        result[pl.ds(row, MEMBERS, stride=4), :] = analysed[:, at : at + 128]
    copies[2].start()
    for copy in copies:
        copy.wait()


def analyse(predicted, slot_rows, state):
    return pl.pallas_call(
        analyse_kernel,
        out_shape=(
            pltpu.HBM((MEMBERS, MEMBERS), bf16),
            pltpu.HBM((MEMBERS, MEMBERS), bf16),
            pltpu.HBM((MEMBERS * 4, 128), f32),
        ),
        in_specs=[VMEM, VMEM, VMEM],
        out_specs=(HBM, HBM, HBM),
        scratch_shapes=[
            pltpu.VMEM((2, MEMBERS, MEMBERS), bf16),
            pltpu.VMEM((MEMBERS * 4, 128), f32),
            pltpu.SemaphoreType.DMA((3,)),
        ],
        compiler_params=params(32),
        name="analyse",
    )(predicted, slot_rows, state)


def smooth_kernel(gain_hi, gain_lo, state, out):
    out[0] = product((gain_hi[...], gain_lo[...]), halves(state[0]))


def smooth(gain_hi, gain_lo, states):
    whole = pl.BlockSpec((MEMBERS, MEMBERS), lambda i: (0, 0))
    one = pl.BlockSpec((1, MEMBERS, STATE), lambda i: (i, 0, 0))
    return pl.pallas_call(
        smooth_kernel,
        out_shape=jax.ShapeDtypeStruct((LAGS, MEMBERS, STATE), f32),
        grid=(LAGS,),
        in_specs=[whole, whole, one],
        out_specs=one,
        compiler_params=params(24),
        cost_estimate=pl.CostEstimate(
            flops=2 * 3 * LAGS * MEMBERS**2 * STATE, bytes_accessed=8 * LAGS * MEMBERS * STATE, transcendentals=0
        ),
        name="smooth",
    )(gain_hi, gain_lo, states)


def assemble_kernel(parts, out, sems):
    copies = [pltpu.make_async_copy(parts.at[k], out.at[:, k], sems.at[k]) for k in range(PARTS)]
    for copy in copies:
        copy.start()
    for copy in copies:
        copy.wait()


def assemble(parts):
    return pl.pallas_call(
        assemble_kernel,
        out_shape=pltpu.HBM((ROWS, PARTS, 4, 128), f32),
        in_specs=[pl.BlockSpec(memory_space=pl.ANY)],
        out_specs=HBM,
        scratch_shapes=[pltpu.SemaphoreType.DMA((PARTS,))],
        compiler_params=params(8),
        name="assemble",
    )(parts)


def along_tiles(x, by):
    return lax.ppermute(x, "tile", [(i, (i + by) % TILES) for i in range(TILES)])


def far(x):
    return pltpu.with_memory_space_constraint(x, pltpu.HBM)


def exchange(x):
    return lax.all_to_all(x, GROUP, split_axis=0, concat_axis=0, tiled=True)


def per_device(
    current_state, lagged_states, water_depth, obs_cells, obs_values, obs_errors, tile_obs
):
    cur = current_state.reshape(ROWS, 2, CHUNKS, 128).transpose(0, 2, 1, 3)
    depth = water_depth.reshape(CHUNKS, 128)
    to_right, to_left = edges(far(cur.reshape(ROWS, 2 * CHUNKS, 128)), far(depth))
    left = along_tiles(to_right, 1)
    right = along_tiles(to_left, -1)
    to_left, listed = lax.optimization_barrier((to_left, tile_obs[0, 0].reshape(8, 128)))
    ordered, payload, cur, depth, cells = order(
        far(listed),
        far(cur.reshape(ROWS, PARTS, 4, 128)),
        far(cur.reshape(ROWS * 2 * CHUNKS, 128)),
        far(depth),
        far(obs_cells.reshape(TILES, 8, 128)),
    )
    payload = with_beside(payload, cur, left, right)
    received = exchange(payload.reshape(PARTS, ROWS * 4 + 16, 128))
    own = heights(cur, depth, left, right, cells)
    below = along_tiles(own, 1)
    above = along_tiles(own, -1)
    picked = pick(received, below, own, above)
    predicted = exchange(picked).reshape(MEMBERS, SLOTS)
    state = forecast(received, depth, left, right)
    slot_rows = slots(
        ordered,
        obs_values.reshape(TILES, 8, 128),
        obs_errors.reshape(TILES, 8, 128),
        obs_cells.reshape(TILES, 8, 128),
    )
    gain_hi, gain_lo, analysis = analyse(predicted, slot_rows, state)
    returned = exchange(analysis.reshape(PARTS, ROWS * 4, 128))
    older = smooth(gain_hi, gain_lo, lagged_states.reshape(LAGS, MEMBERS, STATE))
    analysed = assemble(returned.reshape(PARTS, ROWS, 4, 128))
    analysed = analysed.reshape(ROWS, CHUNKS, 2, 128).transpose(0, 2, 1, 3)
    return (
        analysed.reshape(ROWS, 2, CELLS),
        older.reshape(LAGS, 1, 1, MEMBERS, STATE),
    )


def solution(mesh):
    placed = (
        P(GROUP, None, "tile"),
        P(None, "tile", GROUP, None, None),
        P("tile"),
        P(),
        P(),
        P(),
        P("tile", GROUP, None),
    )
    return jax.shard_map(
        per_device,
        mesh=mesh,
        in_specs=placed,
        out_specs=(P(GROUP, None, "tile"), P(None, "tile", GROUP, None, None)),
        check_vma=False,
    )
```

```python
import functools
import math

import jax
import jax.numpy as jnp
from jax import lax
from jax.experimental import pallas as pl
from jax.experimental.pallas import tpu as pltpu
from jax.sharding import PartitionSpec as P

GROUP = ("grp", "mem")
PARTS = 8
ROWS = 64
MEMBERS = 512
CELLS = 2048
CHUNKS = 16
CELLS_TILE = 256
STATE = 512
OBS = 1024
SLOTS = 1024
NOBS = 32768
NCELLS = 65536
TILES = 32
LOC = 512
LAGS = 3
DIRECT = 3
f32 = jnp.float32
bf16 = jnp.bfloat16
VMEM = pl.BlockSpec(memory_space=pltpu.VMEM)
HBM = pl.BlockSpec(memory_space=pltpu.HBM)
SMEM = pl.BlockSpec(memory_space=pltpu.SMEM)


def params(mib):
    return pltpu.CompilerParams(vmem_limit_bytes=mib * 1024 * 1024)


def cost(flops):
    return pl.CostEstimate(flops=flops, bytes_accessed=2**20, transcendentals=0)


def halves(x):
    hi = x.astype(bf16)
    return hi, (x - hi.astype(f32)).astype(bf16)


def dot(a, b):
    return jnp.dot(a, b, preferred_element_type=f32)


def dot_nt(a, b):
    return lax.dot_general(a, b, (((1,), (1,)), ((), ())), preferred_element_type=f32)


def product(a, b):
    (ah, al), (bh, bl) = a, b
    return dot(ah, bh) + (dot(ah, bl) + dot(al, bh))


def edges_kernel(cur, far_depth, to_right, to_left, ends, depth, sems):
    copies = [
        pltpu.make_async_copy(cur.at[:, pl.ds(at, 8), :], ends.at[n], sems.at[n])
        for n, at in enumerate((0, 2 * CHUNKS - 8))
    ]
    copies.append(pltpu.make_async_copy(far_depth, depth, sems.at[2]))
    for copy in copies:
        copy.start()
    low_half = lax.broadcasted_iota(jnp.int32, (ROWS, 128), 1) < ROWS
    end = CHUNKS - 1
    copies[2].wait()
    to_right[ROWS:, :] = jnp.broadcast_to(depth[end : end + 1, :], (8, 128))
    to_left[ROWS:, :] = jnp.broadcast_to(depth[0:1, :], (8, 128))
    copies[1].wait()
    h, u = ends[1, :, 6, :], ends[1, :, 7, :]
    to_right[:ROWS, :] = jnp.where(low_half, pltpu.roll(h, ROWS, 1), u)
    copies[0].wait()
    h, u = ends[0, :, 0, :], ends[0, :, 1, :]
    to_left[:ROWS, :] = jnp.where(low_half, h, pltpu.roll(u, ROWS, 1))


def edges(cur, depth):
    message = jax.ShapeDtypeStruct((ROWS + 8, 128), f32)
    return pl.pallas_call(
        edges_kernel,
        out_shape=(message, message),
        in_specs=[HBM, HBM],
        out_specs=(VMEM, VMEM),
        scratch_shapes=[
            pltpu.VMEM((2, ROWS, 8, 128), f32),
            pltpu.VMEM((CHUNKS, 128), f32),
            pltpu.SemaphoreType.DMA((3,)),
        ],
        compiler_params=params(8),
        name="edges",
    )(cur, depth)


def order_kernel(
    far_list, far_parts, far_cur, far_depth, far_cells,
    ordered, payload, cur, depth, cells, tile_list, row_list, row_place, filled, by_part, sems, sent,
):
    tile = lax.axis_index("tile")
    arrivals = [
        pltpu.make_async_copy(source, target, sems.at[n])
        for n, (source, target) in enumerate(
            (
                (far_list, tile_list),
                (far_parts, by_part),
                (far_cells.at[tile], cells),
                (far_depth, depth),
                (far_cur, cur),
            )
        )
    ]
    raw = [
        pltpu.make_async_copy(by_part.at[:, k], payload.at[k, pl.ds(0, ROWS)], sent.at[k])
        for k in range(PARTS)
    ]
    for arrival in arrivals:
        arrival.start()
    arrivals[0].wait()
    arrivals[1].wait()
    for copy in raw:
        copy.start()
    listed = tile_list[...]
    rel = jnp.where(listed >= 0, (listed - (tile - 1) * OBS) & (NOBS - 1), -1)
    count = jnp.sum(jnp.where(rel >= 0, 1.0, 0.0))
    top = jnp.max(rel)
    for j in range(8):
        row_list[0:1, j * 128 : (j + 1) * 128] = rel[j : j + 1, :]
    row = row_list[0:1, :]
    chunks = 3 * OBS // 128

    def iota(shape, dim):
        return lax.broadcasted_iota(jnp.int32, shape, dim)

    def flags(x):
        return jnp.where(x, 1.0, 0.0).astype(bf16)

    in_chunk = flags((row >> 7) == iota((32, SLOTS), 0))
    in_lane = flags((row & 127) == iota((128, SLOTS), 0))
    present = dot_nt(in_chunk, in_lane).astype(bf16)
    before = dot(present, flags(iota((128, 128), 0) < iota((128, 128), 1)))
    totals = dot(present, jnp.ones((128, 128), bf16)).astype(bf16)
    place = before + dot(flags(iota((32, 32), 1) < iota((32, 32), 0)), totals)
    place = jnp.where(present.astype(f32) > 0.5, place, -1.0).astype(jnp.int32)
    for c in range(chunks):
        row_place[0:1, c * 128 : (c + 1) * 128] = place[c : c + 1, :]
    row = row_place[0:1, :]
    wide = 3 * OBS
    to_row = (row >> 7) == iota((8, wide), 0)
    number = iota((8, wide), 1)
    parts = jnp.concatenate(
        [jnp.where(to_row, number >> 7, 0), jnp.where(to_row, number & 127, 0)], axis=0
    )
    found = dot_nt(parts.astype(f32).astype(bf16), flags((row & 127) == iota((128, wide), 0)))
    found = (found[:8] * 128.0 + found[8:]).astype(jnp.int32)
    used = (iota((8, 128), 0) * 128 + iota((8, 128), 1)).astype(f32) < count
    ordered[...] = jnp.where(used, found, -1)
    whole = jnp.where(used, found, jnp.maximum(top, 0)).astype(f32)
    filled[0], filled[1] = whole[:4], whole[4:]
    lists = [
        pltpu.make_async_copy(filled, payload.at[k, pl.ds(ROWS, 2)], sent.at[PARTS + k])
        for k in range(PARTS)
    ]
    for copy in lists:
        copy.start()
    for copy in arrivals[2:] + raw + lists:
        copy.wait()
    cells[...] = cells[...] - tile * CELLS


def order(tile_list, parts, cur, depth, cells):
    return pl.pallas_call(
        order_kernel,
        out_shape=(
            jax.ShapeDtypeStruct((8, 128), jnp.int32),
            pltpu.HBM((PARTS, ROWS + 4, 4, 128), f32),
            jax.ShapeDtypeStruct((ROWS * 2 * CHUNKS, 128), f32),
            jax.ShapeDtypeStruct((CHUNKS, 128), f32),
            jax.ShapeDtypeStruct((8, 128), jnp.int32),
        ),
        in_specs=[HBM] * 5,
        out_specs=(VMEM, HBM, VMEM, VMEM, VMEM),
        scratch_shapes=[
            pltpu.VMEM((8, 128), jnp.int32),
            pltpu.VMEM((8, SLOTS), jnp.int32),
            pltpu.VMEM((8, 3 * OBS), jnp.int32),
            pltpu.VMEM((2, 4, 128), f32),
            pltpu.VMEM((ROWS, PARTS, 4, 128), f32),
            pltpu.SemaphoreType.DMA((5,)),
            pltpu.SemaphoreType.DMA((2 * PARTS,)),
        ],
        cost_estimate=pl.CostEstimate(flops=0, bytes_accessed=100 * 2**20, transcendentals=0),
        compiler_params=params(12),
        name="order",
    )(tile_list, parts, cur, depth, cells)


def chunk_with_halo(cur, left, right, c, v):
    if c < 0:
        x = left[:ROWS, :]
        return x if v else pltpu.roll(x, ROWS, 1)
    if c == CHUNKS:
        x = right[:ROWS, :]
        return pltpu.roll(x, ROWS, 1) if v else x
    return cur[pl.ds(2 * c + v, ROWS, stride=2 * CHUNKS), :]


def beside_kernel(_, cur, left, right, payload, rows, sems):
    def turned(c):
        pair = [chunk_with_halo(cur, left, right, c, v) for v in range(2)]
        return jnp.concatenate(pair, axis=0).T

    upper = lax.broadcasted_iota(jnp.int32, (8, 128), 0) < 4
    copies = []
    for k in range(PARTS):
        chosen = jnp.where(upper, turned(2 * k + 2)[:8], turned(2 * k - 1)[120:])
        rows[k, 0], rows[k, 1] = chosen[:4], chosen[4:]
        copies.append(
            pltpu.make_async_copy(rows.at[k], payload.at[k, pl.ds(ROWS + 2, 2)], sems.at[k])
        )
        copies[k].start()
    for copy in copies:
        copy.wait()


def with_beside(payload, cur, left, right):
    return pl.pallas_call(
        beside_kernel,
        out_shape=pltpu.HBM(payload.shape, f32),
        in_specs=[HBM, VMEM, VMEM, VMEM],
        out_specs=HBM,
        scratch_shapes=[pltpu.VMEM((PARTS, 2, 4, 128), f32), pltpu.SemaphoreType.DMA((PARTS,))],
        input_output_aliases={0: 0},
        compiler_params=params(8),
        cost_estimate=cost(1000),
        name="beside",
    )(payload, cur, left, right)


def take_lanes(chunk_of, chunks, index):
    at = jnp.broadcast_to(index, (8, 128))
    lane = at & 127
    chunk = at >> 7
    out = []
    for g in range(ROWS // 8):
        found = jnp.take_along_axis(chunk_of(g, 0), lane, axis=1)
        out.append(found)
    for c in range(1, chunks):
        here = chunk == c
        for g in range(ROWS // 8):
            out[g] = jnp.where(here, jnp.take_along_axis(chunk_of(g, c), lane, axis=1), out[g])
    return out


def heights_kernel(cur, depth, left, right, cells, own, hbuf, ubuf):
    lane = lax.broadcasted_iota(jnp.int32, (ROWS, 128), 1)
    first, last = lane == 0, lane == 127

    def old(c, v):
        return chunk_with_halo(cur, left, right, c, v)

    def scaled_depth(c):
        if c < 0:
            row = left[ROWS : ROWS + 1, :]
        elif c == CHUNKS:
            row = right[ROWS : ROWS + 1, :]
        else:
            row = depth[c : c + 1, :]
        return 0.9 * row

    def height_step(h_of, u_of):
        before = None
        for c in range(-1, CHUNKS + 1):
            u = u_of(c)
            turned = pltpu.roll(u, 1, 1)
            previous = turned if before is None else jnp.where(first, before, turned)
            before = turned
            hbuf[c + 1] = h_of(c) - scaled_depth(c) * (u - previous)

    height_step(lambda c: old(c, 0), lambda c: old(c, 1))
    turned = pltpu.roll(hbuf[0], 127, 1)
    for c in range(-1, CHUNKS + 1):
        after = pltpu.roll(hbuf[c + 2], 127, 1) if c < CHUNKS else turned
        following = jnp.where(last, after, turned)
        turned = after
        ubuf[c + 1] = old(c, 1) - 0.9 * (following - hbuf[c + 1])
    height_step(lambda c: hbuf[c + 1], lambda c: ubuf[c + 1])

    for j in range(OBS // 128):
        rows = take_lanes(lambda g, c: hbuf[c + 1, g * 8 : g * 8 + 8, :], CHUNKS, cells[j : j + 1, :])
        for g in range(ROWS // 8):
            own[g * 8 : g * 8 + 8, j * 128 : (j + 1) * 128] = rows[g]


def heights(cur, depth, left, right, cells):
    buffer = pltpu.VMEM((CHUNKS + 2, ROWS, 128), f32)
    return pl.pallas_call(
        heights_kernel,
        out_shape=jax.ShapeDtypeStruct((ROWS, OBS), f32),
        in_specs=[VMEM] * 5,
        out_specs=VMEM,
        scratch_shapes=[buffer, buffer],
        compiler_params=params(12),
        cost_estimate=cost(10**12),
        name="heights",
    )(cur, depth, left, right, cells)


def forecast_kernel(received, depth, left, right, state, beside, depths):
    part = lax.axis_index("grp") * lax.axis_size("mem") + lax.axis_index("mem")
    depths[0:1, :] = left[ROWS : ROWS + 1, :]
    depths[1 : CHUNKS + 1, :] = depth[...]
    depths[CHUNKS + 1 : CHUNKS + 2, :] = right[ROWS : ROWS + 1, :]
    scaled = [0.9 * depths[pl.ds(2 * part + i, 1), :] for i in range(4)]
    lane = lax.broadcasted_iota(jnp.int32, (ROWS, 128), 1)
    first, last = lane == 0, lane == 127
    beside[...] = jnp.zeros((128, 128), f32)

    def height_step(h, u, low):
        turned = [pltpu.roll(x, 1, 1) for x in u]
        out = list(h)
        for i in range(low, 4):
            previous = turned[i] if i == 0 else jnp.where(first, turned[i - 1], turned[i])
            out[i] = h[i] - scaled[i] * (u[i] - previous)
        return out

    def speed_step(h, u, low, high):
        turned = [pltpu.roll(x, 127, 1) for x in h]
        out = list(u)
        for i in range(low, high):
            following = turned[i] if i == 3 else jnp.where(last, turned[i + 1], turned[i])
            out[i] = u[i] - 0.9 * (following - h[i])
        return out

    for b in range(PARTS):
        edge = received[b, 4 * ROWS + 8 : 4 * ROWS + 16, :]
        beside[0:8, :] = edge
        beside[120:128, :] = edge
        turned = beside[...].T
        own = [received[b, pl.ds(j, ROWS, stride=4), :] for j in range(4)]
        h = [turned[:ROWS], own[0], own[2], turned[:ROWS]]
        u = [turned[ROWS:], own[1], own[3], turned[ROWS:]]
        h = height_step(h, u, 0)
        u = speed_step(h, u, 0, 4)
        h = height_step(h, u, 1)
        u = speed_step(h, u, 1, 3)
        for i, x in enumerate((h[1], h[2], u[1], u[2])):
            state[b * ROWS : (b + 1) * ROWS, i * 128 : (i + 1) * 128] = x


def forecast(received, depth, left, right):
    return pl.pallas_call(
        forecast_kernel,
        out_shape=jax.ShapeDtypeStruct((MEMBERS, STATE), f32),
        in_specs=[VMEM] * 4,
        out_specs=VMEM,
        scratch_shapes=[pltpu.VMEM((128, 128), f32), pltpu.VMEM((24, 128), f32)],
        compiler_params=params(8),
        cost_estimate=cost(10**10),
        name="forecast",
    )(received, depth, left, right)


def pick_kernel(
    received, below, own, above, out, source, held, floats, lists, bounds, sems, list_sems
):
    arrivals = [
        pltpu.make_async_copy(
            received.at[k, pl.ds(4 * ROWS, 8), :], floats.at[k], list_sems.at[k]
        )
        for k in range(PARTS)
    ]
    for arrival in arrivals:
        arrival.start()
    for arrival in arrivals:
        arrival.wait()
    lists[...] = floats[...].astype(jnp.int32)
    to_scalars = pltpu.make_async_copy(lists, bounds, list_sems.at[PARTS])
    to_scalars.start()
    for n, part in enumerate((below, own, above)):
        for c in range(8):
            source[n * 8 + c] = part[:, c * 128 : (c + 1) * 128]
    to_scalars.wait()

    def send(k):
        return pltpu.make_async_copy(held.at[k], out.at[k], sems.at[k])

    def take(c, g, lane):
        return jnp.take_along_axis(source[c, g * 8 : g * 8 + 8, :], lane, axis=1)

    def one_list(k, carry):
        blocks = []
        for j in range(8):
            at = jnp.broadcast_to(lists[k, j : j + 1, :], (8, 128))
            lane, chunk = at & 127, at >> 7
            low, high = bounds[k, j, 0] >> 7, bounds[k, j, 127] >> 7
            blocks.append((j, lane, chunk, low, high))
            found = [take(low, g, lane) for g in range(ROWS // 8)]
            for d in range(1, DIRECT):
                here = chunk == low + d
                found = [jnp.where(here, take(low + d, g, lane), f) for g, f in enumerate(found)]
            for g in range(ROWS // 8):
                held[k, g * 8 : g * 8 + 8, j * 128 : (j + 1) * 128] = found[g]
        for j, lane, chunk, low, high in blocks:

            def more(c, carry):
                here = chunk == c
                for g in range(ROWS // 8):
                    at = (k, slice(g * 8, g * 8 + 8), slice(j * 128, (j + 1) * 128))
                    held[at] = jnp.where(here, take(c, g, lane), held[at])
                return carry

            lax.fori_loop(low + DIRECT, high + 1, more, 0)
        send(k).start()
        return carry

    lax.fori_loop(0, PARTS, one_list, 0)
    for k in range(PARTS):
        send(k).wait()


def pick(received, below, own, above):
    return pl.pallas_call(
        pick_kernel,
        out_shape=pltpu.HBM((PARTS, ROWS, SLOTS), f32),
        in_specs=[pl.BlockSpec(memory_space=pl.ANY)] + [VMEM] * 3,
        out_specs=HBM,
        scratch_shapes=[
            pltpu.VMEM((24 + DIRECT, ROWS, 128), f32),
            pltpu.VMEM((PARTS, ROWS, SLOTS), f32),
            pltpu.VMEM((PARTS, 8, 128), f32),
            pltpu.VMEM((PARTS, 8, 128), jnp.int32),
            pltpu.SMEM((PARTS, 8, 128), jnp.int32),
            pltpu.SemaphoreType.DMA((PARTS,)),
            pltpu.SemaphoreType.DMA((PARTS + 1,)),
        ],
        compiler_params=params(16),
        cost_estimate=cost(10**12),
        name="pick",
    )(received, below, own, above)


def slots_kernel(rel, values, errors, cells, out):
    tile = lax.axis_index("tile")
    part = lax.axis_index("grp") * lax.axis_size("mem") + lax.axis_index("mem")
    center = tile * CELLS + part * CELLS_TILE + CELLS_TILE // 2
    listed = rel[...]
    at = jnp.maximum(listed, 0)
    lane = at & 127
    chunk = at >> 7
    value = jnp.zeros((8, 128), f32)
    error = jnp.ones((8, 128), f32)
    cell = jnp.zeros((8, 128), jnp.int32)
    for n in range(3):
        t = lax.rem(tile + (TILES - 1 + n), TILES)
        for j in range(8):
            here = chunk == n * 8 + j

            def found(ref):
                row = jnp.broadcast_to(ref[t, j : j + 1, :], (8, 128))
                return jnp.take_along_axis(row, lane, axis=1)

            value = jnp.where(here, found(values), value)
            error = jnp.where(here, found(errors), error)
            cell = jnp.where(here, found(cells), cell)
    distance = jnp.abs(cell - center)
    distance = jnp.minimum(distance, NCELLS - distance).astype(f32)
    weight = jnp.exp(-0.5 * (distance / LOC) ** 2) / (error * error)
    weight = jnp.where(listed >= 0, weight, 0.0)
    for j in range(8):
        out[0:1, j * 128 : (j + 1) * 128] = weight[j : j + 1, :]
        out[1:2, j * 128 : (j + 1) * 128] = value[j : j + 1, :]


def slots(rel, values, errors, cells):
    return pl.pallas_call(
        slots_kernel,
        out_shape=jax.ShapeDtypeStruct((8, SLOTS), f32),
        in_specs=[VMEM] * 4,
        out_specs=VMEM,
        compiler_params=params(8),
        name="slots",
    )(rel, values, errors, cells)


def analyse_kernel(predicted, slot_rows, state, gain_hi, gain_lo, analysis, held, result, sems):
    y = predicted[...]
    weight = slot_rows[0:1, :]
    mean = jnp.sum(y, axis=0, keepdims=True) * (1.0 / MEMBERS)
    root_weight = jnp.sqrt(weight)
    spread = (y - mean) * root_weight
    departure = (slot_rows[1:2, :] - mean) * root_weight
    sh, sl = halves(spread)
    dh, dl = halves(jnp.broadcast_to(departure, (16, SLOTS)))
    rows_i = lax.broadcasted_iota(jnp.int32, (MEMBERS, MEMBERS), 0)
    cols_i = lax.broadcasted_iota(jnp.int32, (MEMBERS, MEMBERS), 1)
    eye = jnp.where(rows_i == cols_i, 1.0, 0.0)
    a = dot_nt(sh, sh) + (dot_nt(sh, sl) + dot_nt(sl, sh)) + (MEMBERS - 1.0) * eye
    innovation = (dot_nt(dh, sh) + (dot_nt(dh, sl) + dot_nt(dl, sh)))[0:1, :]
    bound = jnp.max(jnp.sum(jnp.abs(a), axis=0, keepdims=True), axis=1, keepdims=True)
    approx = a / bound

    def two_steps(m):
        mp = halves(m)
        m2 = product(mp, mp)
        q = 1.6875 * eye - 0.5625 * m + 0.0625 * m2
        return 2.25 * eye - 2.4375 * m + product(halves(m2), halves(q))

    r = halves(two_steps(approx))
    z = r
    w = halves(product(halves(approx), r))
    r = halves(two_steps(product(z, w)))
    z, w = halves(product(r, z)), halves(product(w, r))
    r = halves(two_steps(product(z, w)))
    root = product(r, z) * lax.rsqrt(bound)
    once = jnp.sum(root * innovation, axis=1, keepdims=True)
    mean_weight = jnp.sum(root * once, axis=0, keepdims=True)
    moved = math.sqrt(MEMBERS - 1) * root + mean_weight
    gain = moved + (1.0 - jnp.sum(moved, axis=1, keepdims=True)) * (1.0 / MEMBERS)
    gain = halves(gain)
    held[0], held[1] = gain
    copies = [
        pltpu.make_async_copy(held.at[0], gain_hi, sems.at[0]),
        pltpu.make_async_copy(held.at[1], gain_lo, sems.at[1]),
        pltpu.make_async_copy(result, analysis, sems.at[2]),
    ]
    copies[0].start()
    copies[1].start()
    analysed = product(gain, halves(state[...]))
    for row in range(4):
        at = (row % 2) * CELLS_TILE + (row // 2) * 128
        result[pl.ds(row, MEMBERS, stride=4), :] = analysed[:, at : at + 128]
    copies[2].start()
    for copy in copies:
        copy.wait()


def analyse(predicted, slot_rows, state):
    return pl.pallas_call(
        analyse_kernel,
        out_shape=(
            pltpu.HBM((MEMBERS, MEMBERS), bf16),
            pltpu.HBM((MEMBERS, MEMBERS), bf16),
            pltpu.HBM((MEMBERS * 4, 128), f32),
        ),
        in_specs=[VMEM, VMEM, VMEM],
        out_specs=(HBM, HBM, HBM),
        scratch_shapes=[
            pltpu.VMEM((2, MEMBERS, MEMBERS), bf16),
            pltpu.VMEM((MEMBERS * 4, 128), f32),
            pltpu.SemaphoreType.DMA((3,)),
        ],
        compiler_params=params(32),
        name="analyse",
    )(predicted, slot_rows, state)


def smooth_kernel(gain_hi, gain_lo, state, out):
    out[0] = product((gain_hi[...], gain_lo[...]), halves(state[0]))


def smooth(gain_hi, gain_lo, states):
    whole = pl.BlockSpec((MEMBERS, MEMBERS), lambda i: (0, 0))
    one = pl.BlockSpec((1, MEMBERS, STATE), lambda i: (i, 0, 0))
    return pl.pallas_call(
        smooth_kernel,
        out_shape=jax.ShapeDtypeStruct((LAGS, MEMBERS, STATE), f32),
        grid=(LAGS,),
        in_specs=[whole, whole, one],
        out_specs=one,
        compiler_params=params(24),
        cost_estimate=pl.CostEstimate(
            flops=2 * 3 * LAGS * MEMBERS**2 * STATE, bytes_accessed=8 * LAGS * MEMBERS * STATE, transcendentals=0
        ),
        name="smooth",
    )(gain_hi, gain_lo, states)


def assemble_kernel(parts, out, sems):
    copies = [pltpu.make_async_copy(parts.at[k], out.at[:, k], sems.at[k]) for k in range(PARTS)]
    for copy in copies:
        copy.start()
    for copy in copies:
        copy.wait()


def assemble(parts):
    return pl.pallas_call(
        assemble_kernel,
        out_shape=pltpu.HBM((ROWS, PARTS, 4, 128), f32),
        in_specs=[pl.BlockSpec(memory_space=pl.ANY)],
        out_specs=HBM,
        scratch_shapes=[pltpu.SemaphoreType.DMA((PARTS,))],
        compiler_params=params(8),
        name="assemble",
    )(parts)


def along_tiles(x, by):
    return lax.ppermute(x, "tile", [(i, (i + by) % TILES) for i in range(TILES)])


def far(x):
    return pltpu.with_memory_space_constraint(x, pltpu.HBM)


def exchange(x):
    return lax.all_to_all(x, GROUP, split_axis=0, concat_axis=0, tiled=True)


def per_device(
    current_state, lagged_states, water_depth, obs_cells, obs_values, obs_errors, tile_obs
):
    cur = current_state.reshape(ROWS, 2, CHUNKS, 128).transpose(0, 2, 1, 3)
    depth = water_depth.reshape(CHUNKS, 128)
    to_right, to_left = edges(far(cur.reshape(ROWS, 2 * CHUNKS, 128)), far(depth))
    left = along_tiles(to_right, 1)
    right = along_tiles(to_left, -1)
    to_left, listed = lax.optimization_barrier((to_left, tile_obs[0, 0].reshape(8, 128)))
    ordered, payload, cur, depth, cells = order(
        far(listed),
        far(cur.reshape(ROWS, PARTS, 4, 128)),
        far(cur.reshape(ROWS * 2 * CHUNKS, 128)),
        far(depth),
        far(obs_cells.reshape(TILES, 8, 128)),
    )
    payload = with_beside(payload, cur, left, right)
    received = exchange(payload.reshape(PARTS, ROWS * 4 + 16, 128))
    own = heights(cur, depth, left, right, cells)
    below = along_tiles(own, 1)
    above = along_tiles(own, -1)
    picked = pick(received, below, own, above)
    predicted = exchange(picked).reshape(MEMBERS, SLOTS)
    state = forecast(received, depth, left, right)
    slot_rows = slots(
        ordered,
        obs_values.reshape(TILES, 8, 128),
        obs_errors.reshape(TILES, 8, 128),
        obs_cells.reshape(TILES, 8, 128),
    )
    gain_hi, gain_lo, analysis = analyse(predicted, slot_rows, state)
    returned = exchange(analysis.reshape(PARTS, ROWS * 4, 128))
    older = smooth(gain_hi, gain_lo, lagged_states.reshape(LAGS, MEMBERS, STATE))
    analysed = assemble(returned.reshape(PARTS, ROWS, 4, 128))
    analysed = analysed.reshape(ROWS, CHUNKS, 2, 128).transpose(0, 2, 1, 3)
    return (
        analysed.reshape(ROWS, 2, CELLS),
        older.reshape(LAGS, 1, 1, MEMBERS, STATE),
    )


def solution(mesh):
    placed = (
        P(GROUP, None, "tile"),
        P(None, "tile", GROUP, None, None),
        P("tile"),
        P(),
        P(),
        P(),
        P("tile", GROUP, None),
    )
    return jax.shard_map(
        per_device,
        mesh=mesh,
        in_specs=placed,
        out_specs=(P(GROUP, None, "tile"), P(None, "tile", GROUP, None, None)),
        check_vma=False,
    )
```

```python
import functools
import math

import jax
import jax.numpy as jnp
from jax import lax
from jax.experimental import pallas as pl
from jax.experimental.pallas import tpu as pltpu
from jax.sharding import PartitionSpec as P

GROUP = ("grp", "mem")
PARTS = 8
ROWS = 64
MEMBERS = 512
CELLS = 2048
CHUNKS = 16
CELLS_TILE = 256
STATE = 512
OBS = 1024
SLOTS = 1024
NOBS = 32768
NCELLS = 65536
TILES = 32
LOC = 512
LAGS = 3
DIRECT = 4
f32 = jnp.float32
bf16 = jnp.bfloat16
VMEM = pl.BlockSpec(memory_space=pltpu.VMEM)
HBM = pl.BlockSpec(memory_space=pltpu.HBM)
SMEM = pl.BlockSpec(memory_space=pltpu.SMEM)


def params(mib):
    return pltpu.CompilerParams(vmem_limit_bytes=mib * 1024 * 1024)


def cost(flops):
    return pl.CostEstimate(flops=flops, bytes_accessed=2**20, transcendentals=0)


def halves(x):
    hi = x.astype(bf16)
    return hi, (x - hi.astype(f32)).astype(bf16)


def dot(a, b):
    return jnp.dot(a, b, preferred_element_type=f32)


def dot_nt(a, b):
    return lax.dot_general(a, b, (((1,), (1,)), ((), ())), preferred_element_type=f32)


def product(a, b):
    (ah, al), (bh, bl) = a, b
    return dot(ah, bh) + (dot(ah, bl) + dot(al, bh))


def edges_kernel(far_cur, far_depth, cur, to_right, to_left, depth, sems):
    arrivals = [
        pltpu.make_async_copy(far_cur, cur, sems.at[0]),
        pltpu.make_async_copy(far_depth, depth, sems.at[1]),
    ]
    for arrival in arrivals:
        arrival.start()
    low_half = lax.broadcasted_iota(jnp.int32, (ROWS, 128), 1) < ROWS
    end = CHUNKS - 1
    arrivals[1].wait()
    to_right[ROWS:, :] = jnp.broadcast_to(depth[end : end + 1, :], (8, 128))
    to_left[ROWS:, :] = jnp.broadcast_to(depth[0:1, :], (8, 128))
    arrivals[0].wait()

    def old(c, v):
        return cur[pl.ds(2 * c + v, ROWS, stride=2 * CHUNKS), :]

    to_right[:ROWS, :] = jnp.where(low_half, pltpu.roll(old(end, 0), ROWS, 1), old(end, 1))
    to_left[:ROWS, :] = jnp.where(low_half, old(0, 0), pltpu.roll(old(0, 1), ROWS, 1))


def edges(cur, depth):
    message = jax.ShapeDtypeStruct((ROWS + 8, 128), f32)
    return pl.pallas_call(
        edges_kernel,
        out_shape=(jax.ShapeDtypeStruct(cur.shape, f32), message, message),
        in_specs=[HBM, HBM],
        out_specs=(VMEM, VMEM, VMEM),
        scratch_shapes=[pltpu.VMEM((CHUNKS, 128), f32), pltpu.SemaphoreType.DMA((2,))],
        compiler_params=params(8),
        name="edges",
    )(cur, depth)


def order_kernel(
    far_list, by_part, far_depth, far_cells,
    ordered, payload, depth, cells, tile_list, row_list, row_place, filled, sems, sent,
):
    tile = lax.axis_index("tile")
    arrivals = [
        pltpu.make_async_copy(source, target, sems.at[n])
        for n, (source, target) in enumerate(
            ((far_list, tile_list), (far_cells.at[tile], cells), (far_depth, depth))
        )
    ]
    raw = [
        pltpu.make_async_copy(by_part.at[:, k], payload.at[k, pl.ds(0, ROWS)], sent.at[k])
        for k in range(PARTS)
    ]
    for copy in arrivals + raw:
        copy.start()
    arrivals[0].wait()
    listed = tile_list[...]
    rel = jnp.where(listed >= 0, (listed - (tile - 1) * OBS) & (NOBS - 1), -1)
    count = jnp.sum(jnp.where(rel >= 0, 1.0, 0.0))
    top = jnp.max(rel)
    for j in range(8):
        row_list[0:1, j * 128 : (j + 1) * 128] = rel[j : j + 1, :]
    row = row_list[0:1, :]
    chunks = 3 * OBS // 128

    def iota(shape, dim):
        return lax.broadcasted_iota(jnp.int32, shape, dim)

    def flags(x):
        return jnp.where(x, 1.0, 0.0).astype(bf16)

    in_chunk = flags((row >> 7) == iota((32, SLOTS), 0))
    in_lane = flags((row & 127) == iota((128, SLOTS), 0))
    present = dot_nt(in_chunk, in_lane).astype(bf16)
    before = dot(present, flags(iota((128, 128), 0) < iota((128, 128), 1)))
    totals = dot(present, jnp.ones((128, 128), bf16)).astype(bf16)
    place = before + dot(flags(iota((32, 32), 1) < iota((32, 32), 0)), totals)
    place = jnp.where(present.astype(f32) > 0.5, place, -1.0).astype(jnp.int32)
    for c in range(chunks):
        row_place[0:1, c * 128 : (c + 1) * 128] = place[c : c + 1, :]
    row = row_place[0:1, :]
    wide = 3 * OBS
    to_row = (row >> 7) == iota((8, wide), 0)
    number = iota((8, wide), 1)
    parts = jnp.concatenate(
        [jnp.where(to_row, number >> 7, 0), jnp.where(to_row, number & 127, 0)], axis=0
    )
    found = dot_nt(parts.astype(f32).astype(bf16), flags((row & 127) == iota((128, wide), 0)))
    found = (found[:8] * 128.0 + found[8:]).astype(jnp.int32)
    used = (iota((8, 128), 0) * 128 + iota((8, 128), 1)).astype(f32) < count
    ordered[...] = jnp.where(used, found, -1)
    whole = jnp.where(used, found, jnp.maximum(top, 0)).astype(f32)
    filled[0], filled[1] = whole[:4], whole[4:]
    lists = [
        pltpu.make_async_copy(filled, payload.at[k, pl.ds(ROWS, 2)], sent.at[PARTS + k])
        for k in range(PARTS)
    ]
    for copy in lists:
        copy.start()
    for copy in arrivals[1:] + raw + lists:
        copy.wait()
    cells[...] = cells[...] - tile * CELLS


def order(tile_list, parts, depth, cells):
    return pl.pallas_call(
        order_kernel,
        out_shape=(
            jax.ShapeDtypeStruct((8, 128), jnp.int32),
            pltpu.HBM((PARTS, ROWS + 4, 4, 128), f32),
            jax.ShapeDtypeStruct((CHUNKS, 128), f32),
            jax.ShapeDtypeStruct((8, 128), jnp.int32),
        ),
        in_specs=[HBM, VMEM, HBM, HBM],
        out_specs=(VMEM, HBM, VMEM, VMEM),
        scratch_shapes=[
            pltpu.VMEM((8, 128), jnp.int32),
            pltpu.VMEM((8, SLOTS), jnp.int32),
            pltpu.VMEM((8, 3 * OBS), jnp.int32),
            pltpu.VMEM((2, 4, 128), f32),
            pltpu.SemaphoreType.DMA((3,)),
            pltpu.SemaphoreType.DMA((2 * PARTS,)),
        ],
        cost_estimate=pl.CostEstimate(flops=0, bytes_accessed=100 * 2**20, transcendentals=0),
        compiler_params=params(12),
        name="order",
    )(tile_list, parts, depth, cells)


def chunk_with_halo(cur, left, right, c, v):
    if c < 0:
        x = left[:ROWS, :]
        return x if v else pltpu.roll(x, ROWS, 1)
    if c == CHUNKS:
        x = right[:ROWS, :]
        return pltpu.roll(x, ROWS, 1) if v else x
    return cur[pl.ds(2 * c + v, ROWS, stride=2 * CHUNKS), :]


def beside_kernel(_, cur, left, right, payload, rows, sems):
    def turned(c):
        pair = [chunk_with_halo(cur, left, right, c, v) for v in range(2)]
        return jnp.concatenate(pair, axis=0).T

    upper = lax.broadcasted_iota(jnp.int32, (8, 128), 0) < 4
    copies = []
    for k in range(PARTS):
        chosen = jnp.where(upper, turned(2 * k + 2)[:8], turned(2 * k - 1)[120:])
        rows[k, 0], rows[k, 1] = chosen[:4], chosen[4:]
        copies.append(
            pltpu.make_async_copy(rows.at[k], payload.at[k, pl.ds(ROWS + 2, 2)], sems.at[k])
        )
        copies[k].start()
    for copy in copies:
        copy.wait()


def with_beside(payload, cur, left, right):
    return pl.pallas_call(
        beside_kernel,
        out_shape=pltpu.HBM(payload.shape, f32),
        in_specs=[HBM, VMEM, VMEM, VMEM],
        out_specs=HBM,
        scratch_shapes=[pltpu.VMEM((PARTS, 2, 4, 128), f32), pltpu.SemaphoreType.DMA((PARTS,))],
        input_output_aliases={0: 0},
        compiler_params=params(8),
        cost_estimate=cost(1000),
        name="beside",
    )(payload, cur, left, right)


def take_lanes(chunk_of, chunks, index):
    at = jnp.broadcast_to(index, (8, 128))
    lane = at & 127
    chunk = at >> 7
    out = []
    for g in range(ROWS // 8):
        found = jnp.take_along_axis(chunk_of(g, 0), lane, axis=1)
        out.append(found)
    for c in range(1, chunks):
        here = chunk == c
        for g in range(ROWS // 8):
            out[g] = jnp.where(here, jnp.take_along_axis(chunk_of(g, c), lane, axis=1), out[g])
    return out


def heights_kernel(cur, depth, left, right, cells, own, hbuf, ubuf):
    lane = lax.broadcasted_iota(jnp.int32, (ROWS, 128), 1)
    first, last = lane == 0, lane == 127

    def old(c, v):
        return chunk_with_halo(cur, left, right, c, v)

    def scaled_depth(c):
        if c < 0:
            row = left[ROWS : ROWS + 1, :]
        elif c == CHUNKS:
            row = right[ROWS : ROWS + 1, :]
        else:
            row = depth[c : c + 1, :]
        return 0.9 * row

    def height_step(h_of, u_of):
        before = None
        for c in range(-1, CHUNKS + 1):
            u = u_of(c)
            turned = pltpu.roll(u, 1, 1)
            previous = turned if before is None else jnp.where(first, before, turned)
            before = turned
            hbuf[c + 1] = h_of(c) - scaled_depth(c) * (u - previous)

    height_step(lambda c: old(c, 0), lambda c: old(c, 1))
    turned = pltpu.roll(hbuf[0], 127, 1)
    for c in range(-1, CHUNKS + 1):
        after = pltpu.roll(hbuf[c + 2], 127, 1) if c < CHUNKS else turned
        following = jnp.where(last, after, turned)
        turned = after
        ubuf[c + 1] = old(c, 1) - 0.9 * (following - hbuf[c + 1])
    height_step(lambda c: hbuf[c + 1], lambda c: ubuf[c + 1])

    for j in range(OBS // 128):
        rows = take_lanes(lambda g, c: hbuf[c + 1, g * 8 : g * 8 + 8, :], CHUNKS, cells[j : j + 1, :])
        for g in range(ROWS // 8):
            own[g * 8 : g * 8 + 8, j * 128 : (j + 1) * 128] = rows[g]


def heights(cur, depth, left, right, cells):
    buffer = pltpu.VMEM((CHUNKS + 2, ROWS, 128), f32)
    return pl.pallas_call(
        heights_kernel,
        out_shape=jax.ShapeDtypeStruct((ROWS, OBS), f32),
        in_specs=[VMEM] * 5,
        out_specs=VMEM,
        scratch_shapes=[buffer, buffer],
        compiler_params=params(12),
        cost_estimate=cost(10**12),
        name="heights",
    )(cur, depth, left, right, cells)


def forecast_kernel(received, depth, left, right, state, beside, depths):
    part = lax.axis_index("grp") * lax.axis_size("mem") + lax.axis_index("mem")
    depths[0:1, :] = left[ROWS : ROWS + 1, :]
    depths[1 : CHUNKS + 1, :] = depth[...]
    depths[CHUNKS + 1 : CHUNKS + 2, :] = right[ROWS : ROWS + 1, :]
    scaled = [0.9 * depths[pl.ds(2 * part + i, 1), :] for i in range(4)]
    lane = lax.broadcasted_iota(jnp.int32, (ROWS, 128), 1)
    first, last = lane == 0, lane == 127
    beside[...] = jnp.zeros((128, 128), f32)

    def height_step(h, u, low):
        turned = [pltpu.roll(x, 1, 1) for x in u]
        out = list(h)
        for i in range(low, 4):
            previous = turned[i] if i == 0 else jnp.where(first, turned[i - 1], turned[i])
            out[i] = h[i] - scaled[i] * (u[i] - previous)
        return out

    def speed_step(h, u, low, high):
        turned = [pltpu.roll(x, 127, 1) for x in h]
        out = list(u)
        for i in range(low, high):
            following = turned[i] if i == 3 else jnp.where(last, turned[i + 1], turned[i])
            out[i] = u[i] - 0.9 * (following - h[i])
        return out

    for b in range(PARTS):
        edge = received[b, 4 * ROWS + 8 : 4 * ROWS + 16, :]
        beside[0:8, :] = edge
        beside[120:128, :] = edge
        turned = beside[...].T
        own = [received[b, pl.ds(j, ROWS, stride=4), :] for j in range(4)]
        h = [turned[:ROWS], own[0], own[2], turned[:ROWS]]
        u = [turned[ROWS:], own[1], own[3], turned[ROWS:]]
        h = height_step(h, u, 0)
        u = speed_step(h, u, 0, 4)
        h = height_step(h, u, 1)
        u = speed_step(h, u, 1, 3)
        for i, x in enumerate((h[1], h[2], u[1], u[2])):
            state[b * ROWS : (b + 1) * ROWS, i * 128 : (i + 1) * 128] = x


def forecast(received, depth, left, right):
    return pl.pallas_call(
        forecast_kernel,
        out_shape=jax.ShapeDtypeStruct((MEMBERS, STATE), f32),
        in_specs=[VMEM] * 4,
        out_specs=VMEM,
        scratch_shapes=[pltpu.VMEM((128, 128), f32), pltpu.VMEM((24, 128), f32)],
        compiler_params=params(8),
        cost_estimate=cost(10**10),
        name="forecast",
    )(received, depth, left, right)


def pick_kernel(received, below, own, above, out, source, held, lists, bounds, sems, list_sem):
    for k in range(PARTS):
        lists[k] = received[k, 4 * ROWS : 4 * ROWS + 8, :].astype(jnp.int32)
    to_scalars = pltpu.make_async_copy(lists, bounds, list_sem)
    to_scalars.start()
    for n, part in enumerate((below, own, above)):
        for c in range(8):
            source[n * 8 + c] = part[:, c * 128 : (c + 1) * 128]
    to_scalars.wait()

    def send(k):
        return pltpu.make_async_copy(held.at[k], out.at[k], sems.at[k])

    def take(c, g, lane):
        return jnp.take_along_axis(source[c, g * 8 : g * 8 + 8, :], lane, axis=1)

    def one_list(k, carry):
        blocks = []
        for j in range(8):
            at = jnp.broadcast_to(lists[k, j : j + 1, :], (8, 128))
            lane, chunk = at & 127, at >> 7
            low, high = bounds[k, j, 0] >> 7, bounds[k, j, 127] >> 7
            blocks.append((j, lane, chunk, low, high))
            found = [take(low, g, lane) for g in range(ROWS // 8)]
            for d in range(1, DIRECT):
                here = chunk == low + d
                found = [jnp.where(here, take(low + d, g, lane), f) for g, f in enumerate(found)]
            for g in range(ROWS // 8):
                held[k, g * 8 : g * 8 + 8, j * 128 : (j + 1) * 128] = found[g]
        for j, lane, chunk, low, high in blocks:

            def more(c, carry):
                here = chunk == c
                for g in range(ROWS // 8):
                    at = (k, slice(g * 8, g * 8 + 8), slice(j * 128, (j + 1) * 128))
                    held[at] = jnp.where(here, take(c, g, lane), held[at])
                return carry

            lax.fori_loop(low + DIRECT, high + 1, more, 0)
        send(k).start()
        return carry

    lax.fori_loop(0, PARTS, one_list, 0)
    for k in range(PARTS):
        send(k).wait()


def pick(received, below, own, above):
    return pl.pallas_call(
        pick_kernel,
        out_shape=pltpu.HBM((PARTS, ROWS, SLOTS), f32),
        in_specs=[VMEM] * 4,
        out_specs=HBM,
        scratch_shapes=[
            pltpu.VMEM((24 + DIRECT, ROWS, 128), f32),
            pltpu.VMEM((PARTS, ROWS, SLOTS), f32),
            pltpu.VMEM((PARTS, 8, 128), jnp.int32),
            pltpu.SMEM((PARTS, 8, 128), jnp.int32),
            pltpu.SemaphoreType.DMA((PARTS,)),
            pltpu.SemaphoreType.DMA,
        ],
        compiler_params=params(16),
        cost_estimate=cost(10**12),
        name="pick",
    )(received, below, own, above)


def slots_kernel(rel, values, errors, cells, out):
    tile = lax.axis_index("tile")
    part = lax.axis_index("grp") * lax.axis_size("mem") + lax.axis_index("mem")
    center = tile * CELLS + part * CELLS_TILE + CELLS_TILE // 2
    listed = rel[...]
    at = jnp.maximum(listed, 0)
    lane = at & 127
    chunk = at >> 7
    value = jnp.zeros((8, 128), f32)
    error = jnp.ones((8, 128), f32)
    cell = jnp.zeros((8, 128), jnp.int32)
    for n in range(3):
        t = lax.rem(tile + (TILES - 1 + n), TILES)
        for j in range(8):
            here = chunk == n * 8 + j

            def found(ref):
                row = jnp.broadcast_to(ref[t, j : j + 1, :], (8, 128))
                return jnp.take_along_axis(row, lane, axis=1)

            value = jnp.where(here, found(values), value)
            error = jnp.where(here, found(errors), error)
            cell = jnp.where(here, found(cells), cell)
    distance = jnp.abs(cell - center)
    distance = jnp.minimum(distance, NCELLS - distance).astype(f32)
    weight = jnp.exp(-0.5 * (distance / LOC) ** 2) / (error * error)
    weight = jnp.where(listed >= 0, weight, 0.0)
    for j in range(8):
        out[0:1, j * 128 : (j + 1) * 128] = weight[j : j + 1, :]
        out[1:2, j * 128 : (j + 1) * 128] = value[j : j + 1, :]


def slots(rel, values, errors, cells):
    return pl.pallas_call(
        slots_kernel,
        out_shape=jax.ShapeDtypeStruct((8, SLOTS), f32),
        in_specs=[VMEM] * 4,
        out_specs=VMEM,
        compiler_params=params(8),
        name="slots",
    )(rel, values, errors, cells)


def analyse_kernel(
    predicted, slot_rows, state, gain_hi, gain_lo, analysis,
    left, right, z_left, z_right, y_right, slots_left, slots_right, held, result, sems,
):
    n = MEMBERS

    def put_left(ref, x, rows=slice(None)):
        high, low = halves(x)
        k = x.shape[1]
        ref[rows, :k] = high
        ref[rows, k : 2 * k] = high
        ref[rows, 2 * k :] = low

    def put_right(ref, x):
        high, low = halves(x)
        ref[:n] = high
        ref[n : 2 * n] = low
        ref[2 * n :] = high

    def times(a, b):
        return dot(a[...], b[...])

    y = predicted[...]
    weight = slot_rows[0:1, :]
    mean = jnp.sum(y, axis=0, keepdims=True) * (1.0 / MEMBERS)
    root_weight = jnp.sqrt(weight)
    spread = (y - mean) * root_weight
    departure = (slot_rows[1:2, :] - mean) * root_weight
    put_left(slots_left, spread, slice(0, n))
    put_left(slots_left, jnp.broadcast_to(departure, (16, SLOTS)), slice(n, n + 16))
    high, low = halves(spread)
    slots_right[:, :SLOTS] = high
    slots_right[:, SLOTS : 2 * SLOTS] = low
    slots_right[:, 2 * SLOTS :] = high
    on_diagonal = lax.broadcasted_iota(jnp.int32, (n, n), 0) == lax.broadcasted_iota(
        jnp.int32, (n, n), 1
    )

    def plus(x, d):
        return jnp.where(on_diagonal, x + d, x)

    products = dot_nt(slots_left[...], slots_right[...])
    a = plus(products[:n], MEMBERS - 1.0)
    innovation = products[n : n + 1]
    bound = jnp.max(jnp.sum(jnp.abs(a), axis=0, keepdims=True), axis=1, keepdims=True)
    approx = a / bound

    def two_steps(m):
        put_left(left, m)
        put_right(right, m)
        m2 = times(left, right)
        put_left(left, m2)
        put_right(right, plus(0.0625 * m2 - 0.5625 * m, 1.6875))
        return plus(times(left, right) - 2.4375 * m, 2.25)

    r = two_steps(approx)
    put_left(left, r)
    put_right(z_right, r)
    put_right(y_right, approx)
    put_right(y_right, times(left, y_right))
    r = two_steps(times(left, y_right))
    put_left(left, r)
    z = times(left, z_right)
    put_right(y_right, times(left, y_right))
    put_right(z_right, z)
    put_left(z_left, z)
    put_left(left, two_steps(times(z_left, y_right)))
    root = times(left, z_right) * lax.rsqrt(bound)
    once = jnp.sum(root * innovation, axis=1, keepdims=True)
    mean_weight = jnp.sum(root * once, axis=0, keepdims=True)
    moved = math.sqrt(MEMBERS - 1) * root + mean_weight
    gain = moved + (1.0 - jnp.sum(moved, axis=1, keepdims=True)) * (1.0 / MEMBERS)
    put_left(left, gain)
    held[0], held[1] = halves(gain)
    copies = [
        pltpu.make_async_copy(held.at[0], gain_hi, sems.at[0]),
        pltpu.make_async_copy(held.at[1], gain_lo, sems.at[1]),
        pltpu.make_async_copy(result, analysis, sems.at[2]),
    ]
    copies[0].start()
    copies[1].start()
    put_right(right, state[...])
    analysed = times(left, right)
    for row in range(4):
        at = (row % 2) * CELLS_TILE + (row // 2) * 128
        result[pl.ds(row, MEMBERS, stride=4), :] = analysed[:, at : at + 128]
    copies[2].start()
    for copy in copies:
        copy.wait()


def analyse(predicted, slot_rows, state):
    return pl.pallas_call(
        analyse_kernel,
        out_shape=(
            pltpu.HBM((MEMBERS, MEMBERS), bf16),
            pltpu.HBM((MEMBERS, MEMBERS), bf16),
            pltpu.HBM((MEMBERS * 4, 128), f32),
        ),
        in_specs=[VMEM, VMEM, VMEM],
        out_specs=(HBM, HBM, HBM),
        scratch_shapes=[
            pltpu.VMEM((MEMBERS, 3 * MEMBERS), bf16),
            pltpu.VMEM((3 * MEMBERS, MEMBERS), bf16),
            pltpu.VMEM((MEMBERS, 3 * MEMBERS), bf16),
            pltpu.VMEM((3 * MEMBERS, MEMBERS), bf16),
            pltpu.VMEM((3 * MEMBERS, MEMBERS), bf16),
            pltpu.VMEM((MEMBERS + 16, 3 * SLOTS), bf16),
            pltpu.VMEM((MEMBERS, 3 * SLOTS), bf16),
            pltpu.VMEM((2, MEMBERS, MEMBERS), bf16),
            pltpu.VMEM((MEMBERS * 4, 128), f32),
            pltpu.SemaphoreType.DMA((3,)),
        ],
        compiler_params=params(40),
        name="analyse",
    )(predicted, slot_rows, state)


def smooth_kernel(gain_hi, gain_lo, state, out):
    out[0] = product((gain_hi[...], gain_lo[...]), halves(state[0]))


def smooth(gain_hi, gain_lo, states):
    whole = pl.BlockSpec((MEMBERS, MEMBERS), lambda i: (0, 0))
    one = pl.BlockSpec((1, MEMBERS, STATE), lambda i: (i, 0, 0))
    return pl.pallas_call(
        smooth_kernel,
        out_shape=jax.ShapeDtypeStruct((LAGS, MEMBERS, STATE), f32),
        grid=(LAGS,),
        in_specs=[whole, whole, one],
        out_specs=one,
        compiler_params=params(24),
        cost_estimate=pl.CostEstimate(
            flops=2 * 3 * LAGS * MEMBERS**2 * STATE, bytes_accessed=8 * LAGS * MEMBERS * STATE, transcendentals=0
        ),
        name="smooth",
    )(gain_hi, gain_lo, states)


def assemble_kernel(parts, out, sems):
    copies = [pltpu.make_async_copy(parts.at[k], out.at[:, k], sems.at[k]) for k in range(PARTS)]
    for copy in copies:
        copy.start()
    for copy in copies:
        copy.wait()


def assemble(parts):
    return pl.pallas_call(
        assemble_kernel,
        out_shape=pltpu.HBM((ROWS, PARTS, 4, 128), f32),
        in_specs=[pl.BlockSpec(memory_space=pl.ANY)],
        out_specs=HBM,
        scratch_shapes=[pltpu.SemaphoreType.DMA((PARTS,))],
        compiler_params=params(8),
        name="assemble",
    )(parts)


def along_tiles(x, by):
    return lax.ppermute(x, "tile", [(i, (i + by) % TILES) for i in range(TILES)])


def far(x):
    return pltpu.with_memory_space_constraint(x, pltpu.HBM)


def exchange(x):
    return lax.all_to_all(x, GROUP, split_axis=0, concat_axis=0, tiled=True)


def per_device(
    current_state, lagged_states, water_depth, obs_cells, obs_values, obs_errors, tile_obs
):
    cur = current_state.reshape(ROWS, 2, CHUNKS, 128).transpose(0, 2, 1, 3)
    depth = water_depth.reshape(CHUNKS, 128)
    cur, to_right, to_left = edges(far(cur.reshape(ROWS * 2 * CHUNKS, 128)), far(depth))
    left = along_tiles(to_right, 1)
    right = along_tiles(to_left, -1)
    to_left, listed = lax.optimization_barrier((to_left, tile_obs[0, 0].reshape(8, 128)))
    ordered, payload, depth, cells = order(
        far(listed),
        cur.reshape(ROWS, PARTS, 4, 128),
        far(depth),
        far(obs_cells.reshape(TILES, 8, 128)),
    )
    payload = with_beside(payload, cur, left, right)
    received = exchange(payload.reshape(PARTS, ROWS * 4 + 16, 128))
    own = heights(cur, depth, left, right, cells)
    below = along_tiles(own, 1)
    above = along_tiles(own, -1)
    picked = pick(received, below, own, above)
    predicted = exchange(picked).reshape(MEMBERS, SLOTS)
    state = forecast(received, depth, left, right)
    slot_rows = slots(
        ordered,
        obs_values.reshape(TILES, 8, 128),
        obs_errors.reshape(TILES, 8, 128),
        obs_cells.reshape(TILES, 8, 128),
    )
    gain_hi, gain_lo, analysis = analyse(predicted, slot_rows, state)
    returned = exchange(analysis.reshape(PARTS, ROWS * 4, 128))
    older = smooth(gain_hi, gain_lo, lagged_states.reshape(LAGS, MEMBERS, STATE))
    analysed = assemble(returned.reshape(PARTS, ROWS, 4, 128))
    analysed = analysed.reshape(ROWS, CHUNKS, 2, 128).transpose(0, 2, 1, 3)
    return (
        analysed.reshape(ROWS, 2, CELLS),
        older.reshape(LAGS, 1, 1, MEMBERS, STATE),
    )


def solution(mesh):
    placed = (
        P(GROUP, None, "tile"),
        P(None, "tile", GROUP, None, None),
        P("tile"),
        P(),
        P(),
        P(),
        P("tile", GROUP, None),
    )
    return jax.shard_map(
        per_device,
        mesh=mesh,
        in_specs=placed,
        out_specs=(P(GROUP, None, "tile"), P(None, "tile", GROUP, None, None)),
        check_vma=False,
    )
```

```python
import functools
import math

import jax
import jax.numpy as jnp
from jax import lax
from jax.experimental import pallas as pl
from jax.experimental.pallas import tpu as pltpu
from jax.sharding import PartitionSpec as P

GROUP = ("grp", "mem")
PARTS = 8
ROWS = 64
MEMBERS = 512
CELLS = 2048
CHUNKS = 16
CELLS_TILE = 256
STATE = 512
OBS = 1024
SLOTS = 1024
NOBS = 32768
NCELLS = 65536
TILES = 32
LOC = 512
LAGS = 3
DIRECT = 3
f32 = jnp.float32
bf16 = jnp.bfloat16
VMEM = pl.BlockSpec(memory_space=pltpu.VMEM)
HBM = pl.BlockSpec(memory_space=pltpu.HBM)
SMEM = pl.BlockSpec(memory_space=pltpu.SMEM)


def params(mib):
    return pltpu.CompilerParams(vmem_limit_bytes=mib * 1024 * 1024)


def cost(flops):
    return pl.CostEstimate(flops=flops, bytes_accessed=2**20, transcendentals=0)


def halves(x):
    hi = x.astype(bf16)
    return hi, (x - hi.astype(f32)).astype(bf16)


def dot(a, b):
    return jnp.dot(a, b, preferred_element_type=f32)


def dot_nt(a, b):
    return lax.dot_general(a, b, (((1,), (1,)), ((), ())), preferred_element_type=f32)


def product(a, b):
    (ah, al), (bh, bl) = a, b
    return dot(ah, bh) + (dot(ah, bl) + dot(al, bh))


def edges_kernel(far_cur, far_depth, cur, to_right, to_left, depth, sems):
    arrivals = [
        pltpu.make_async_copy(far_cur, cur, sems.at[0]),
        pltpu.make_async_copy(far_depth, depth, sems.at[1]),
    ]
    for arrival in arrivals:
        arrival.start()
    low_half = lax.broadcasted_iota(jnp.int32, (ROWS, 128), 1) < ROWS
    end = CHUNKS - 1
    arrivals[1].wait()
    to_right[ROWS:, :] = jnp.broadcast_to(depth[end : end + 1, :], (8, 128))
    to_left[ROWS:, :] = jnp.broadcast_to(depth[0:1, :], (8, 128))
    arrivals[0].wait()

    def old(c, v):
        return cur[pl.ds(2 * c + v, ROWS, stride=2 * CHUNKS), :]

    to_right[:ROWS, :] = jnp.where(low_half, pltpu.roll(old(end, 0), ROWS, 1), old(end, 1))
    to_left[:ROWS, :] = jnp.where(low_half, old(0, 0), pltpu.roll(old(0, 1), ROWS, 1))


def edges(cur, depth):
    message = jax.ShapeDtypeStruct((ROWS + 8, 128), f32)
    return pl.pallas_call(
        edges_kernel,
        out_shape=(jax.ShapeDtypeStruct(cur.shape, f32), message, message),
        in_specs=[HBM, HBM],
        out_specs=(VMEM, VMEM, VMEM),
        scratch_shapes=[pltpu.VMEM((CHUNKS, 128), f32), pltpu.SemaphoreType.DMA((2,))],
        compiler_params=params(8),
        name="edges",
    )(cur, depth)


def order_kernel(
    far_list, by_part, far_depth, far_cells,
    ordered, payload, depth, cells, tile_list, row_list, row_place, filled, sems, sent,
):
    tile = lax.axis_index("tile")
    arrivals = [
        pltpu.make_async_copy(source, target, sems.at[n])
        for n, (source, target) in enumerate(
            ((far_list, tile_list), (far_cells.at[tile], cells), (far_depth, depth))
        )
    ]
    raw = [
        pltpu.make_async_copy(by_part.at[:, k], payload.at[k, pl.ds(0, ROWS)], sent.at[k])
        for k in range(PARTS)
    ]
    for copy in arrivals + raw:
        copy.start()
    arrivals[0].wait()
    listed = tile_list[...]
    rel = jnp.where(listed >= 0, (listed - (tile - 1) * OBS) & (NOBS - 1), -1)
    count = jnp.sum(jnp.where(rel >= 0, 1.0, 0.0))
    top = jnp.max(rel)
    for j in range(8):
        row_list[0:1, j * 128 : (j + 1) * 128] = rel[j : j + 1, :]
    row = row_list[0:1, :]
    chunks = 3 * OBS // 128

    def iota(shape, dim):
        return lax.broadcasted_iota(jnp.int32, shape, dim)

    def flags(x):
        return jnp.where(x, 1.0, 0.0).astype(bf16)

    in_chunk = flags((row >> 7) == iota((32, SLOTS), 0))
    in_lane = flags((row & 127) == iota((128, SLOTS), 0))
    present = dot_nt(in_chunk, in_lane).astype(bf16)
    before = dot(present, flags(iota((128, 128), 0) < iota((128, 128), 1)))
    totals = dot(present, jnp.ones((128, 128), bf16)).astype(bf16)
    place = before + dot(flags(iota((32, 32), 1) < iota((32, 32), 0)), totals)
    place = jnp.where(present.astype(f32) > 0.5, place, -1.0).astype(jnp.int32)
    for c in range(chunks):
        row_place[0:1, c * 128 : (c + 1) * 128] = place[c : c + 1, :]
    row = row_place[0:1, :]
    wide = 3 * OBS
    to_row = (row >> 7) == iota((8, wide), 0)
    number = iota((8, wide), 1)
    parts = jnp.concatenate(
        [jnp.where(to_row, number >> 7, 0), jnp.where(to_row, number & 127, 0)], axis=0
    )
    found = dot_nt(parts.astype(f32).astype(bf16), flags((row & 127) == iota((128, wide), 0)))
    found = (found[:8] * 128.0 + found[8:]).astype(jnp.int32)
    used = (iota((8, 128), 0) * 128 + iota((8, 128), 1)).astype(f32) < count
    ordered[...] = jnp.where(used, found, -1)
    whole = jnp.where(used, found, jnp.maximum(top, 0)).astype(f32)
    filled[0], filled[1] = whole[:4], whole[4:]
    lists = [
        pltpu.make_async_copy(filled, payload.at[k, pl.ds(ROWS, 2)], sent.at[PARTS + k])
        for k in range(PARTS)
    ]
    for copy in lists:
        copy.start()
    for copy in arrivals[1:] + raw + lists:
        copy.wait()
    cells[...] = cells[...] - tile * CELLS


def order(tile_list, parts, depth, cells):
    return pl.pallas_call(
        order_kernel,
        out_shape=(
            jax.ShapeDtypeStruct((8, 128), jnp.int32),
            pltpu.HBM((PARTS, ROWS + 4, 4, 128), f32),
            jax.ShapeDtypeStruct((CHUNKS, 128), f32),
            jax.ShapeDtypeStruct((8, 128), jnp.int32),
        ),
        in_specs=[HBM, VMEM, HBM, HBM],
        out_specs=(VMEM, HBM, VMEM, VMEM),
        scratch_shapes=[
            pltpu.VMEM((8, 128), jnp.int32),
            pltpu.VMEM((8, SLOTS), jnp.int32),
            pltpu.VMEM((8, 3 * OBS), jnp.int32),
            pltpu.VMEM((2, 4, 128), f32),
            pltpu.SemaphoreType.DMA((3,)),
            pltpu.SemaphoreType.DMA((2 * PARTS,)),
        ],
        cost_estimate=pl.CostEstimate(flops=0, bytes_accessed=100 * 2**20, transcendentals=0),
        compiler_params=params(12),
        name="order",
    )(tile_list, parts, depth, cells)


def chunk_with_halo(cur, left, right, c, v):
    if c < 0:
        x = left[:ROWS, :]
        return x if v else pltpu.roll(x, ROWS, 1)
    if c == CHUNKS:
        x = right[:ROWS, :]
        return pltpu.roll(x, ROWS, 1) if v else x
    return cur[pl.ds(2 * c + v, ROWS, stride=2 * CHUNKS), :]


def beside_kernel(_, cur, left, right, payload, rows, sems):
    def turned(c):
        pair = [chunk_with_halo(cur, left, right, c, v) for v in range(2)]
        return jnp.concatenate(pair, axis=0).T

    upper = lax.broadcasted_iota(jnp.int32, (8, 128), 0) < 4
    copies = []
    for k in range(PARTS):
        chosen = jnp.where(upper, turned(2 * k + 2)[:8], turned(2 * k - 1)[120:])
        rows[k, 0], rows[k, 1] = chosen[:4], chosen[4:]
        copies.append(
            pltpu.make_async_copy(rows.at[k], payload.at[k, pl.ds(ROWS + 2, 2)], sems.at[k])
        )
        copies[k].start()
    for copy in copies:
        copy.wait()


def with_beside(payload, cur, left, right):
    return pl.pallas_call(
        beside_kernel,
        out_shape=pltpu.HBM(payload.shape, f32),
        in_specs=[HBM, VMEM, VMEM, VMEM],
        out_specs=HBM,
        scratch_shapes=[pltpu.VMEM((PARTS, 2, 4, 128), f32), pltpu.SemaphoreType.DMA((PARTS,))],
        input_output_aliases={0: 0},
        compiler_params=params(8),
        cost_estimate=cost(1000),
        name="beside",
    )(payload, cur, left, right)


def take_lanes(chunk_of, chunks, index):
    at = jnp.broadcast_to(index, (8, 128))
    lane = at & 127
    chunk = at >> 7
    out = []
    for g in range(ROWS // 8):
        found = jnp.take_along_axis(chunk_of(g, 0), lane, axis=1)
        out.append(found)
    for c in range(1, chunks):
        here = chunk == c
        for g in range(ROWS // 8):
            out[g] = jnp.where(here, jnp.take_along_axis(chunk_of(g, c), lane, axis=1), out[g])
    return out


def heights_kernel(cur, depth, left, right, cells, own, hbuf, ubuf):
    lane = lax.broadcasted_iota(jnp.int32, (ROWS, 128), 1)
    first, last = lane == 0, lane == 127

    def old(c, v):
        return chunk_with_halo(cur, left, right, c, v)

    def scaled_depth(c):
        if c < 0:
            row = left[ROWS : ROWS + 1, :]
        elif c == CHUNKS:
            row = right[ROWS : ROWS + 1, :]
        else:
            row = depth[c : c + 1, :]
        return 0.9 * row

    def height_step(h_of, u_of):
        before = None
        for c in range(-1, CHUNKS + 1):
            u = u_of(c)
            turned = pltpu.roll(u, 1, 1)
            previous = turned if before is None else jnp.where(first, before, turned)
            before = turned
            hbuf[c + 1] = h_of(c) - scaled_depth(c) * (u - previous)

    height_step(lambda c: old(c, 0), lambda c: old(c, 1))
    turned = pltpu.roll(hbuf[0], 127, 1)
    for c in range(-1, CHUNKS + 1):
        after = pltpu.roll(hbuf[c + 2], 127, 1) if c < CHUNKS else turned
        following = jnp.where(last, after, turned)
        turned = after
        ubuf[c + 1] = old(c, 1) - 0.9 * (following - hbuf[c + 1])
    height_step(lambda c: hbuf[c + 1], lambda c: ubuf[c + 1])

    for j in range(OBS // 128):
        rows = take_lanes(lambda g, c: hbuf[c + 1, g * 8 : g * 8 + 8, :], CHUNKS, cells[j : j + 1, :])
        for g in range(ROWS // 8):
            own[g * 8 : g * 8 + 8, j * 128 : (j + 1) * 128] = rows[g]


def heights(cur, depth, left, right, cells):
    buffer = pltpu.VMEM((CHUNKS + 2, ROWS, 128), f32)
    return pl.pallas_call(
        heights_kernel,
        out_shape=jax.ShapeDtypeStruct((ROWS, OBS), f32),
        in_specs=[VMEM] * 5,
        out_specs=VMEM,
        scratch_shapes=[buffer, buffer],
        compiler_params=params(12),
        cost_estimate=cost(10**12),
        name="heights",
    )(cur, depth, left, right, cells)


def forecast_kernel(received, depth, left, right, state, beside, depths):
    part = lax.axis_index("grp") * lax.axis_size("mem") + lax.axis_index("mem")
    depths[0:1, :] = left[ROWS : ROWS + 1, :]
    depths[1 : CHUNKS + 1, :] = depth[...]
    depths[CHUNKS + 1 : CHUNKS + 2, :] = right[ROWS : ROWS + 1, :]
    scaled = [0.9 * depths[pl.ds(2 * part + i, 1), :] for i in range(4)]
    lane = lax.broadcasted_iota(jnp.int32, (ROWS, 128), 1)
    first, last = lane == 0, lane == 127
    beside[...] = jnp.zeros((128, 128), f32)

    def height_step(h, u, low):
        turned = [pltpu.roll(x, 1, 1) for x in u]
        out = list(h)
        for i in range(low, 4):
            previous = turned[i] if i == 0 else jnp.where(first, turned[i - 1], turned[i])
            out[i] = h[i] - scaled[i] * (u[i] - previous)
        return out

    def speed_step(h, u, low, high):
        turned = [pltpu.roll(x, 127, 1) for x in h]
        out = list(u)
        for i in range(low, high):
            following = turned[i] if i == 3 else jnp.where(last, turned[i + 1], turned[i])
            out[i] = u[i] - 0.9 * (following - h[i])
        return out

    for b in range(PARTS):
        edge = received[b, 4 * ROWS + 8 : 4 * ROWS + 16, :]
        beside[0:8, :] = edge
        beside[120:128, :] = edge
        turned = beside[...].T
        own = [received[b, pl.ds(j, ROWS, stride=4), :] for j in range(4)]
        h = [turned[:ROWS], own[0], own[2], turned[:ROWS]]
        u = [turned[ROWS:], own[1], own[3], turned[ROWS:]]
        h = height_step(h, u, 0)
        u = speed_step(h, u, 0, 4)
        h = height_step(h, u, 1)
        u = speed_step(h, u, 1, 3)
        for i, x in enumerate((h[1], h[2], u[1], u[2])):
            high, low = halves(x)
            for place, part_of in enumerate((high, low, high)):
                at = place * MEMBERS + b * ROWS
                state[at : at + ROWS, i * 128 : (i + 1) * 128] = part_of


def forecast(received, depth, left, right):
    return pl.pallas_call(
        forecast_kernel,
        out_shape=jax.ShapeDtypeStruct((3 * MEMBERS, STATE), bf16),
        in_specs=[VMEM] * 4,
        out_specs=VMEM,
        scratch_shapes=[pltpu.VMEM((128, 128), f32), pltpu.VMEM((24, 128), f32)],
        compiler_params=params(8),
        cost_estimate=cost(10**10),
        name="forecast",
    )(received, depth, left, right)


def pick_kernel(received, above, own, below, out, source, held, lists, bounds, sems, list_sem):
    for k in range(PARTS):
        lists[k] = received[k, 4 * ROWS : 4 * ROWS + 8, :].astype(jnp.int32)
    to_scalars = pltpu.make_async_copy(lists, bounds, list_sem)
    to_scalars.start()
    for n, part in enumerate((below, own, above)):
        for c in range(8):
            source[n * 8 + c] = part[:, c * 128 : (c + 1) * 128]
    to_scalars.wait()

    def send(k):
        return pltpu.make_async_copy(held.at[k], out.at[k], sems.at[k])

    def take(c, g, lane):
        return jnp.take_along_axis(source[c, g * 8 : g * 8 + 8, :], lane, axis=1)

    def one_list(k, carry):
        blocks = []
        for j in range(8):
            at = jnp.broadcast_to(lists[k, j : j + 1, :], (8, 128))
            lane, chunk = at & 127, at >> 7
            low, high = bounds[k, j, 0] >> 7, bounds[k, j, 127] >> 7
            blocks.append((j, lane, chunk, low, high))
            found = [take(low, g, lane) for g in range(ROWS // 8)]
            for d in range(1, DIRECT):
                here = chunk == low + d
                found = [jnp.where(here, take(low + d, g, lane), f) for g, f in enumerate(found)]
            for g in range(ROWS // 8):
                held[k, g * 8 : g * 8 + 8, j * 128 : (j + 1) * 128] = found[g]
        for j, lane, chunk, low, high in blocks:

            def more(c, carry):
                here = chunk == c
                for g in range(ROWS // 8):
                    at = (k, slice(g * 8, g * 8 + 8), slice(j * 128, (j + 1) * 128))
                    held[at] = jnp.where(here, take(c, g, lane), held[at])
                return carry

            lax.fori_loop(low + DIRECT, high + 1, more, 0)
        send(k).start()
        return carry

    lax.fori_loop(0, PARTS, one_list, 0)
    for k in range(PARTS):
        send(k).wait()


def pick(received, above, own, below):
    return pl.pallas_call(
        pick_kernel,
        out_shape=pltpu.HBM((PARTS, ROWS, SLOTS), f32),
        in_specs=[VMEM] * 4,
        out_specs=HBM,
        scratch_shapes=[
            pltpu.VMEM((24 + DIRECT, ROWS, 128), f32),
            pltpu.VMEM((PARTS, ROWS, SLOTS), f32),
            pltpu.VMEM((PARTS, 8, 128), jnp.int32),
            pltpu.SMEM((PARTS, 8, 128), jnp.int32),
            pltpu.SemaphoreType.DMA((PARTS,)),
            pltpu.SemaphoreType.DMA,
        ],
        compiler_params=params(16),
        cost_estimate=cost(10**12),
        name="pick",
    )(received, above, own, below)


def slots_kernel(rel, values, errors, cells, out):
    tile = lax.axis_index("tile")
    part = lax.axis_index("grp") * lax.axis_size("mem") + lax.axis_index("mem")
    center = tile * CELLS + part * CELLS_TILE + CELLS_TILE // 2
    listed = rel[...]
    at = jnp.maximum(listed, 0)
    lane = at & 127
    chunk = at >> 7
    value = jnp.zeros((8, 128), f32)
    error = jnp.ones((8, 128), f32)
    cell = jnp.zeros((8, 128), jnp.int32)
    for n in range(3):
        t = lax.rem(tile + (TILES - 1 + n), TILES)
        for j in range(8):
            here = chunk == n * 8 + j

            def found(ref):
                row = jnp.broadcast_to(ref[t, j : j + 1, :], (8, 128))
                return jnp.take_along_axis(row, lane, axis=1)

            value = jnp.where(here, found(values), value)
            error = jnp.where(here, found(errors), error)
            cell = jnp.where(here, found(cells), cell)
    distance = jnp.abs(cell - center)
    distance = jnp.minimum(distance, NCELLS - distance).astype(f32)
    weight = jnp.exp(-0.5 * (distance / LOC) ** 2) / (error * error)
    weight = jnp.where(listed >= 0, weight, 0.0)
    for j in range(8):
        out[0:1, j * 128 : (j + 1) * 128] = weight[j : j + 1, :]
        out[1:2, j * 128 : (j + 1) * 128] = value[j : j + 1, :]


def slots(rel, values, errors, cells):
    return pl.pallas_call(
        slots_kernel,
        out_shape=jax.ShapeDtypeStruct((8, SLOTS), f32),
        in_specs=[VMEM] * 4,
        out_specs=VMEM,
        compiler_params=params(8),
        name="slots",
    )(rel, values, errors, cells)


def analyse_kernel(
    predicted, slot_rows, state, gain_hi, gain_lo, analysis,
    left, right, z_left, z_right, y_right, slots_left, slots_right, held, result, sems,
):
    n = MEMBERS

    def put_left(ref, x, rows=slice(None)):
        high, low = halves(x)
        k = x.shape[1]
        ref[rows, :k] = high
        ref[rows, k : 2 * k] = high
        ref[rows, 2 * k :] = low

    def put_right(ref, x):
        high, low = halves(x)
        ref[:n] = high
        ref[n : 2 * n] = low
        ref[2 * n :] = high

    def times(a, b):
        return dot(a[...], b[...])

    y = predicted[...]
    weight = slot_rows[0:1, :]
    mean = jnp.sum(y, axis=0, keepdims=True) * (1.0 / MEMBERS)
    root_weight = jnp.sqrt(weight)
    spread = (y - mean) * root_weight
    departure = (slot_rows[1:2, :] - mean) * root_weight
    put_left(slots_left, spread, slice(0, n))
    put_left(slots_left, jnp.broadcast_to(departure, (16, SLOTS)), slice(n, n + 16))
    high, low = halves(spread)
    slots_right[:, :SLOTS] = high
    slots_right[:, SLOTS : 2 * SLOTS] = low
    slots_right[:, 2 * SLOTS :] = high
    on_diagonal = lax.broadcasted_iota(jnp.int32, (n, n), 0) == lax.broadcasted_iota(
        jnp.int32, (n, n), 1
    )

    def plus(x, d):
        return jnp.where(on_diagonal, x + d, x)

    products = dot_nt(slots_left[...], slots_right[...])
    a = plus(products[:n], MEMBERS - 1.0)
    innovation = products[n : n + 1]
    bound = jnp.max(jnp.sum(jnp.abs(a), axis=0, keepdims=True), axis=1, keepdims=True)
    approx = a / bound

    def two_steps(m):
        put_left(left, m)
        put_right(right, m)
        m2 = times(left, right)
        put_left(left, m2)
        put_right(right, plus(0.0625 * m2 - 0.5625 * m, 1.6875))
        return plus(times(left, right) - 2.4375 * m, 2.25)

    r = two_steps(approx)
    put_left(left, r)
    put_right(z_right, r)
    put_right(y_right, approx)
    put_right(y_right, times(left, y_right))
    r = two_steps(times(left, y_right))
    put_left(left, r)
    z = times(left, z_right)
    put_right(y_right, times(left, y_right))
    put_right(z_right, z)
    put_left(z_left, z)
    put_left(left, two_steps(times(z_left, y_right)))
    root = times(left, z_right) * lax.rsqrt(bound)
    once = jnp.sum(root * innovation, axis=1, keepdims=True)
    mean_weight = jnp.sum(root * once, axis=0, keepdims=True)
    moved = math.sqrt(MEMBERS - 1) * root + mean_weight
    gain = moved + (1.0 - jnp.sum(moved, axis=1, keepdims=True)) * (1.0 / MEMBERS)
    put_left(left, gain)
    held[0], held[1] = halves(gain)
    copies = [
        pltpu.make_async_copy(held.at[0], gain_hi, sems.at[0]),
        pltpu.make_async_copy(held.at[1], gain_lo, sems.at[1]),
        pltpu.make_async_copy(result, analysis, sems.at[2]),
    ]
    copies[0].start()
    copies[1].start()
    analysed = times(left, state)
    for row in range(4):
        at = (row % 2) * CELLS_TILE + (row // 2) * 128
        result[pl.ds(row, MEMBERS, stride=4), :] = analysed[:, at : at + 128]
    copies[2].start()
    for copy in copies:
        copy.wait()


def analyse(predicted, slot_rows, state):
    return pl.pallas_call(
        analyse_kernel,
        out_shape=(
            pltpu.HBM((MEMBERS, MEMBERS), bf16),
            pltpu.HBM((MEMBERS, MEMBERS), bf16),
            pltpu.HBM((MEMBERS * 4, 128), f32),
        ),
        in_specs=[VMEM, VMEM, VMEM],
        out_specs=(HBM, HBM, HBM),
        scratch_shapes=[
            pltpu.VMEM((MEMBERS, 3 * MEMBERS), bf16),
            pltpu.VMEM((3 * MEMBERS, MEMBERS), bf16),
            pltpu.VMEM((MEMBERS, 3 * MEMBERS), bf16),
            pltpu.VMEM((3 * MEMBERS, MEMBERS), bf16),
            pltpu.VMEM((3 * MEMBERS, MEMBERS), bf16),
            pltpu.VMEM((MEMBERS + 16, 3 * SLOTS), bf16),
            pltpu.VMEM((MEMBERS, 3 * SLOTS), bf16),
            pltpu.VMEM((2, MEMBERS, MEMBERS), bf16),
            pltpu.VMEM((MEMBERS * 4, 128), f32),
            pltpu.SemaphoreType.DMA((3,)),
        ],
        compiler_params=params(40),
        name="analyse",
    )(predicted, slot_rows, state)


def smooth_kernel(gain_hi, gain_lo, state, out):
    out[0] = product((gain_hi[...], gain_lo[...]), halves(state[0]))


def smooth(gain_hi, gain_lo, states):
    whole = pl.BlockSpec((MEMBERS, MEMBERS), lambda i: (0, 0))
    one = pl.BlockSpec((1, MEMBERS, STATE), lambda i: (i, 0, 0))
    return pl.pallas_call(
        smooth_kernel,
        out_shape=jax.ShapeDtypeStruct((LAGS, MEMBERS, STATE), f32),
        grid=(LAGS,),
        in_specs=[whole, whole, one],
        out_specs=one,
        compiler_params=params(24),
        cost_estimate=pl.CostEstimate(
            flops=2 * 3 * LAGS * MEMBERS**2 * STATE, bytes_accessed=8 * LAGS * MEMBERS * STATE, transcendentals=0
        ),
        name="smooth",
    )(gain_hi, gain_lo, states)


def assemble_kernel(parts, out, sems):
    copies = [pltpu.make_async_copy(parts.at[k], out.at[:, k], sems.at[k]) for k in range(PARTS)]
    for copy in copies:
        copy.start()
    for copy in copies:
        copy.wait()


def assemble(parts):
    return pl.pallas_call(
        assemble_kernel,
        out_shape=pltpu.HBM((ROWS, PARTS, 4, 128), f32),
        in_specs=[pl.BlockSpec(memory_space=pl.ANY)],
        out_specs=HBM,
        scratch_shapes=[pltpu.SemaphoreType.DMA((PARTS,))],
        compiler_params=params(8),
        name="assemble",
    )(parts)


def along_tiles(x, by):
    return lax.ppermute(x, "tile", [(i, (i + by) % TILES) for i in range(TILES)])


def far(x):
    return pltpu.with_memory_space_constraint(x, pltpu.HBM)


def exchange(x):
    return lax.all_to_all(x, GROUP, split_axis=0, concat_axis=0, tiled=True)


def per_device(
    current_state, lagged_states, water_depth, obs_cells, obs_values, obs_errors, tile_obs
):
    cur = current_state.reshape(ROWS, 2, CHUNKS, 128).transpose(0, 2, 1, 3)
    depth = water_depth.reshape(CHUNKS, 128)
    cur, to_right, to_left = edges(far(cur.reshape(ROWS * 2 * CHUNKS, 128)), far(depth))
    left = along_tiles(to_right, 1)
    right = along_tiles(to_left, -1)
    to_left, listed = lax.optimization_barrier((to_left, tile_obs[0, 0].reshape(8, 128)))
    ordered, payload, depth, cells = order(
        far(listed),
        cur.reshape(ROWS, PARTS, 4, 128),
        far(depth),
        far(obs_cells.reshape(TILES, 8, 128)),
    )
    payload = with_beside(payload, cur, left, right)
    received = exchange(payload.reshape(PARTS, ROWS * 4 + 16, 128))
    own = heights(cur, depth, left, right, cells)
    below = along_tiles(own, 1)
    above = along_tiles(own, -1)
    picked = pick(received, above, own, below)
    predicted = exchange(picked).reshape(MEMBERS, SLOTS)
    state = forecast(received, depth, left, right)
    slot_rows = slots(
        ordered,
        obs_values.reshape(TILES, 8, 128),
        obs_errors.reshape(TILES, 8, 128),
        obs_cells.reshape(TILES, 8, 128),
    )
    gain_hi, gain_lo, analysis = analyse(predicted, slot_rows, state)
    returned = exchange(analysis.reshape(PARTS, ROWS * 4, 128))
    older = smooth(gain_hi, gain_lo, lagged_states.reshape(LAGS, MEMBERS, STATE))
    analysed = assemble(returned.reshape(PARTS, ROWS, 4, 128))
    analysed = analysed.reshape(ROWS, CHUNKS, 2, 128).transpose(0, 2, 1, 3)
    return (
        analysed.reshape(ROWS, 2, CELLS),
        older.reshape(LAGS, 1, 1, MEMBERS, STATE),
    )


def solution(mesh):
    placed = (
        P(GROUP, None, "tile"),
        P(None, "tile", GROUP, None, None),
        P("tile"),
        P(),
        P(),
        P(),
        P("tile", GROUP, None),
    )
    return jax.shard_map(
        per_device,
        mesh=mesh,
        in_specs=placed,
        out_specs=(P(GROUP, None, "tile"), P(None, "tile", GROUP, None, None)),
        check_vma=False,
    )
```

```python
import functools
import math

import jax
import jax.numpy as jnp
from jax import lax
from jax.experimental import pallas as pl
from jax.experimental.pallas import tpu as pltpu
from jax.sharding import PartitionSpec as P

GROUP = ("grp", "mem")
PARTS = 8
ROWS = 64
MEMBERS = 512
CELLS = 2048
CHUNKS = 16
CELLS_TILE = 256
STATE = 512
OBS = 1024
SLOTS = 1024
NOBS = 32768
NCELLS = 65536
TILES = 32
LOC = 512
LAGS = 3
DIRECT = 3
f32 = jnp.float32
bf16 = jnp.bfloat16
VMEM = pl.BlockSpec(memory_space=pltpu.VMEM)
HBM = pl.BlockSpec(memory_space=pltpu.HBM)
SMEM = pl.BlockSpec(memory_space=pltpu.SMEM)


def params(mib):
    return pltpu.CompilerParams(vmem_limit_bytes=mib * 1024 * 1024)


def cost(flops):
    return pl.CostEstimate(flops=flops, bytes_accessed=2**20, transcendentals=0)


def halves(x):
    hi = x.astype(bf16)
    return hi, (x - hi.astype(f32)).astype(bf16)


def dot(a, b):
    return jnp.dot(a, b, preferred_element_type=f32)


def dot_nt(a, b):
    return lax.dot_general(a, b, (((1,), (1,)), ((), ())), preferred_element_type=f32)


def product(a, b):
    (ah, al), (bh, bl) = a, b
    return dot(ah, bh) + (dot(ah, bl) + dot(al, bh))


def edges_kernel(far_cur, far_depth, cur, to_right, to_left, depth, sems):
    arrivals = [
        pltpu.make_async_copy(far_cur, cur, sems.at[0]),
        pltpu.make_async_copy(far_depth, depth, sems.at[1]),
    ]
    for arrival in arrivals:
        arrival.start()
    low_half = lax.broadcasted_iota(jnp.int32, (ROWS, 128), 1) < ROWS
    end = CHUNKS - 1
    arrivals[1].wait()
    to_right[ROWS:, :] = jnp.broadcast_to(depth[end : end + 1, :], (8, 128))
    to_left[ROWS:, :] = jnp.broadcast_to(depth[0:1, :], (8, 128))
    arrivals[0].wait()

    def old(c, v):
        return cur[pl.ds(2 * c + v, ROWS, stride=2 * CHUNKS), :]

    to_right[:ROWS, :] = jnp.where(low_half, pltpu.roll(old(end, 0), ROWS, 1), old(end, 1))
    to_left[:ROWS, :] = jnp.where(low_half, old(0, 0), pltpu.roll(old(0, 1), ROWS, 1))


def edges(cur, depth):
    message = jax.ShapeDtypeStruct((ROWS + 8, 128), f32)
    return pl.pallas_call(
        edges_kernel,
        out_shape=(jax.ShapeDtypeStruct(cur.shape, f32), message, message),
        in_specs=[HBM, HBM],
        out_specs=(VMEM, VMEM, VMEM),
        scratch_shapes=[pltpu.VMEM((CHUNKS, 128), f32), pltpu.SemaphoreType.DMA((2,))],
        compiler_params=params(8),
        name="edges",
    )(cur, depth)


def order_kernel(
    far_list, by_part, far_depth, far_cells,
    ordered, payload, depth, cells, tile_list, row_list, row_place, filled, sems, sent,
):
    tile = lax.axis_index("tile")
    arrivals = [
        pltpu.make_async_copy(source, target, sems.at[n])
        for n, (source, target) in enumerate(
            ((far_list, tile_list), (far_cells.at[tile], cells), (far_depth, depth))
        )
    ]
    raw = [
        pltpu.make_async_copy(by_part.at[:, k], payload.at[k, pl.ds(0, ROWS)], sent.at[k])
        for k in range(PARTS)
    ]
    for copy in arrivals + raw:
        copy.start()
    arrivals[0].wait()
    listed = tile_list[...]
    rel = jnp.where(listed >= 0, (listed - (tile - 1) * OBS) & (NOBS - 1), -1)
    count = jnp.sum(jnp.where(rel >= 0, 1.0, 0.0))
    top = jnp.max(rel)
    for j in range(8):
        row_list[0:1, j * 128 : (j + 1) * 128] = rel[j : j + 1, :]
    row = row_list[0:1, :]
    chunks = 3 * OBS // 128

    def iota(shape, dim):
        return lax.broadcasted_iota(jnp.int32, shape, dim)

    def flags(x):
        return jnp.where(x, 1.0, 0.0).astype(bf16)

    in_chunk = flags((row >> 7) == iota((32, SLOTS), 0))
    in_lane = flags((row & 127) == iota((128, SLOTS), 0))
    present = dot_nt(in_chunk, in_lane).astype(bf16)
    before = dot(present, flags(iota((128, 128), 0) < iota((128, 128), 1)))
    totals = dot(present, jnp.ones((128, 128), bf16)).astype(bf16)
    place = before + dot(flags(iota((32, 32), 1) < iota((32, 32), 0)), totals)
    place = jnp.where(present.astype(f32) > 0.5, place, -1.0).astype(jnp.int32)
    for c in range(chunks):
        row_place[0:1, c * 128 : (c + 1) * 128] = place[c : c + 1, :]
    row = row_place[0:1, :]
    wide = 3 * OBS
    to_row = (row >> 7) == iota((8, wide), 0)
    number = iota((8, wide), 1)
    parts = jnp.concatenate(
        [jnp.where(to_row, number >> 7, 0), jnp.where(to_row, number & 127, 0)], axis=0
    )
    found = dot_nt(parts.astype(f32).astype(bf16), flags((row & 127) == iota((128, wide), 0)))
    found = (found[:8] * 128.0 + found[8:]).astype(jnp.int32)
    used = (iota((8, 128), 0) * 128 + iota((8, 128), 1)).astype(f32) < count
    ordered[...] = jnp.where(used, found, -1)
    whole = jnp.where(used, found, jnp.maximum(top, 0)).astype(f32)
    filled[0], filled[1] = whole[:4], whole[4:]
    lists = [
        pltpu.make_async_copy(filled, payload.at[k, pl.ds(ROWS, 2)], sent.at[PARTS + k])
        for k in range(PARTS)
    ]
    for copy in lists:
        copy.start()
    for copy in arrivals[1:] + raw + lists:
        copy.wait()
    cells[...] = cells[...] - tile * CELLS


def order(tile_list, parts, depth, cells):
    return pl.pallas_call(
        order_kernel,
        out_shape=(
            jax.ShapeDtypeStruct((8, 128), jnp.int32),
            pltpu.HBM((PARTS, ROWS + 4, 4, 128), f32),
            jax.ShapeDtypeStruct((CHUNKS, 128), f32),
            jax.ShapeDtypeStruct((8, 128), jnp.int32),
        ),
        in_specs=[HBM, VMEM, HBM, HBM],
        out_specs=(VMEM, HBM, VMEM, VMEM),
        scratch_shapes=[
            pltpu.VMEM((8, 128), jnp.int32),
            pltpu.VMEM((8, SLOTS), jnp.int32),
            pltpu.VMEM((8, 3 * OBS), jnp.int32),
            pltpu.VMEM((2, 4, 128), f32),
            pltpu.SemaphoreType.DMA((3,)),
            pltpu.SemaphoreType.DMA((2 * PARTS,)),
        ],
        cost_estimate=pl.CostEstimate(flops=0, bytes_accessed=100 * 2**20, transcendentals=0),
        compiler_params=params(12),
        name="order",
    )(tile_list, parts, depth, cells)


def chunk_with_halo(cur, left, right, c, v):
    if c < 0:
        x = left[:ROWS, :]
        return x if v else pltpu.roll(x, ROWS, 1)
    if c == CHUNKS:
        x = right[:ROWS, :]
        return pltpu.roll(x, ROWS, 1) if v else x
    return cur[pl.ds(2 * c + v, ROWS, stride=2 * CHUNKS), :]


def beside_kernel(_, cur, left, right, payload, rows, sems):
    def turned(c):
        pair = [chunk_with_halo(cur, left, right, c, v) for v in range(2)]
        return jnp.concatenate(pair, axis=0).T

    upper = lax.broadcasted_iota(jnp.int32, (8, 128), 0) < 4
    copies = []
    for k in range(PARTS):
        chosen = jnp.where(upper, turned(2 * k + 2)[:8], turned(2 * k - 1)[120:])
        rows[k, 0], rows[k, 1] = chosen[:4], chosen[4:]
        copies.append(
            pltpu.make_async_copy(rows.at[k], payload.at[k, pl.ds(ROWS + 2, 2)], sems.at[k])
        )
        copies[k].start()
    for copy in copies:
        copy.wait()


def with_beside(payload, cur, left, right):
    return pl.pallas_call(
        beside_kernel,
        out_shape=pltpu.HBM(payload.shape, f32),
        in_specs=[HBM, VMEM, VMEM, VMEM],
        out_specs=HBM,
        scratch_shapes=[pltpu.VMEM((PARTS, 2, 4, 128), f32), pltpu.SemaphoreType.DMA((PARTS,))],
        input_output_aliases={0: 0},
        compiler_params=params(8),
        cost_estimate=cost(1000),
        name="beside",
    )(payload, cur, left, right)


def take_lanes(chunk_of, chunks, index):
    at = jnp.broadcast_to(index, (8, 128))
    lane = at & 127
    chunk = at >> 7
    out = []
    for g in range(ROWS // 8):
        found = jnp.take_along_axis(chunk_of(g, 0), lane, axis=1)
        out.append(found)
    for c in range(1, chunks):
        here = chunk == c
        for g in range(ROWS // 8):
            out[g] = jnp.where(here, jnp.take_along_axis(chunk_of(g, c), lane, axis=1), out[g])
    return out


def heights_kernel(cur, depth, left, right, cells, own, hbuf, ubuf):
    lane = lax.broadcasted_iota(jnp.int32, (ROWS, 128), 1)
    first, last = lane == 0, lane == 127

    def old(c, v):
        return chunk_with_halo(cur, left, right, c, v)

    def scaled_depth(c):
        if c < 0:
            row = left[ROWS : ROWS + 1, :]
        elif c == CHUNKS:
            row = right[ROWS : ROWS + 1, :]
        else:
            row = depth[c : c + 1, :]
        return 0.9 * row

    def height_step(h_of, u_of):
        before = None
        for c in range(-1, CHUNKS + 1):
            u = u_of(c)
            turned = pltpu.roll(u, 1, 1)
            previous = turned if before is None else jnp.where(first, before, turned)
            before = turned
            hbuf[c + 1] = h_of(c) - scaled_depth(c) * (u - previous)

    height_step(lambda c: old(c, 0), lambda c: old(c, 1))
    turned = pltpu.roll(hbuf[0], 127, 1)
    for c in range(-1, CHUNKS + 1):
        after = pltpu.roll(hbuf[c + 2], 127, 1) if c < CHUNKS else turned
        following = jnp.where(last, after, turned)
        turned = after
        ubuf[c + 1] = old(c, 1) - 0.9 * (following - hbuf[c + 1])
    height_step(lambda c: hbuf[c + 1], lambda c: ubuf[c + 1])

    for j in range(OBS // 128):
        rows = take_lanes(lambda g, c: hbuf[c + 1, g * 8 : g * 8 + 8, :], CHUNKS, cells[j : j + 1, :])
        for g in range(ROWS // 8):
            own[g * 8 : g * 8 + 8, j * 128 : (j + 1) * 128] = rows[g]


def heights(cur, depth, left, right, cells):
    buffer = pltpu.VMEM((CHUNKS + 2, ROWS, 128), f32)
    return pl.pallas_call(
        heights_kernel,
        out_shape=jax.ShapeDtypeStruct((ROWS, OBS), f32),
        in_specs=[VMEM] * 5,
        out_specs=VMEM,
        scratch_shapes=[buffer, buffer],
        compiler_params=params(12),
        cost_estimate=cost(10**12),
        name="heights",
    )(cur, depth, left, right, cells)


def forecast_kernel(received, depth, left, right, state, beside, depths):
    part = lax.axis_index("grp") * lax.axis_size("mem") + lax.axis_index("mem")
    depths[0:1, :] = left[ROWS : ROWS + 1, :]
    depths[1 : CHUNKS + 1, :] = depth[...]
    depths[CHUNKS + 1 : CHUNKS + 2, :] = right[ROWS : ROWS + 1, :]
    scaled = [0.9 * depths[pl.ds(2 * part + i, 1), :] for i in range(4)]
    lane = lax.broadcasted_iota(jnp.int32, (ROWS, 128), 1)
    first, last = lane == 0, lane == 127
    beside[...] = jnp.zeros((128, 128), f32)

    def height_step(h, u, low):
        turned = [pltpu.roll(x, 1, 1) for x in u]
        out = list(h)
        for i in range(low, 4):
            previous = turned[i] if i == 0 else jnp.where(first, turned[i - 1], turned[i])
            out[i] = h[i] - scaled[i] * (u[i] - previous)
        return out

    def speed_step(h, u, low, high):
        turned = [pltpu.roll(x, 127, 1) for x in h]
        out = list(u)
        for i in range(low, high):
            following = turned[i] if i == 3 else jnp.where(last, turned[i + 1], turned[i])
            out[i] = u[i] - 0.9 * (following - h[i])
        return out

    for b in range(PARTS):
        edge = received[b, 4 * ROWS + 8 : 4 * ROWS + 16, :]
        beside[0:8, :] = edge
        beside[120:128, :] = edge
        turned = beside[...].T
        own = [received[b, pl.ds(j, ROWS, stride=4), :] for j in range(4)]
        h = [turned[:ROWS], own[0], own[2], turned[:ROWS]]
        u = [turned[ROWS:], own[1], own[3], turned[ROWS:]]
        h = height_step(h, u, 0)
        u = speed_step(h, u, 0, 4)
        h = height_step(h, u, 1)
        u = speed_step(h, u, 1, 3)
        for i, x in enumerate((h[1], h[2], u[1], u[2])):
            state[b * ROWS : (b + 1) * ROWS, i * 128 : (i + 1) * 128] = x


def forecast(received, depth, left, right):
    return pl.pallas_call(
        forecast_kernel,
        out_shape=jax.ShapeDtypeStruct((MEMBERS, STATE), f32),
        in_specs=[VMEM] * 4,
        out_specs=VMEM,
        scratch_shapes=[pltpu.VMEM((128, 128), f32), pltpu.VMEM((24, 128), f32)],
        compiler_params=params(8),
        cost_estimate=cost(10**10),
        name="forecast",
    )(received, depth, left, right)


def pick_kernel(received, above, own, below, out, source, held, lists, bounds, sems, list_sem):
    for k in range(PARTS):
        lists[k] = received[k, 4 * ROWS : 4 * ROWS + 8, :].astype(jnp.int32)
    to_scalars = pltpu.make_async_copy(lists, bounds, list_sem)
    to_scalars.start()
    for n, part in enumerate((below, own, above)):
        for c in range(8):
            source[n * 8 + c] = part[:, c * 128 : (c + 1) * 128]
    to_scalars.wait()

    def send(k):
        return pltpu.make_async_copy(held.at[k], out.at[k], sems.at[k])

    def take(c, g, lane):
        return jnp.take_along_axis(source[c, g * 8 : g * 8 + 8, :], lane, axis=1)

    def one_list(k, carry):
        blocks = []
        for j in range(8):
            at = jnp.broadcast_to(lists[k, j : j + 1, :], (8, 128))
            lane, chunk = at & 127, at >> 7
            low, high = bounds[k, j, 0] >> 7, bounds[k, j, 127] >> 7
            blocks.append((j, lane, chunk, low, high))
            found = [take(low, g, lane) for g in range(ROWS // 8)]
            for d in range(1, DIRECT):
                here = chunk == low + d
                found = [jnp.where(here, take(low + d, g, lane), f) for g, f in enumerate(found)]
            for g in range(ROWS // 8):
                held[k, g * 8 : g * 8 + 8, j * 128 : (j + 1) * 128] = found[g]
        for j, lane, chunk, low, high in blocks:

            def more(i, carry):
                c = low + DIRECT * i
                at = [
                    (k, slice(g * 8, g * 8 + 8), slice(j * 128, (j + 1) * 128))
                    for g in range(ROWS // 8)
                ]
                found = [held[place] for place in at]
                for d in range(DIRECT):
                    here = chunk == c + d
                    found = [jnp.where(here, take(c + d, g, lane), f) for g, f in enumerate(found)]
                for place, f in zip(at, found):
                    held[place] = f
                return carry

            lax.fori_loop(1, (high - low) // DIRECT + 1, more, 0)
        send(k).start()
        return carry

    lax.fori_loop(0, PARTS, one_list, 0)
    for k in range(PARTS):
        send(k).wait()


def pick(received, above, own, below):
    return pl.pallas_call(
        pick_kernel,
        out_shape=pltpu.HBM((PARTS, ROWS, SLOTS), f32),
        in_specs=[VMEM] * 4,
        out_specs=HBM,
        scratch_shapes=[
            pltpu.VMEM((24 + DIRECT, ROWS, 128), f32),
            pltpu.VMEM((PARTS, ROWS, SLOTS), f32),
            pltpu.VMEM((PARTS, 8, 128), jnp.int32),
            pltpu.SMEM((PARTS, 8, 128), jnp.int32),
            pltpu.SemaphoreType.DMA((PARTS,)),
            pltpu.SemaphoreType.DMA,
        ],
        compiler_params=params(16),
        cost_estimate=cost(10**12),
        name="pick",
    )(received, above, own, below)


def slots_kernel(rel, values, errors, cells, out):
    tile = lax.axis_index("tile")
    part = lax.axis_index("grp") * lax.axis_size("mem") + lax.axis_index("mem")
    center = tile * CELLS + part * CELLS_TILE + CELLS_TILE // 2
    listed = rel[...]
    at = jnp.maximum(listed, 0)
    lane = at & 127
    chunk = at >> 7
    value = jnp.zeros((8, 128), f32)
    error = jnp.ones((8, 128), f32)
    cell = jnp.zeros((8, 128), jnp.int32)
    for n in range(3):
        t = lax.rem(tile + (TILES - 1 + n), TILES)
        for j in range(8):
            here = chunk == n * 8 + j

            def found(ref):
                row = jnp.broadcast_to(ref[t, j : j + 1, :], (8, 128))
                return jnp.take_along_axis(row, lane, axis=1)

            value = jnp.where(here, found(values), value)
            error = jnp.where(here, found(errors), error)
            cell = jnp.where(here, found(cells), cell)
    distance = jnp.abs(cell - center)
    distance = jnp.minimum(distance, NCELLS - distance).astype(f32)
    weight = jnp.exp(-0.5 * (distance / LOC) ** 2) / (error * error)
    weight = jnp.where(listed >= 0, weight, 0.0)
    for j in range(8):
        out[0:1, j * 128 : (j + 1) * 128] = weight[j : j + 1, :]
        out[1:2, j * 128 : (j + 1) * 128] = value[j : j + 1, :]


def slots(rel, values, errors, cells):
    return pl.pallas_call(
        slots_kernel,
        out_shape=jax.ShapeDtypeStruct((8, SLOTS), f32),
        in_specs=[VMEM] * 4,
        out_specs=VMEM,
        compiler_params=params(8),
        name="slots",
    )(rel, values, errors, cells)


def analyse_kernel(
    predicted, slot_rows, state, gain_hi, gain_lo, analysis,
    left, right, z_left, z_right, y_right, slots_left, slots_right, held, result, sems,
):
    n = MEMBERS

    def put_left(ref, x, rows=slice(None)):
        high, low = halves(x)
        k = x.shape[1]
        ref[rows, :k] = high
        ref[rows, k : 2 * k] = high
        ref[rows, 2 * k :] = low

    def put_right(ref, x):
        high, low = halves(x)
        ref[:n] = high
        ref[n : 2 * n] = low
        ref[2 * n :] = high

    def times(a, b):
        return dot(a[...], b[...])

    y = predicted[...]
    weight = slot_rows[0:1, :]
    mean = jnp.sum(y, axis=0, keepdims=True) * (1.0 / MEMBERS)
    root_weight = jnp.sqrt(weight)
    spread = (y - mean) * root_weight
    departure = (slot_rows[1:2, :] - mean) * root_weight
    put_left(slots_left, spread, slice(0, n))
    put_left(slots_left, jnp.broadcast_to(departure, (16, SLOTS)), slice(n, n + 16))
    high, low = halves(spread)
    slots_right[:, :SLOTS] = high
    slots_right[:, SLOTS : 2 * SLOTS] = low
    slots_right[:, 2 * SLOTS :] = high
    on_diagonal = lax.broadcasted_iota(jnp.int32, (n, n), 0) == lax.broadcasted_iota(
        jnp.int32, (n, n), 1
    )

    def plus(x, d):
        return jnp.where(on_diagonal, x + d, x)

    products = dot_nt(slots_left[...], slots_right[...])
    a = plus(products[:n], MEMBERS - 1.0)
    innovation = products[n : n + 1]
    bound = jnp.max(jnp.sum(jnp.abs(a), axis=0, keepdims=True), axis=1, keepdims=True)
    approx = a / bound

    def two_steps(m):
        put_left(left, m)
        put_right(right, m)
        m2 = times(left, right)
        put_left(left, m2)
        put_right(right, plus(0.0625 * m2 - 0.5625 * m, 1.6875))
        return plus(times(left, right) - 2.4375 * m, 2.25)

    r = two_steps(approx)
    put_left(left, r)
    put_right(z_right, r)
    put_right(y_right, approx)
    put_right(y_right, times(left, y_right))
    r = two_steps(times(left, y_right))
    put_left(left, r)
    z = times(left, z_right)
    put_right(y_right, times(left, y_right))
    put_right(z_right, z)
    put_left(z_left, z)
    put_left(left, two_steps(times(z_left, y_right)))
    root = times(left, z_right) * lax.rsqrt(bound)
    once = jnp.sum(root * innovation, axis=1, keepdims=True)
    mean_weight = jnp.sum(root * once, axis=0, keepdims=True)
    moved = math.sqrt(MEMBERS - 1) * root + mean_weight
    gain = moved + (1.0 - jnp.sum(moved, axis=1, keepdims=True)) * (1.0 / MEMBERS)
    put_left(left, gain)
    held[0], held[1] = halves(gain)
    copies = [
        pltpu.make_async_copy(held.at[0], gain_hi, sems.at[0]),
        pltpu.make_async_copy(held.at[1], gain_lo, sems.at[1]),
        pltpu.make_async_copy(result, analysis, sems.at[2]),
    ]
    copies[0].start()
    copies[1].start()
    put_right(right, state[...])
    analysed = times(left, right)
    for row in range(4):
        at = (row % 2) * CELLS_TILE + (row // 2) * 128
        result[pl.ds(row, MEMBERS, stride=4), :] = analysed[:, at : at + 128]
    copies[2].start()
    for copy in copies:
        copy.wait()


def analyse(predicted, slot_rows, state):
    return pl.pallas_call(
        analyse_kernel,
        out_shape=(
            pltpu.HBM((MEMBERS, MEMBERS), bf16),
            pltpu.HBM((MEMBERS, MEMBERS), bf16),
            pltpu.HBM((MEMBERS * 4, 128), f32),
        ),
        in_specs=[VMEM, VMEM, VMEM],
        out_specs=(HBM, HBM, HBM),
        scratch_shapes=[
            pltpu.VMEM((MEMBERS, 3 * MEMBERS), bf16),
            pltpu.VMEM((3 * MEMBERS, MEMBERS), bf16),
            pltpu.VMEM((MEMBERS, 3 * MEMBERS), bf16),
            pltpu.VMEM((3 * MEMBERS, MEMBERS), bf16),
            pltpu.VMEM((3 * MEMBERS, MEMBERS), bf16),
            pltpu.VMEM((MEMBERS + 16, 3 * SLOTS), bf16),
            pltpu.VMEM((MEMBERS, 3 * SLOTS), bf16),
            pltpu.VMEM((2, MEMBERS, MEMBERS), bf16),
            pltpu.VMEM((MEMBERS * 4, 128), f32),
            pltpu.SemaphoreType.DMA((3,)),
        ],
        compiler_params=params(40),
        name="analyse",
    )(predicted, slot_rows, state)


def smooth_kernel(gain_hi, gain_lo, state, out):
    out[0] = product((gain_hi[...], gain_lo[...]), halves(state[0]))


def smooth(gain_hi, gain_lo, states):
    whole = pl.BlockSpec((MEMBERS, MEMBERS), lambda i: (0, 0))
    one = pl.BlockSpec((1, MEMBERS, STATE), lambda i: (i, 0, 0))
    return pl.pallas_call(
        smooth_kernel,
        out_shape=jax.ShapeDtypeStruct((LAGS, MEMBERS, STATE), f32),
        grid=(LAGS,),
        in_specs=[whole, whole, one],
        out_specs=one,
        compiler_params=params(24),
        cost_estimate=pl.CostEstimate(
            flops=2 * 3 * LAGS * MEMBERS**2 * STATE, bytes_accessed=8 * LAGS * MEMBERS * STATE, transcendentals=0
        ),
        name="smooth",
    )(gain_hi, gain_lo, states)


def assemble_kernel(parts, out, sems):
    copies = [pltpu.make_async_copy(parts.at[k], out.at[:, k], sems.at[k]) for k in range(PARTS)]
    for copy in copies:
        copy.start()
    for copy in copies:
        copy.wait()


def assemble(parts):
    return pl.pallas_call(
        assemble_kernel,
        out_shape=pltpu.HBM((ROWS, PARTS, 4, 128), f32),
        in_specs=[pl.BlockSpec(memory_space=pl.ANY)],
        out_specs=HBM,
        scratch_shapes=[pltpu.SemaphoreType.DMA((PARTS,))],
        compiler_params=params(8),
        name="assemble",
    )(parts)


def along_tiles(x, by):
    return lax.ppermute(x, "tile", [(i, (i + by) % TILES) for i in range(TILES)])


def far(x):
    return pltpu.with_memory_space_constraint(x, pltpu.HBM)


def exchange(x):
    return lax.all_to_all(x, GROUP, split_axis=0, concat_axis=0, tiled=True)


def per_device(
    current_state, lagged_states, water_depth, obs_cells, obs_values, obs_errors, tile_obs
):
    cur = current_state.reshape(ROWS, 2, CHUNKS, 128).transpose(0, 2, 1, 3)
    depth = water_depth.reshape(CHUNKS, 128)
    cur, to_right, to_left = edges(far(cur.reshape(ROWS * 2 * CHUNKS, 128)), far(depth))
    left = along_tiles(to_right, 1)
    right = along_tiles(to_left, -1)
    to_left, listed = lax.optimization_barrier((to_left, tile_obs[0, 0].reshape(8, 128)))
    ordered, payload, depth, cells = order(
        far(listed),
        cur.reshape(ROWS, PARTS, 4, 128),
        far(depth),
        far(obs_cells.reshape(TILES, 8, 128)),
    )
    payload = with_beside(payload, cur, left, right)
    received = exchange(payload.reshape(PARTS, ROWS * 4 + 16, 128))
    own = heights(cur, depth, left, right, cells)
    below = along_tiles(own, 1)
    above = along_tiles(own, -1)
    picked = pick(received, above, own, below)
    predicted = exchange(picked).reshape(MEMBERS, SLOTS)
    state = forecast(received, depth, left, right)
    slot_rows = slots(
        ordered,
        obs_values.reshape(TILES, 8, 128),
        obs_errors.reshape(TILES, 8, 128),
        obs_cells.reshape(TILES, 8, 128),
    )
    gain_hi, gain_lo, analysis = analyse(predicted, slot_rows, state)
    returned = exchange(analysis.reshape(PARTS, ROWS * 4, 128))
    older = smooth(gain_hi, gain_lo, lagged_states.reshape(LAGS, MEMBERS, STATE))
    analysed = assemble(returned.reshape(PARTS, ROWS, 4, 128))
    analysed = analysed.reshape(ROWS, CHUNKS, 2, 128).transpose(0, 2, 1, 3)
    return (
        analysed.reshape(ROWS, 2, CELLS),
        older.reshape(LAGS, 1, 1, MEMBERS, STATE),
    )


def solution(mesh):
    placed = (
        P(GROUP, None, "tile"),
        P(None, "tile", GROUP, None, None),
        P("tile"),
        P(),
        P(),
        P(),
        P("tile", GROUP, None),
    )
    return jax.shard_map(
        per_device,
        mesh=mesh,
        in_specs=placed,
        out_specs=(P(GROUP, None, "tile"), P(None, "tile", GROUP, None, None)),
        check_vma=False,
    )
```

```python
import functools
import math

import jax
import jax.numpy as jnp
from jax import lax
from jax.experimental import pallas as pl
from jax.experimental.pallas import tpu as pltpu
from jax.sharding import PartitionSpec as P

GROUP = ("grp", "mem")
PARTS = 8
ROWS = 64
MEMBERS = 512
CELLS = 2048
CHUNKS = 16
CELLS_TILE = 256
STATE = 512
OBS = 1024
SLOTS = 1024
NOBS = 32768
NCELLS = 65536
TILES = 32
LOC = 512
LAGS = 3
DIRECT = 3
OUTER = (0, PARTS - 1)
INNER = range(1, PARTS - 1)
f32 = jnp.float32
bf16 = jnp.bfloat16
VMEM = pl.BlockSpec(memory_space=pltpu.VMEM)
HBM = pl.BlockSpec(memory_space=pltpu.HBM)
SMEM = pl.BlockSpec(memory_space=pltpu.SMEM)


def params(mib):
    return pltpu.CompilerParams(vmem_limit_bytes=mib * 1024 * 1024)


def cost(flops):
    return pl.CostEstimate(flops=flops, bytes_accessed=2**20, transcendentals=0)


def halves(x):
    hi = x.astype(bf16)
    return hi, (x - hi.astype(f32)).astype(bf16)


def dot(a, b):
    return jnp.dot(a, b, preferred_element_type=f32)


def dot_nt(a, b):
    return lax.dot_general(a, b, (((1,), (1,)), ((), ())), preferred_element_type=f32)


def product(a, b):
    (ah, al), (bh, bl) = a, b
    return dot(ah, bh) + (dot(ah, bl) + dot(al, bh))


def edges_kernel(far_cur, far_depth, cur, to_right, to_left, depth, sems):
    arrivals = [
        pltpu.make_async_copy(far_cur, cur, sems.at[0]),
        pltpu.make_async_copy(far_depth, depth, sems.at[1]),
    ]
    for arrival in arrivals:
        arrival.start()
    low_half = lax.broadcasted_iota(jnp.int32, (ROWS, 128), 1) < ROWS
    end = CHUNKS - 1
    arrivals[1].wait()
    to_right[ROWS:, :] = jnp.broadcast_to(depth[end : end + 1, :], (8, 128))
    to_left[ROWS:, :] = jnp.broadcast_to(depth[0:1, :], (8, 128))
    arrivals[0].wait()

    def old(c, v):
        return cur[pl.ds(2 * c + v, ROWS, stride=2 * CHUNKS), :]

    to_right[:ROWS, :] = jnp.where(low_half, pltpu.roll(old(end, 0), ROWS, 1), old(end, 1))
    to_left[:ROWS, :] = jnp.where(low_half, old(0, 0), pltpu.roll(old(0, 1), ROWS, 1))


def edges(cur, depth):
    message = jax.ShapeDtypeStruct((ROWS + 8, 128), f32)
    return pl.pallas_call(
        edges_kernel,
        out_shape=(jax.ShapeDtypeStruct(cur.shape, f32), message, message),
        in_specs=[HBM, HBM],
        out_specs=(VMEM, VMEM, VMEM),
        scratch_shapes=[pltpu.VMEM((CHUNKS, 128), f32), pltpu.SemaphoreType.DMA((2,))],
        compiler_params=params(8),
        name="edges",
    )(cur, depth)


def order_kernel(
    far_list, by_part, cur, far_depth, far_cells,
    ordered, payload, depth, cells, tile_list, row_list, row_place, filled, rows, sems, sent,
):
    tile = lax.axis_index("tile")
    arrivals = [
        pltpu.make_async_copy(source, target, sems.at[n])
        for n, (source, target) in enumerate(
            ((far_list, tile_list), (far_cells.at[tile], cells), (far_depth, depth))
        )
    ]
    raw = [
        pltpu.make_async_copy(by_part.at[:, k], payload.at[k, pl.ds(0, ROWS)], sent.at[k])
        for k in range(PARTS)
    ]
    for copy in arrivals + raw:
        copy.start()
    beside = [put_beside(k, cur, None, None, payload, rows, sent.at[2 * PARTS + k]) for k in INNER]
    arrivals[0].wait()
    listed = tile_list[...]
    rel = jnp.where(listed >= 0, (listed - (tile - 1) * OBS) & (NOBS - 1), -1)
    count = jnp.sum(jnp.where(rel >= 0, 1.0, 0.0))
    top = jnp.max(rel)
    for j in range(8):
        row_list[0:1, j * 128 : (j + 1) * 128] = rel[j : j + 1, :]
    row = row_list[0:1, :]
    chunks = 3 * OBS // 128

    def iota(shape, dim):
        return lax.broadcasted_iota(jnp.int32, shape, dim)

    def flags(x):
        return jnp.where(x, 1.0, 0.0).astype(bf16)

    in_chunk = flags((row >> 7) == iota((32, SLOTS), 0))
    in_lane = flags((row & 127) == iota((128, SLOTS), 0))
    present = dot_nt(in_chunk, in_lane).astype(bf16)
    before = dot(present, flags(iota((128, 128), 0) < iota((128, 128), 1)))
    totals = dot(present, jnp.ones((128, 128), bf16)).astype(bf16)
    place = before + dot(flags(iota((32, 32), 1) < iota((32, 32), 0)), totals)
    place = jnp.where(present.astype(f32) > 0.5, place, -1.0).astype(jnp.int32)
    for c in range(chunks):
        row_place[0:1, c * 128 : (c + 1) * 128] = place[c : c + 1, :]
    row = row_place[0:1, :]
    wide = 3 * OBS
    to_row = (row >> 7) == iota((8, wide), 0)
    number = iota((8, wide), 1)
    parts = jnp.concatenate(
        [jnp.where(to_row, number >> 7, 0), jnp.where(to_row, number & 127, 0)], axis=0
    )
    found = dot_nt(parts.astype(f32).astype(bf16), flags((row & 127) == iota((128, wide), 0)))
    found = (found[:8] * 128.0 + found[8:]).astype(jnp.int32)
    used = (iota((8, 128), 0) * 128 + iota((8, 128), 1)).astype(f32) < count
    ordered[...] = jnp.where(used, found, -1)
    whole = jnp.where(used, found, jnp.maximum(top, 0)).astype(f32)
    filled[0], filled[1] = whole[:4], whole[4:]
    lists = [
        pltpu.make_async_copy(filled, payload.at[k, pl.ds(ROWS, 2)], sent.at[PARTS + k])
        for k in range(PARTS)
    ]
    for copy in lists:
        copy.start()
    for copy in arrivals[1:] + raw + lists + beside:
        copy.wait()
    cells[...] = cells[...] - tile * CELLS


def order(tile_list, parts, cur, depth, cells):
    return pl.pallas_call(
        order_kernel,
        out_shape=(
            jax.ShapeDtypeStruct((8, 128), jnp.int32),
            pltpu.HBM((PARTS, ROWS + 4, 4, 128), f32),
            jax.ShapeDtypeStruct((CHUNKS, 128), f32),
            jax.ShapeDtypeStruct((8, 128), jnp.int32),
        ),
        in_specs=[HBM, VMEM, VMEM, HBM, HBM],
        out_specs=(VMEM, HBM, VMEM, VMEM),
        scratch_shapes=[
            pltpu.VMEM((8, 128), jnp.int32),
            pltpu.VMEM((8, SLOTS), jnp.int32),
            pltpu.VMEM((8, 3 * OBS), jnp.int32),
            pltpu.VMEM((2, 4, 128), f32),
            pltpu.VMEM((PARTS, 2, 4, 128), f32),
            pltpu.SemaphoreType.DMA((3,)),
            pltpu.SemaphoreType.DMA((3 * PARTS,)),
        ],
        cost_estimate=pl.CostEstimate(flops=0, bytes_accessed=100 * 2**20, transcendentals=0),
        compiler_params=params(12),
        name="order",
    )(tile_list, parts, cur, depth, cells)


def chunk_with_halo(cur, left, right, c, v):
    if c < 0:
        x = left[:ROWS, :]
        return x if v else pltpu.roll(x, ROWS, 1)
    if c == CHUNKS:
        x = right[:ROWS, :]
        return pltpu.roll(x, ROWS, 1) if v else x
    return cur[pl.ds(2 * c + v, ROWS, stride=2 * CHUNKS), :]


def put_beside(k, cur, left, right, payload, rows, sem):
    def turned(c):
        pair = [chunk_with_halo(cur, left, right, c, v) for v in range(2)]
        return jnp.concatenate(pair, axis=0).T

    rows[k, 0] = turned(2 * k + 2)[:4]
    rows[k, 1] = turned(2 * k - 1)[124:]
    copy = pltpu.make_async_copy(rows.at[k], payload.at[k, pl.ds(ROWS + 2, 2)], sem)
    copy.start()
    return copy


def beside_kernel(_, cur, left, right, payload, rows, sems):
    for copy in [put_beside(k, cur, left, right, payload, rows, sems.at[k]) for k in OUTER]:
        copy.wait()


def with_beside(payload, cur, left, right):
    return pl.pallas_call(
        beside_kernel,
        out_shape=pltpu.HBM(payload.shape, f32),
        in_specs=[HBM, VMEM, VMEM, VMEM],
        out_specs=HBM,
        scratch_shapes=[pltpu.VMEM((PARTS, 2, 4, 128), f32), pltpu.SemaphoreType.DMA((PARTS,))],
        input_output_aliases={0: 0},
        compiler_params=params(8),
        cost_estimate=cost(1000),
        name="beside",
    )(payload, cur, left, right)


def take_lanes(chunk_of, chunks, index):
    at = jnp.broadcast_to(index, (8, 128))
    lane = at & 127
    chunk = at >> 7
    out = []
    for g in range(ROWS // 8):
        found = jnp.take_along_axis(chunk_of(g, 0), lane, axis=1)
        out.append(found)
    for c in range(1, chunks):
        here = chunk == c
        for g in range(ROWS // 8):
            out[g] = jnp.where(here, jnp.take_along_axis(chunk_of(g, c), lane, axis=1), out[g])
    return out


def heights_kernel(cur, depth, left, right, cells, own, hbuf, ubuf):
    lane = lax.broadcasted_iota(jnp.int32, (ROWS, 128), 1)
    first, last = lane == 0, lane == 127

    def old(c, v):
        return chunk_with_halo(cur, left, right, c, v)

    def scaled_depth(c):
        if c < 0:
            row = left[ROWS : ROWS + 1, :]
        elif c == CHUNKS:
            row = right[ROWS : ROWS + 1, :]
        else:
            row = depth[c : c + 1, :]
        return 0.9 * row

    def height_step(h_of, u_of):
        before = None
        for c in range(-1, CHUNKS + 1):
            u = u_of(c)
            turned = pltpu.roll(u, 1, 1)
            previous = turned if before is None else jnp.where(first, before, turned)
            before = turned
            hbuf[c + 1] = h_of(c) - scaled_depth(c) * (u - previous)

    height_step(lambda c: old(c, 0), lambda c: old(c, 1))
    turned = pltpu.roll(hbuf[0], 127, 1)
    for c in range(-1, CHUNKS + 1):
        after = pltpu.roll(hbuf[c + 2], 127, 1) if c < CHUNKS else turned
        following = jnp.where(last, after, turned)
        turned = after
        ubuf[c + 1] = old(c, 1) - 0.9 * (following - hbuf[c + 1])
    height_step(lambda c: hbuf[c + 1], lambda c: ubuf[c + 1])

    for j in range(OBS // 128):
        rows = take_lanes(lambda g, c: hbuf[c + 1, g * 8 : g * 8 + 8, :], CHUNKS, cells[j : j + 1, :])
        for g in range(ROWS // 8):
            own[g * 8 : g * 8 + 8, j * 128 : (j + 1) * 128] = rows[g]


def heights(cur, depth, left, right, cells):
    buffer = pltpu.VMEM((CHUNKS + 2, ROWS, 128), f32)
    return pl.pallas_call(
        heights_kernel,
        out_shape=jax.ShapeDtypeStruct((ROWS, OBS), f32),
        in_specs=[VMEM] * 5,
        out_specs=VMEM,
        scratch_shapes=[buffer, buffer],
        compiler_params=params(12),
        cost_estimate=cost(10**12),
        name="heights",
    )(cur, depth, left, right, cells)


def forecast_kernel(received, depth, left, right, state, beside, depths):
    part = lax.axis_index("grp") * lax.axis_size("mem") + lax.axis_index("mem")
    depths[0:1, :] = left[ROWS : ROWS + 1, :]
    depths[1 : CHUNKS + 1, :] = depth[...]
    depths[CHUNKS + 1 : CHUNKS + 2, :] = right[ROWS : ROWS + 1, :]
    scaled = [0.9 * depths[pl.ds(2 * part + i, 1), :] for i in range(4)]
    lane = lax.broadcasted_iota(jnp.int32, (ROWS, 128), 1)
    first, last = lane == 0, lane == 127
    beside[...] = jnp.zeros((128, 128), f32)

    def height_step(h, u, low):
        turned = [pltpu.roll(x, 1, 1) for x in u]
        out = list(h)
        for i in range(low, 4):
            previous = turned[i] if i == 0 else jnp.where(first, turned[i - 1], turned[i])
            out[i] = h[i] - scaled[i] * (u[i] - previous)
        return out

    def speed_step(h, u, low, high):
        turned = [pltpu.roll(x, 127, 1) for x in h]
        out = list(u)
        for i in range(low, high):
            following = turned[i] if i == 3 else jnp.where(last, turned[i + 1], turned[i])
            out[i] = u[i] - 0.9 * (following - h[i])
        return out

    for b in range(PARTS):
        edge = received[b, 4 * ROWS + 8 : 4 * ROWS + 16, :]
        beside[0:8, :] = edge
        beside[120:128, :] = edge
        turned = beside[...].T
        own = [received[b, pl.ds(j, ROWS, stride=4), :] for j in range(4)]
        h = [turned[:ROWS], own[0], own[2], turned[:ROWS]]
        u = [turned[ROWS:], own[1], own[3], turned[ROWS:]]
        h = height_step(h, u, 0)
        u = speed_step(h, u, 0, 4)
        h = height_step(h, u, 1)
        u = speed_step(h, u, 1, 3)
        for i, x in enumerate((h[1], h[2], u[1], u[2])):
            state[b * ROWS : (b + 1) * ROWS, i * 128 : (i + 1) * 128] = x


def forecast(received, depth, left, right):
    return pl.pallas_call(
        forecast_kernel,
        out_shape=jax.ShapeDtypeStruct((MEMBERS, STATE), f32),
        in_specs=[VMEM] * 4,
        out_specs=VMEM,
        scratch_shapes=[pltpu.VMEM((128, 128), f32), pltpu.VMEM((24, 128), f32)],
        compiler_params=params(8),
        cost_estimate=cost(10**10),
        name="forecast",
    )(received, depth, left, right)


def pick_kernel(received, below, own, above, out, source, held, lists, bounds, sems, list_sem):
    for k in range(PARTS):
        lists[k] = received[k, 4 * ROWS : 4 * ROWS + 8, :].astype(jnp.int32)
    to_scalars = pltpu.make_async_copy(lists, bounds, list_sem)
    to_scalars.start()
    for n, part in enumerate((below, own, above)):
        for c in range(8):
            source[n * 8 + c] = part[:, c * 128 : (c + 1) * 128]
    to_scalars.wait()

    def send(k):
        return pltpu.make_async_copy(held.at[k], out.at[k], sems.at[k])

    def take(c, g, lane):
        return jnp.take_along_axis(source[c, g * 8 : g * 8 + 8, :], lane, axis=1)

    def one_list(k, carry):
        blocks = []
        for j in range(8):
            at = jnp.broadcast_to(lists[k, j : j + 1, :], (8, 128))
            lane, chunk = at & 127, at >> 7
            low, high = bounds[k, j, 0] >> 7, bounds[k, j, 127] >> 7
            blocks.append((j, lane, chunk, low, high))
            found = [take(low, g, lane) for g in range(ROWS // 8)]
            for d in range(1, DIRECT):
                here = chunk == low + d
                found = [jnp.where(here, take(low + d, g, lane), f) for g, f in enumerate(found)]
            for g in range(ROWS // 8):
                held[k, g * 8 : g * 8 + 8, j * 128 : (j + 1) * 128] = found[g]
        for j, lane, chunk, low, high in blocks:

            def more(i, carry):
                c = low + DIRECT * i
                at = [
                    (k, slice(g * 8, g * 8 + 8), slice(j * 128, (j + 1) * 128))
                    for g in range(ROWS // 8)
                ]
                found = [held[place] for place in at]
                for d in range(DIRECT):
                    here = chunk == c + d
                    found = [jnp.where(here, take(c + d, g, lane), f) for g, f in enumerate(found)]
                for place, f in zip(at, found):
                    held[place] = f
                return carry

            lax.fori_loop(1, (high - low) // DIRECT + 1, more, 0)
        send(k).start()
        return carry

    lax.fori_loop(0, PARTS, one_list, 0)
    for k in range(PARTS):
        send(k).wait()


def pick(received, below, own, above):
    return pl.pallas_call(
        pick_kernel,
        out_shape=pltpu.HBM((PARTS, ROWS, SLOTS), f32),
        in_specs=[VMEM] * 4,
        out_specs=HBM,
        scratch_shapes=[
            pltpu.VMEM((24 + DIRECT, ROWS, 128), f32),
            pltpu.VMEM((PARTS, ROWS, SLOTS), f32),
            pltpu.VMEM((PARTS, 8, 128), jnp.int32),
            pltpu.SMEM((PARTS, 8, 128), jnp.int32),
            pltpu.SemaphoreType.DMA((PARTS,)),
            pltpu.SemaphoreType.DMA,
        ],
        compiler_params=params(16),
        cost_estimate=cost(10**12),
        name="pick",
    )(received, below, own, above)


def slots_kernel(rel, values, errors, cells, out):
    tile = lax.axis_index("tile")
    part = lax.axis_index("grp") * lax.axis_size("mem") + lax.axis_index("mem")
    center = tile * CELLS + part * CELLS_TILE + CELLS_TILE // 2
    listed = rel[...]
    at = jnp.maximum(listed, 0)
    lane = at & 127
    chunk = at >> 7
    value = jnp.zeros((8, 128), f32)
    error = jnp.ones((8, 128), f32)
    cell = jnp.zeros((8, 128), jnp.int32)
    for n in range(3):
        t = lax.rem(tile + (TILES - 1 + n), TILES)
        for j in range(8):
            here = chunk == n * 8 + j

            def found(ref):
                row = jnp.broadcast_to(ref[t, j : j + 1, :], (8, 128))
                return jnp.take_along_axis(row, lane, axis=1)

            value = jnp.where(here, found(values), value)
            error = jnp.where(here, found(errors), error)
            cell = jnp.where(here, found(cells), cell)
    distance = jnp.abs(cell - center)
    distance = jnp.minimum(distance, NCELLS - distance).astype(f32)
    weight = jnp.exp(-0.5 * (distance / LOC) ** 2) / (error * error)
    weight = jnp.where(listed >= 0, weight, 0.0)
    for j in range(8):
        out[0:1, j * 128 : (j + 1) * 128] = weight[j : j + 1, :]
        out[1:2, j * 128 : (j + 1) * 128] = value[j : j + 1, :]


def slots(rel, values, errors, cells):
    return pl.pallas_call(
        slots_kernel,
        out_shape=jax.ShapeDtypeStruct((8, SLOTS), f32),
        in_specs=[VMEM] * 4,
        out_specs=VMEM,
        compiler_params=params(8),
        name="slots",
    )(rel, values, errors, cells)


def analyse_kernel(
    predicted, slot_rows, state, gain_hi, gain_lo, analysis,
    left, right, z_left, z_right, y_right, slots_left, slots_right, held, result, sems,
):
    n = MEMBERS

    def put_left(ref, x, rows=slice(None)):
        high, low = halves(x)
        k = x.shape[1]
        ref[rows, :k] = high
        ref[rows, k : 2 * k] = high
        ref[rows, 2 * k :] = low

    def put_right(ref, x):
        high, low = halves(x)
        ref[:n] = high
        ref[n : 2 * n] = low
        ref[2 * n :] = high

    def times(a, b):
        return dot(a[...], b[...])

    y = predicted[...]
    weight = slot_rows[0:1, :]
    mean = jnp.sum(y, axis=0, keepdims=True) * (1.0 / MEMBERS)
    root_weight = jnp.sqrt(weight)
    spread = (y - mean) * root_weight
    departure = (slot_rows[1:2, :] - mean) * root_weight
    put_left(slots_left, spread, slice(0, n))
    put_left(slots_left, jnp.broadcast_to(departure, (16, SLOTS)), slice(n, n + 16))
    high, low = halves(spread)
    slots_right[:, :SLOTS] = high
    slots_right[:, SLOTS : 2 * SLOTS] = low
    slots_right[:, 2 * SLOTS :] = high
    on_diagonal = lax.broadcasted_iota(jnp.int32, (n, n), 0) == lax.broadcasted_iota(
        jnp.int32, (n, n), 1
    )

    def plus(x, d):
        return jnp.where(on_diagonal, x + d, x)

    products = dot_nt(slots_left[...], slots_right[...])
    a = plus(products[:n], MEMBERS - 1.0)
    innovation = products[n : n + 1]
    bound = jnp.max(jnp.sum(jnp.abs(a), axis=0, keepdims=True), axis=1, keepdims=True)
    approx = a / bound

    def two_steps(m):
        put_left(left, m)
        put_right(right, m)
        m2 = times(left, right)
        put_left(left, m2)
        put_right(right, plus(0.0625 * m2 - 0.5625 * m, 1.6875))
        return plus(times(left, right) - 2.4375 * m, 2.25)

    r = two_steps(approx)
    put_left(left, r)
    put_right(z_right, r)
    put_right(y_right, approx)
    put_right(y_right, times(left, y_right))
    r = two_steps(times(left, y_right))
    put_left(left, r)
    z = times(left, z_right)
    put_right(y_right, times(left, y_right))
    put_right(z_right, z)
    put_left(z_left, z)
    put_left(left, two_steps(times(z_left, y_right)))
    root = times(left, z_right) * lax.rsqrt(bound)
    once = jnp.sum(root * innovation, axis=1, keepdims=True)
    mean_weight = jnp.sum(root * once, axis=0, keepdims=True)
    moved = math.sqrt(MEMBERS - 1) * root + mean_weight
    gain = moved + (1.0 - jnp.sum(moved, axis=1, keepdims=True)) * (1.0 / MEMBERS)
    put_left(left, gain)
    held[0], held[1] = halves(gain)
    copies = [
        pltpu.make_async_copy(held.at[0], gain_hi, sems.at[0]),
        pltpu.make_async_copy(held.at[1], gain_lo, sems.at[1]),
        pltpu.make_async_copy(result, analysis, sems.at[2]),
    ]
    copies[0].start()
    copies[1].start()
    put_right(right, state[...])
    analysed = times(left, right)
    for row in range(4):
        at = (row % 2) * CELLS_TILE + (row // 2) * 128
        result[pl.ds(row, MEMBERS, stride=4), :] = analysed[:, at : at + 128]
    copies[2].start()
    for copy in copies:
        copy.wait()


def analyse(predicted, slot_rows, state):
    return pl.pallas_call(
        analyse_kernel,
        out_shape=(
            pltpu.HBM((MEMBERS, MEMBERS), bf16),
            pltpu.HBM((MEMBERS, MEMBERS), bf16),
            pltpu.HBM((MEMBERS * 4, 128), f32),
        ),
        in_specs=[VMEM, VMEM, VMEM],
        out_specs=(HBM, HBM, HBM),
        scratch_shapes=[
            pltpu.VMEM((MEMBERS, 3 * MEMBERS), bf16),
            pltpu.VMEM((3 * MEMBERS, MEMBERS), bf16),
            pltpu.VMEM((MEMBERS, 3 * MEMBERS), bf16),
            pltpu.VMEM((3 * MEMBERS, MEMBERS), bf16),
            pltpu.VMEM((3 * MEMBERS, MEMBERS), bf16),
            pltpu.VMEM((MEMBERS + 16, 3 * SLOTS), bf16),
            pltpu.VMEM((MEMBERS, 3 * SLOTS), bf16),
            pltpu.VMEM((2, MEMBERS, MEMBERS), bf16),
            pltpu.VMEM((MEMBERS * 4, 128), f32),
            pltpu.SemaphoreType.DMA((3,)),
        ],
        compiler_params=params(40),
        name="analyse",
    )(predicted, slot_rows, state)


def smooth_kernel(gain_hi, gain_lo, state, out):
    out[0] = product((gain_hi[...], gain_lo[...]), halves(state[0]))


def smooth(gain_hi, gain_lo, states):
    whole = pl.BlockSpec((MEMBERS, MEMBERS), lambda i: (0, 0))
    one = pl.BlockSpec((1, MEMBERS, STATE), lambda i: (i, 0, 0))
    return pl.pallas_call(
        smooth_kernel,
        out_shape=jax.ShapeDtypeStruct((LAGS, MEMBERS, STATE), f32),
        grid=(LAGS,),
        in_specs=[whole, whole, one],
        out_specs=one,
        compiler_params=params(24),
        cost_estimate=pl.CostEstimate(
            flops=2 * 3 * LAGS * MEMBERS**2 * STATE, bytes_accessed=8 * LAGS * MEMBERS * STATE, transcendentals=0
        ),
        name="smooth",
    )(gain_hi, gain_lo, states)


def assemble_kernel(parts, out, sems):
    copies = [pltpu.make_async_copy(parts.at[k], out.at[:, k], sems.at[k]) for k in range(PARTS)]
    for copy in copies:
        copy.start()
    for copy in copies:
        copy.wait()


def assemble(parts):
    return pl.pallas_call(
        assemble_kernel,
        out_shape=pltpu.HBM((ROWS, PARTS, 4, 128), f32),
        in_specs=[pl.BlockSpec(memory_space=pl.ANY)],
        out_specs=HBM,
        scratch_shapes=[pltpu.SemaphoreType.DMA((PARTS,))],
        compiler_params=params(8),
        name="assemble",
    )(parts)


def along_tiles(x, by):
    return lax.ppermute(x, "tile", [(i, (i + by) % TILES) for i in range(TILES)])


def far(x):
    return pltpu.with_memory_space_constraint(x, pltpu.HBM)


def exchange(x):
    return lax.all_to_all(x, GROUP, split_axis=0, concat_axis=0, tiled=True)


def per_device(
    current_state, lagged_states, water_depth, obs_cells, obs_values, obs_errors, tile_obs
):
    cur = current_state.reshape(ROWS, 2, CHUNKS, 128).transpose(0, 2, 1, 3)
    depth = water_depth.reshape(CHUNKS, 128)
    cur, to_right, to_left = edges(far(cur.reshape(ROWS * 2 * CHUNKS, 128)), far(depth))
    left = along_tiles(to_right, 1)
    right = along_tiles(to_left, -1)
    to_left, listed = lax.optimization_barrier((to_left, tile_obs[0, 0].reshape(8, 128)))
    ordered, payload, depth, cells = order(
        far(listed),
        cur.reshape(ROWS, PARTS, 4, 128),
        cur,
        far(depth),
        far(obs_cells.reshape(TILES, 8, 128)),
    )
    payload = with_beside(payload, cur, left, right)
    received = exchange(payload.reshape(PARTS, ROWS * 4 + 16, 128))
    own = heights(cur, depth, left, right, cells)
    below = along_tiles(own, 1)
    above = along_tiles(own, -1)
    picked = pick(received, below, own, above)
    predicted = exchange(picked).reshape(MEMBERS, SLOTS)
    state = forecast(received, depth, left, right)
    slot_rows = slots(
        ordered,
        obs_values.reshape(TILES, 8, 128),
        obs_errors.reshape(TILES, 8, 128),
        obs_cells.reshape(TILES, 8, 128),
    )
    gain_hi, gain_lo, analysis = analyse(predicted, slot_rows, state)
    returned = exchange(analysis.reshape(PARTS, ROWS * 4, 128))
    older = smooth(gain_hi, gain_lo, lagged_states.reshape(LAGS, MEMBERS, STATE))
    analysed = assemble(returned.reshape(PARTS, ROWS, 4, 128))
    analysed = analysed.reshape(ROWS, CHUNKS, 2, 128).transpose(0, 2, 1, 3)
    return (
        analysed.reshape(ROWS, 2, CELLS),
        older.reshape(LAGS, 1, 1, MEMBERS, STATE),
    )


def solution(mesh):
    placed = (
        P(GROUP, None, "tile"),
        P(None, "tile", GROUP, None, None),
        P("tile"),
        P(),
        P(),
        P(),
        P("tile", GROUP, None),
    )
    return jax.shard_map(
        per_device,
        mesh=mesh,
        in_specs=placed,
        out_specs=(P(GROUP, None, "tile"), P(None, "tile", GROUP, None, None)),
        check_vma=False,
    )
```
